128 devices in a mesh: view: 2 (over core), tile: 64 (over z, x, y).
Axes of the slice: x: 4, y: 4, z: 4, core: 2. Of those that a mesh axis runs over, the one named last changes fastest.
Arguments:
- params: float32 [59, 1048576], P(None, 'tile'), may hold values from -5 to 1032, as said below
- first_moment: float32 [59, 1048576], P(None, 'tile'), may hold values from -4 to 4
- second_moment: float32 [59, 1048576], P(None, 'tile'), may hold values from 0.1 to 10
- target: float32 [2, 3, 1024, 512], P('view', None, 'tile'), may hold values from 0 to 1
- view_shear: float32 [2, 2], replicated, may hold values from -1 to 1
- view_offset: float32 [2, 2], replicated, may hold values from -1.5 to 1.5
- cam_center: float32 [2, 3], replicated, may hold values from 40 to 200
- background: float32 [2, 3], replicated, may hold values from 0 to 1
- send_index: int32 [64, 64, 128], P('tile'), may hold values from 0 to 16383, as said below
- send_count: int32 [64, 64], P('tile'), may hold values from 0 to 128, as said below
- tile_list: int32 [2, 64, 32, 256], P('view', 'tile'), may hold values from 0 to 8191, as said below
- tile_count: int32 [64, 32], P('tile'), may hold values from 16 to 256, as said below
Outputs:
- new_params: float32 [59, 1048576], P(None, 'tile')
- new_first: float32 [59, 1048576], P(None, 'tile')
- new_second: float32 [59, 1048576], P(None, 'tile')
- mean_loss: float32 [], replicated
The draws below stay inside these ranges and needn't reach their ends.
Inputs may be any that keep to these rules, and one draw needn't show every extreme that they name: `params`: row 2 lies in [-3, 3], row 6 in [0.6, 1.4], rows 7 to 9 in [-0.6, 0.6]. `send_index`: slot k of pair (o, d) holds a local index when k < send_count[o, d], else 0; no Gaussian of an owner is live in two slots. `send_count`: some pair fills all 128 slots. `tile_list`: a live entry of row d is o * 128 + k with k < send_count[o, d]; entries past tile_count are 0; in each view every live slot of row d appears in exactly one live entry of row d. `tile_count`: some tile holds all 256 entries.
All inputs are finite; a program needn't handle non-finite values.
Results may differ from the reference program's by a relative error of at most 0.0003.
Values sent between devices are 32-bit elements; how exact they have to be, the bound alone decides.
A program may use at most 256 MiB of HBM per device.

```python
import math
import jax
import jax.numpy as jnp
from jax import lax

PARAMS = 59
G_DEV = 16384
TILES_DEV = 32
STEP_COUNT = 20
LIST = 256
BANDS = 64
VIEWS = 2
CAP = 128
HEIGHT = 1024
WIDTH = 512
GAUSSIANS = 1048576


def routing(key):
    subkeys = jax.random.split(key, 7)
    row_ids = jnp.arange(BANDS, dtype=jnp.int32)
    levels = jnp.array([1, 2, 4, 8], jnp.int32)[jax.random.randint(subkeys[0], (BANDS,), 0, 4)]
    busiest = jax.random.randint(subkeys[1], (), 0, BANDS)
    levels = jnp.where(row_ids == busiest, 8, levels)
    lowest = jnp.maximum(levels * LIST // 16, 1)
    highest = levels * LIST // 8 + 1
    counts = jax.random.randint(subkeys[2], (BANDS, TILES_DEV), lowest[:, None], highest[:, None])
    counts = jnp.minimum(counts, LIST).astype(jnp.int32)
    counts = counts.at[busiest, 0].set(LIST)
    totals = jnp.sum(counts, axis=1)
    slot_total = BANDS * CAP
    ranking = jax.vmap(lambda subkey: jax.random.permutation(subkey, slot_total))(jax.random.split(subkeys[3], BANDS)).astype(jnp.int32)
    favored = jax.random.randint(subkeys[4], (), 0, BANDS)
    sources = jnp.arange(slot_total, dtype=jnp.int32) // CAP
    ranking = jnp.where((row_ids[:, None] == busiest) & (sources[None, :] == favored), ranking - slot_total, ranking)
    ordering = jnp.argsort(ranking, axis=1).astype(jnp.int32)
    position = jnp.argsort(ordering, axis=1).astype(jnp.int32)
    chosen = position < totals[:, None]
    chosen_grid = chosen.reshape(BANDS, BANDS, CAP).astype(jnp.int32)
    compact = jnp.cumsum(chosen_grid, axis=2) - 1
    send_count = jnp.sum(chosen_grid, axis=2).T.astype(jnp.int32)
    received = jnp.where(chosen_grid > 0, row_ids[None, :, None] * CAP + compact, slot_total).reshape(BANDS, slot_total)
    id_by_position = jnp.take_along_axis(received, ordering, axis=1)
    offsets = jnp.cumsum(counts, axis=1) - counts
    entry_ids = jnp.arange(LIST, dtype=jnp.int32)
    spot_ids = jnp.minimum(offsets[:, :, None] + entry_ids, slot_total - 1).reshape(BANDS, -1)
    is_live = entry_ids[None, None, :] < counts[:, :, None]
    base_list = jnp.where(is_live, jnp.take_along_axis(id_by_position, spot_ids, axis=1).reshape(BANDS, TILES_DEV, LIST), 0)
    scores = jax.random.randint(subkeys[5], (VIEWS, BANDS, TILES_DEV, LIST), 0, LIST) * LIST + entry_ids
    scores = jnp.where(is_live[None], scores, LIST * LIST + entry_ids)
    depth_order = jnp.argsort(scores, axis=3).astype(jnp.int32)
    tile_list = jnp.take_along_axis(jnp.broadcast_to(base_list[None], scores.shape), depth_order, axis=3)
    owners = jax.vmap(lambda subkey: jax.random.permutation(subkey, G_DEV))(jax.random.split(subkeys[6], BANDS)).astype(jnp.int32)
    sent_before = jnp.cumsum(send_count, axis=1) - send_count
    slot_ids = jnp.arange(CAP, dtype=jnp.int32)
    send_live = slot_ids[None, None, :] < send_count[:, :, None]
    pick_ids = jnp.minimum(sent_before[:, :, None] + slot_ids, G_DEV - 1).reshape(BANDS, -1)
    send_index = jnp.where(send_live, jnp.take_along_axis(owners, pick_ids, axis=1).reshape(BANDS, BANDS, CAP), 0)
    inclusive = jnp.cumsum(counts, axis=1)
    places = jnp.arange(slot_total, dtype=jnp.int32)
    tile_at = jnp.sum((inclusive[:, None, :] <= places[None, :, None]).astype(jnp.int32), axis=2)
    tile_by_id = jnp.zeros((BANDS, slot_total + 1), jnp.int32).at[row_ids[:, None], id_by_position].set(tile_at)
    tile_by_id = tile_by_id[:, :slot_total].reshape(BANDS, BANDS, CAP).transpose(1, 0, 2)
    dest_grid = jnp.broadcast_to(row_ids[None, :, None], (BANDS, BANDS, CAP))
    target_ids = jnp.where(send_live, send_index, G_DEV)
    home_tile = jnp.full((BANDS, G_DEV + 1), -1, jnp.int32).at[row_ids[:, None, None], target_ids].set(tile_by_id)
    home_band = jnp.full((BANDS, G_DEV + 1), -1, jnp.int32).at[row_ids[:, None, None], target_ids].set(dest_grid)
    return (send_index, send_count, tile_list, counts, home_tile[:, :G_DEV], home_band[:, :G_DEV])


def draw_send_index(key, part):
    return routing(key)[0]


def draw_send_count(key, part):
    return routing(key)[1]


def draw_tile_list(key, part):
    return routing(key)[2]


def draw_tile_count(key, part):
    return routing(key)[3]


def draw_target(key, part):
    key = jax.random.fold_in(key, 5)
    shape = (VIEWS, 3, HEIGHT, WIDTH)
    row_pos = jnp.arange(HEIGHT, dtype=jnp.float32)
    spread = 0.15 + 0.3 * row_pos / HEIGHT
    noise = jax.random.uniform(key, shape, jnp.float32, -1.0, 1.0)
    return 0.5 + spread[None, None, :, None] * noise


def draw_params(key, part):
    own_key = jax.random.fold_in(key, 7)
    routes = routing(key)
    home_tile = routes[4].reshape(-1)
    home_band = routes[5].reshape(-1)
    gauss_total = BANDS * G_DEV
    subkeys = jax.random.split(own_key, 11)
    reach = 6.0
    opacity_low = -4.5
    detail = jax.random.uniform(subkeys[9], (45, gauss_total), jnp.float32, -0.3, 0.3)
    seen = home_tile >= 0
    pos_x = jnp.where(seen, 16.0 * home_tile.astype(jnp.float32) + 8.0 + jax.random.uniform(subkeys[0], (gauss_total,), jnp.float32, -reach, reach), jax.random.uniform(subkeys[1], (gauss_total,), jnp.float32, 0.0, 1.0 * WIDTH))
    pos_y = jnp.where(seen, 16.0 * home_band.astype(jnp.float32) + 8.0 + jax.random.uniform(subkeys[2], (gauss_total,), jnp.float32, -reach, reach), jax.random.uniform(subkeys[3], (gauss_total,), jnp.float32, 0.0, 1.0 * HEIGHT))
    pos_z = jax.random.uniform(subkeys[4], (gauss_total,), jnp.float32, -3.0, 3.0)
    log_scales = jax.random.uniform(subkeys[5], (3, gauss_total), jnp.float32, 0.405, 1.609)
    quat_w = jax.random.uniform(subkeys[6], (1, gauss_total), jnp.float32, 0.6, 1.4)
    quat_rest = jax.random.uniform(subkeys[7], (3, gauss_total), jnp.float32, -0.6, 0.6)
    logits = jax.random.uniform(subkeys[8], (1, gauss_total), jnp.float32, opacity_low, -1.0)
    base_color = jax.random.uniform(subkeys[10], (3, gauss_total), jnp.float32, -1.5, 1.5)
    return jnp.concatenate([pos_x[None], pos_y[None], pos_z[None], log_scales, quat_w, quat_rest, logits, base_color, detail], axis=0)


def block_scale(stream_key, shape, cuts, low, largest):
    def one(dim, blocks):
        draws = jax.random.uniform(jax.random.fold_in(jax.random.fold_in(stream_key, 6), dim), (blocks,), jnp.float32, low / len(cuts), largest / len(cuts))
        return jnp.repeat(jnp.exp(draws), shape[dim] // blocks).reshape((-1,) + (1,) * (len(shape) - dim - 1))

    factor_of = one(*cuts[0])
    for cut in cuts[1:]:
        factor_of = factor_of * one(*cut)
    return factor_of


def bell_draw(key, extent, width, most, pieces=(), held_as=jnp.bfloat16):
    gain = block_scale(key, extent, pieces, -0.22, 0.18) if pieces else 1.0
    values = jax.random.normal(key, extent, jnp.float32) * width * gain
    return jnp.minimum(jnp.maximum(values, -most), most).astype(held_as)


def setup_inputs(seed: int = 0) -> dict:
    seeds = jax.random.split(jax.random.key(seed), 13)
    return {
        "params": draw_params(jax.random.fold_in(seeds[12], 71), 0),
        "first_moment": bell_draw(seeds[1], (PARAMS, GAUSSIANS), 1.0, 4.0, ((1, 64),), jnp.float32),
        "second_moment": jnp.clip(jnp.exp(math.log(10.0) - 4.6051702 * jax.random.uniform(seeds[2], (PARAMS, GAUSSIANS), jnp.float32) ** block_scale(seeds[2], (PARAMS, GAUSSIANS), ((1, 64),), -0.2, 0.2)), 0.1, 10.0),
        "target": draw_target(jax.random.fold_in(seeds[12], 71), 0),
        "view_shear": jnp.clip(jax.random.uniform(seeds[4], (VIEWS, 2), jnp.float32, -1.0, 1.0), -1.0, 1.0),
        "view_offset": jnp.clip(jax.random.uniform(seeds[5], (VIEWS, 2), jnp.float32, -1.5, 1.5), -1.5, 1.5),
        "cam_center": jnp.clip(jax.random.uniform(seeds[6], (VIEWS, 3), jnp.float32, 40.0, 200.0), 40.0, 200.0),
        "background": jnp.clip(jax.random.uniform(seeds[7], (VIEWS, 3), jnp.float32, 0.0, 1.0), 0.0, 1.0),
        "send_index": draw_send_index(jax.random.fold_in(seeds[12], 71), 0),
        "send_count": draw_send_count(jax.random.fold_in(seeds[12], 71), 0),
        "tile_list": draw_tile_list(jax.random.fold_in(seeds[12], 71), 0),
        "tile_count": draw_tile_count(jax.random.fold_in(seeds[12], 71), 0),
    }


def window_taps():
    raw_taps = [math.exp(-(position - 5) * (position - 5) / 4.5) for position in range(11)]
    return [element / sum(raw_taps) for element in raw_taps]

def harmonics(unit_x, unit_y, unit_z):
    square_x = unit_x * unit_x
    square_y = unit_y * unit_y
    square_z = unit_z * unit_z
    return jnp.stack([0.28209479177387814 * jnp.ones_like(unit_x), -0.4886025119029199 * unit_y, 0.4886025119029199 * unit_z, -0.4886025119029199 * unit_x, 1.0925484305920792 * unit_x * unit_y, -1.0925484305920792 * unit_y * unit_z, 0.31539156525252005 * (2.0 * square_z - square_x - square_y), -1.0925484305920792 * unit_x * unit_z, 0.5462742152960396 * (square_x - square_y), -0.5900435899266435 * unit_y * (3.0 * square_x - square_y), 2.890611442640554 * unit_x * unit_y * unit_z, -0.4570457994644658 * unit_y * (4.0 * square_z - square_x - square_y), 0.3731763325901154 * unit_z * (2.0 * square_z - 3.0 * square_x - 3.0 * square_y), -0.4570457994644658 * unit_x * (4.0 * square_z - square_x - square_y), 1.445305721320277 * unit_z * (square_x - square_y), -0.5900435899266435 * unit_x * (square_x - 3.0 * square_y)])

def project(params, view_shear, view_offset, center):
    pos_x = params[0]
    pos_y = params[1]
    pos_z = params[2]
    scales = jnp.exp(params[3:6])
    quaternion = params[6:10]
    quaternion = quaternion / jnp.sqrt(lax.optimization_barrier(jnp.sum(quaternion * quaternion, axis=0)))
    quat_w = quaternion[0]
    quat_x = quaternion[1]
    quat_y = quaternion[2]
    quat_z = quaternion[3]
    rotation_matrix = [[1.0 - 2.0 * (quat_y * quat_y + quat_z * quat_z), 2.0 * (quat_x * quat_y - quat_w * quat_z), 2.0 * (quat_x * quat_z + quat_w * quat_y)], [2.0 * (quat_x * quat_y + quat_w * quat_z), 1.0 - 2.0 * (quat_x * quat_x + quat_z * quat_z), 2.0 * (quat_y * quat_z - quat_w * quat_x)], [2.0 * (quat_x * quat_z - quat_w * quat_y), 2.0 * (quat_y * quat_z + quat_w * quat_x), 1.0 - 2.0 * (quat_x * quat_x + quat_y * quat_y)]]
    shear_x = view_shear[0]
    shear_y = view_shear[1]
    row_first = [(rotation_matrix[0][column] + shear_x * rotation_matrix[2][column]) * scales[column] for column in range(3)]
    row_second = [(rotation_matrix[1][column] + shear_y * rotation_matrix[2][column]) * scales[column] for column in range(3)]
    cov_xx = row_first[0] * row_first[0] + row_first[1] * row_first[1] + row_first[2] * row_first[2] + 0.3
    cov_yy = row_second[0] * row_second[0] + row_second[1] * row_second[1] + row_second[2] * row_second[2] + 0.3
    cov_xy = row_first[0] * row_second[0] + row_first[1] * row_second[1] + row_first[2] * row_second[2]
    determinant = cov_xx * cov_yy - cov_xy * cov_xy
    screen_u = pos_x + shear_x * pos_z + view_offset[0]
    screen_v = pos_y + shear_y * pos_z + view_offset[1]
    opacity = jax.nn.sigmoid(params[10])
    toward_x = pos_x - center[0]
    toward_y = pos_y - center[1]
    toward_z = pos_z - center[2]
    length = jnp.sqrt(toward_x * toward_x + toward_y * toward_y + toward_z * toward_z)
    harmonic = harmonics(toward_x / length, toward_y / length, toward_z / length)
    coefficients = params[11:].reshape(16, 3, -1)
    splat_colors = 0.5 + lax.optimization_barrier(jnp.sum(harmonic[:, None, :] * coefficients, axis=0))
    return jnp.stack([screen_u, screen_v, cov_yy / determinant, -cov_xy / determinant, cov_xx / determinant, opacity, splat_colors[0], splat_colors[1], splat_colors[2]])

def render_band(entry_records, is_live, band_id, backdrop):
    tile_total = entry_records.shape[1]
    pixels = jnp.arange(256, dtype=jnp.int32)
    column_pos = (pixels % 16).astype(jnp.float32) + 0.5
    row_pos = (pixels // 16).astype(jnp.float32) + 0.5
    pixel_x = 16.0 * jnp.arange(tile_total, dtype=jnp.float32)[:, None] + column_pos[None, :]
    pixel_y = 16.0 * band_id.astype(jnp.float32) + row_pos
    delta_x = pixel_x[:, None, :] - entry_records[0][:, :, None]
    delta_y = pixel_y[None, None, :] - entry_records[1][:, :, None]
    exponent = -0.5 * (entry_records[2][:, :, None] * delta_x * delta_x + entry_records[4][:, :, None] * delta_y * delta_y) - entry_records[3][:, :, None] * delta_x * delta_y
    coverage = jnp.where(is_live[:, :, None], entry_records[5][:, :, None] * jnp.exp(exponent), 0.0)
    log_keep = jnp.log1p(-coverage)
    running_prefix = jnp.cumsum(log_keep, axis=1) - log_keep
    log_total = lax.optimization_barrier(jnp.sum(log_keep, axis=1))
    blend_weights = coverage * jnp.exp(running_prefix)
    splat_colors = jnp.einsum('qvr,fqv->fqr', blend_weights, entry_records[6:9], precision=lax.Precision.HIGHEST)
    splat_colors = splat_colors + jnp.exp(log_total)[None] * backdrop[:, None, None]
    return splat_colors.reshape(3, tile_total, 16, 16).transpose(0, 2, 1, 3).reshape(3, 16, tile_total * 16)

def render_item(bundle):
    entry_records, is_live, band_id, backdrop = bundle
    return render_band(entry_records, is_live, band_id, backdrop)

def gaussian_blur(planes):
    taps = window_taps()
    rows_out = planes.shape[1] - 10
    vertical = taps[0] * planes[:, 0:rows_out]
    for position in range(1, 11):
        vertical = vertical + taps[position] * planes[:, position:position + rows_out]
    image_width = planes.shape[2]
    padded = jnp.pad(vertical, ((0, 0), (0, 0), (5, 5)))
    result = taps[0] * padded[:, :, 0:image_width]
    for position in range(1, 11):
        result = result + taps[position] * padded[:, :, position:position + image_width]
    return result

def ssim_map(level_x, level_y, energy_x, energy_y, product_xy):
    upper = (2.0 * level_x * level_y + 0.0001) * (2.0 * (product_xy - level_x * level_y) + 0.0009)
    lower = (level_x * level_x + level_y * level_y + 0.0001) * (energy_x - level_x * level_x + (energy_y - level_y * level_y) + 0.0009)
    return upper / lower

def padded_blur(planes):
    return gaussian_blur(jnp.pad(planes, ((0, 0), (5, 5), (0, 0))))

def adam_update(params, first_moment, second_moment, gradient):
    row_ids = jnp.arange(params.shape[0], dtype=jnp.int32)[:, None]
    learning = jnp.where(row_ids < 3, 0.016, jnp.where(row_ids < 6, 0.005, jnp.where(row_ids < 10, 0.001, jnp.where(row_ids < 11, 0.05, jnp.where(row_ids < 14, 0.0025, 0.000125)))))
    new_first = 0.9 * first_moment + 0.1 * gradient
    new_second = 0.999 * second_moment + 0.001 * gradient * gradient
    corrected = new_first / (1.0 - 0.9 ** STEP_COUNT)
    scale_second = jnp.sqrt(new_second / (1.0 - 0.999 ** STEP_COUNT)) + 1e-15
    return (params - learning * corrected / scale_second, new_first, new_second)

def reference(params, first_moment, second_moment, target, view_shear, view_offset, cam_center, background, send_index, send_count, tile_list, tile_count):

    def objective(values):
        records = jnp.stack([project(values, view_shear[view_id], view_offset[view_id], cam_center[view_id]) for view_id in range(VIEWS)])
        sources = jnp.arange(BANDS, dtype=jnp.int32)
        global_index_list = sources[:, None, None] * G_DEV + send_index
        alive_slots = jnp.arange(CAP, dtype=jnp.int32)[None, None, :] < send_count[:, :, None]
        gathered = jnp.where(alive_slots[None, None], records[:, :, global_index_list], 0.0)
        slot_rows = gathered.transpose(0, 3, 1, 2, 4).reshape(VIEWS, BANDS, 9, BANDS * CAP)
        entry_records = jax.vmap(jax.vmap(lambda slot_block, chosen: slot_block[:, chosen]))(slot_rows, tile_list)
        alive_entries = jnp.arange(LIST, dtype=jnp.int32)[None, None, :] < tile_count[:, :, None]
        bundle = (entry_records.reshape(VIEWS * BANDS, 9, TILES_DEV, LIST), jnp.tile(alive_entries, (VIEWS, 1, 1)), jnp.tile(jnp.arange(BANDS, dtype=jnp.int32), VIEWS), jnp.repeat(background, BANDS, axis=0))
        bands_out = lax.map(jax.checkpoint(render_item), bundle)
        rendered = bands_out.reshape(VIEWS, BANDS, 3, 16, WIDTH).transpose(0, 2, 1, 3, 4).reshape(VIEWS * 3, HEIGHT, WIDTH)
        target_planes = target.reshape(VIEWS * 3, HEIGHT, WIDTH)
        similarity = ssim_map(padded_blur(rendered), padded_blur(target_planes), padded_blur(rendered * rendered), padded_blur(target_planes * target_planes), padded_blur(rendered * target_planes))
        difference = rendered - target_planes
        return jnp.sum(0.2 * jnp.sqrt(difference * difference + 0.0001) + 0.8 * (1.0 - similarity))
    objective_sum, pull_back = jax.vjp(objective, params)
    gradient = pull_back(jnp.ones_like(objective_sum))[0]
    new_params, new_first, new_second = adam_update(params, first_moment, second_moment, gradient)
    return (new_params, new_first, new_second, objective_sum / (VIEWS * 3 * HEIGHT * WIDTH))
```

```python
import functools
import math

import jax
import jax.numpy as jnp
from jax import lax
from jax.experimental import pallas as pl
from jax.experimental.pallas import tpu as pltpu
from jax.sharding import PartitionSpec as P

STEP_COUNT = 20
LIST = 256


def extended(block, sides, width):
    for axis, dim in sides:
        count = lax.axis_size(axis)
        forward = [(i, i + 1) for i in range(count - 1)]
        backward = [(target, source) for source, target in forward]
        low = lax.ppermute(
            lax.slice_in_dim(block, block.shape[dim] - width, None, axis=dim), axis, forward
        )
        high = lax.ppermute(lax.slice_in_dim(block, 0, width, axis=dim), axis, backward)
        block = jnp.concatenate([low, block, high], axis=dim)
    return block


def window_taps():
    raw_taps = [math.exp(-(position - 5) * (position - 5) / 4.5) for position in range(11)]
    return [element / sum(raw_taps) for element in raw_taps]


def harmonics(unit_x, unit_y, unit_z):
    square_x = unit_x * unit_x
    square_y = unit_y * unit_y
    square_z = unit_z * unit_z
    return [
        0.28209479177387814 * jnp.ones_like(unit_x),
        -0.4886025119029199 * unit_y,
        0.4886025119029199 * unit_z,
        -0.4886025119029199 * unit_x,
        1.0925484305920792 * unit_x * unit_y,
        -1.0925484305920792 * unit_y * unit_z,
        0.31539156525252005 * (2.0 * square_z - square_x - square_y),
        -1.0925484305920792 * unit_x * unit_z,
        0.5462742152960396 * (square_x - square_y),
        -0.5900435899266435 * unit_y * (3.0 * square_x - square_y),
        2.890611442640554 * unit_x * unit_y * unit_z,
        -0.4570457994644658 * unit_y * (4.0 * square_z - square_x - square_y),
        0.3731763325901154 * unit_z * (2.0 * square_z - 3.0 * square_x - 3.0 * square_y),
        -0.4570457994644658 * unit_x * (4.0 * square_z - square_x - square_y),
        1.445305721320277 * unit_z * (square_x - square_y),
        -0.5900435899266435 * unit_x * (square_x - 3.0 * square_y),
    ]


MESH = pl.DeviceIdType.MESH
VMEM_LIMIT = 56 * 1024 * 1024
NN = (((1,), (0,)), ((), ()))
NT = (((1,), (1,)), ((), ()))
TN = (((0,), (0,)), ((), ()))


def mxu(left, right, dims):
    return lax.dot_general(left, right, dims, preferred_element_type=jnp.float32)


def split2(value):
    high = value.astype(jnp.bfloat16)
    low = (value - high.astype(jnp.float32)).astype(jnp.bfloat16)
    return high, low


def split3(value):
    high = value.astype(jnp.bfloat16)
    rest = value - high.astype(jnp.float32)
    middle = rest.astype(jnp.bfloat16)
    low = (rest - middle.astype(jnp.float32)).astype(jnp.bfloat16)
    return high, middle, low


def project_rows(rows, cameras):
    pos_x, pos_y, pos_z = rows[0:3]
    scales = [jnp.exp(row) for row in rows[3:6]]
    quat_w, quat_x, quat_y, quat_z = rows[6:10]
    norm = 1.0 / jnp.sqrt(
        quat_w * quat_w + quat_x * quat_x + quat_y * quat_y + quat_z * quat_z
    )
    quat_w, quat_x, quat_y, quat_z = quat_w * norm, quat_x * norm, quat_y * norm, quat_z * norm
    rotation = [
        [
            1.0 - 2.0 * (quat_y * quat_y + quat_z * quat_z),
            2.0 * (quat_x * quat_y - quat_w * quat_z),
            2.0 * (quat_x * quat_z + quat_w * quat_y),
        ],
        [
            2.0 * (quat_x * quat_y + quat_w * quat_z),
            1.0 - 2.0 * (quat_x * quat_x + quat_z * quat_z),
            2.0 * (quat_y * quat_z - quat_w * quat_x),
        ],
        [
            2.0 * (quat_x * quat_z - quat_w * quat_y),
            2.0 * (quat_y * quat_z + quat_w * quat_x),
            1.0 - 2.0 * (quat_x * quat_x + quat_y * quat_y),
        ],
    ]
    opacity = 1.0 / (1.0 + jnp.exp(-rows[10]))
    records = []
    for shear_x, shear_y, offset_x, offset_y, center_x, center_y, center_z in cameras:
        first = [(rotation[0][k] + shear_x * rotation[2][k]) * scales[k] for k in range(3)]
        second = [(rotation[1][k] + shear_y * rotation[2][k]) * scales[k] for k in range(3)]
        cov_xx = first[0] * first[0] + first[1] * first[1] + first[2] * first[2] + 0.3
        cov_yy = second[0] * second[0] + second[1] * second[1] + second[2] * second[2] + 0.3
        cov_xy = first[0] * second[0] + first[1] * second[1] + first[2] * second[2]
        inverse = 1.0 / (cov_xx * cov_yy - cov_xy * cov_xy)
        toward_x = pos_x - center_x
        toward_y = pos_y - center_y
        toward_z = pos_z - center_z
        shrink = 1.0 / jnp.sqrt(toward_x * toward_x + toward_y * toward_y + toward_z * toward_z)
        basis = harmonics(toward_x * shrink, toward_y * shrink, toward_z * shrink)
        colors = []
        for c in range(3):
            total = basis[0] * rows[11 + c]
            for k in range(1, 16):
                total = total + basis[k] * rows[11 + 3 * k + c]
            colors.append(0.5 + total)
        records.append(
            [
                pos_x + shear_x * pos_z + offset_x,
                pos_y + shear_y * pos_z + offset_y,
                cov_yy * inverse,
                -cov_xy * inverse,
                cov_xx * inverse,
                opacity,
                *colors,
            ]
        )
    return records


def camera_of(refs, view):
    shear_ref, offset_ref, center_ref = refs
    return (
        shear_ref[view, 0],
        shear_ref[view, 1],
        offset_ref[view, 0],
        offset_ref[view, 1],
        center_ref[view, 0],
        center_ref[view, 1],
        center_ref[view, 2],
    )


def spread_rows(source_ref, dense_ref):
    count = source_ref.shape[0]
    for c in range(8):
        lanes = pl.ds(128 * c, 128)
        for first in range(0, count, 8):
            size = min(8, count - first)
            dense_ref[pl.ds(8 * first + c, size, stride=8), :] = source_ref[first : first + size, lanes]


def project_kernel(params_ref, index_ref, shear_ref, offset_ref, center_ref, out_ref, dense, table, parts):
    step = pl.program_id(0)
    spread_rows(params_ref, dense)
    rows = [dense[8 * r : 8 * r + 8, :] for r in range(59)]
    record = project_rows(rows, [camera_of((shear_ref, offset_ref, center_ref), 0)])[0]
    for q in range(9):
        table[q, pl.ds(pl.multiple_of(8 * step, 8), 8), :] = record[q]

    @pl.when(step == pl.num_programs(0) - 1)
    def _():
        for q in range(9):
            for half in range(2):
                for k, part in enumerate(split3(table[q, 64 * half : 64 * half + 64, :])):
                    parts[64 * q : 64 * q + 64, 256 * k + 128 * half : 256 * k + 128 * half + 128] = part
        low_ids = lax.broadcasted_iota(jnp.int32, (256, 256), 0)
        high_ids = lax.broadcasted_iota(jnp.int32, (64, 256), 0)

        def pick(pair, carry):
            index = jnp.concatenate(
                [index_ref[pl.ds(pair, 1), :], index_ref[pl.ds(pair + 32, 1), :]], axis=1
            )
            high = (index >> 7) & 63
            low = (index & 127) + ((index >> 13) << 7)
            hot = (low_ids == low).astype(jnp.float32).astype(jnp.bfloat16)
            found = mxu(parts[...], jnp.concatenate([hot, hot, hot], axis=0), NN)
            mask = high_ids == high
            for q in range(9):
                row = jnp.sum(jnp.where(mask, found[64 * q : 64 * q + 64], 0.0), axis=0, keepdims=True)
                out_ref[pair, q : q + 1, :] = row[:, 0:128]
                out_ref[pair + 32, q : q + 1, :] = row[:, 128:256]
            return carry

        lax.fori_loop(0, 32, pick, 0, unroll=2)


def project_and_pick(params, send_index, shear, offset, center):
    smem = pl.BlockSpec(memory_space=pltpu.SMEM)
    return pl.pallas_call(
        project_kernel,
        grid=(16,),
        out_shape=jax.ShapeDtypeStruct((64, 9, 128), jnp.float32),
        in_specs=[
            pl.BlockSpec((59, 1024), lambda i: (0, i)),
            pl.BlockSpec((64, 128), lambda i: (0, 0)),
            smem,
            smem,
            smem,
        ],
        out_specs=pl.BlockSpec((64, 9, 128), lambda i: (0, 0, 0)),
        scratch_shapes=[
            pltpu.VMEM((59 * 8, 128), jnp.float32),
            pltpu.VMEM((9, 128, 128), jnp.float32),
            pltpu.VMEM((576, 768), jnp.bfloat16),
        ],
        compiler_params=pltpu.CompilerParams(vmem_limit_bytes=VMEM_LIMIT),
        name="project_and_pick",
    )(params, send_index, shear, offset, center)


def exchange_kernel(in_ref, out_ref, send_sem, recv_sem, local_sem):
    total = lax.axis_size("tile")
    me = lax.axis_index("tile")
    barrier = pltpu.get_barrier_semaphore()

    def greet(p, carry):
        pl.semaphore_signal(
            barrier, inc=1, device_id={"tile": lax.rem(me + p, total)}, device_id_type=MESH
        )
        return carry

    lax.fori_loop(1, total, greet, 0)
    own = pltpu.make_async_copy(in_ref.at[me], out_ref.at[me], local_sem)
    own.start()
    pl.semaphore_wait(barrier, total - 1)

    def copy_to(p):
        peer = lax.rem(me + p, total)
        return pltpu.make_async_remote_copy(
            src_ref=in_ref.at[peer],
            dst_ref=out_ref.at[me],
            send_sem=send_sem.at[p],
            recv_sem=recv_sem.at[p],
            device_id={"tile": peer},
            device_id_type=MESH,
        )

    def send(p, carry):
        copy_to(p).start()
        return carry

    def finish(p, carry):
        copy_to(p).wait()
        return carry

    lax.fori_loop(1, total, send, 0)
    own.wait()
    lax.fori_loop(1, total, finish, 0)


def exchange(blocks, collective_id):
    vmem = pl.BlockSpec(memory_space=pltpu.VMEM)
    total = blocks.shape[0]
    return pl.pallas_call(
        exchange_kernel,
        out_shape=jax.ShapeDtypeStruct(blocks.shape, blocks.dtype),
        in_specs=[vmem],
        out_specs=vmem,
        scratch_shapes=[
            pltpu.SemaphoreType.DMA((total,)),
            pltpu.SemaphoreType.DMA((total,)),
            pltpu.SemaphoreType.DMA,
        ],
        compiler_params=pltpu.CompilerParams(
            collective_id=collective_id, has_side_effects=True, vmem_limit_bytes=VMEM_LIMIT
        ),
        name="exchange",
    )(blocks)


TILES_STEP = 4


def slot_place(index):
    return (index >> 7) & 31, (index & 127) + ((index >> 12) << 7)


def tile_deltas(tile, band, u_row, w_row):
    offsets = lax.broadcasted_iota(jnp.int32, (16, 256), 0)
    pixel_x = (offsets + 16 * tile).astype(jnp.float32) + 0.5
    pixel_y = (offsets + 16 * band).astype(jnp.float32) + 0.5
    return pixel_x - u_row, pixel_y - w_row


def forward_kernel(
    slots_ref, list_ref, count_ref, band_ref, back_ref, image_ref, entry_ref, cover_ref, keep_ref, parts, before
):
    step = pl.program_id(0)

    @pl.when(step == 0)
    def _():
        for q in range(9):
            for half in range(2):
                for k, part in enumerate(split3(slots_ref[32 * half : 32 * half + 32, q, :])):
                    parts[32 * q : 32 * q + 32, 256 * k + 128 * half : 256 * k + 128 * half + 128] = part
        row_ids = lax.broadcasted_iota(jnp.int32, (256, 256), 0)
        column_ids = lax.broadcasted_iota(jnp.int32, (256, 256), 1)
        before[...] = (row_ids < column_ids).astype(jnp.float32).astype(jnp.bfloat16)

    band = band_ref[0]
    low_ids = lax.broadcasted_iota(jnp.int32, (256, 256), 0)
    high_ids = lax.broadcasted_iota(jnp.int32, (32, 256), 0)
    lanes = lax.broadcasted_iota(jnp.int32, (1, 256), 1)

    def one(k, carry):
        tile = step * TILES_STEP + k
        high, low = slot_place(list_ref[pl.ds(tile, 1), :])
        hot = (low_ids == low).astype(jnp.float32).astype(jnp.bfloat16)
        found = mxu(parts[...], jnp.concatenate([hot, hot, hot], axis=0), NN)
        mask = high_ids == high
        rows = [
            jnp.sum(jnp.where(mask, found[32 * q : 32 * q + 32], 0.0), axis=0, keepdims=True)
            for q in range(9)
        ]
        rows[5] = jnp.where(lanes < count_ref[0, tile], rows[5], 0.0)
        for c in range(3):
            rows[6 + c] = rows[6 + c] - back_ref[c]
        for q in range(9):
            entry_ref[k, q : q + 1, :] = rows[q]
        delta_x, delta_y = tile_deltas(tile, band, rows[0], rows[1])
        along_x = -0.5 * rows[2] * delta_x * delta_x
        mixed = -rows[3] * delta_x
        along_y = -0.5 * rows[4] * delta_y * delta_y
        pieces = []
        for i in range(16):
            exponent = along_x + (mixed * delta_y[i : i + 1] + along_y[i : i + 1])
            pieces.append(rows[5] * jnp.exp(exponent))
        cover = jnp.concatenate(pieces, axis=0)
        kept_high, kept_low = split2(jnp.log(1.0 - cover))
        keep = jnp.exp(mxu(kept_high, before[...], NN) + mxu(kept_low, before[...], NN))
        cover_ref[k] = cover
        keep_ref[k] = keep
        weight_high, weight_low = split2(cover * keep)
        colors = jnp.concatenate(rows[6:9] + [jnp.zeros((5, 256), jnp.float32)], axis=0)
        color_high, color_low = split2(colors)
        shown = (
            mxu(color_high, weight_high, NT)
            + mxu(color_low, weight_high, NT)
            + mxu(color_high, weight_low, NT)
        )
        for c in range(3):
            image_ref[c, pl.ds(tile, 1), :] = shown[c : c + 1] + back_ref[c]
        return carry

    lax.fori_loop(0, TILES_STEP, one, 0)


def render_forward(slots, lists, counts, band, back):
    smem = pl.BlockSpec(memory_space=pltpu.SMEM)
    field = jax.ShapeDtypeStruct((32, 256, 256), jnp.float32)
    field_spec = pl.BlockSpec((TILES_STEP, 256, 256), lambda i: (i, 0, 0))
    return pl.pallas_call(
        forward_kernel,
        grid=(32 // TILES_STEP,),
        out_shape=(
            jax.ShapeDtypeStruct((3, 32, 256), jnp.float32),
            jax.ShapeDtypeStruct((32, 9, 256), jnp.float32),
            field,
            field,
        ),
        in_specs=[
            pl.BlockSpec((64, 9, 128), lambda i: (0, 0, 0)),
            pl.BlockSpec((32, 256), lambda i: (0, 0)),
            smem,
            smem,
            smem,
        ],
        out_specs=(
            pl.BlockSpec((3, 32, 256), lambda i: (0, 0, 0)),
            pl.BlockSpec((TILES_STEP, 9, 256), lambda i: (i, 0, 0)),
            field_spec,
            field_spec,
        ),
        scratch_shapes=[
            pltpu.VMEM((288, 768), jnp.bfloat16),
            pltpu.VMEM((256, 256), jnp.bfloat16),
        ],
        compiler_params=pltpu.CompilerParams(vmem_limit_bytes=VMEM_LIMIT),
        name="render_forward",
    )(slots, lists, counts, band, back)


def backward_kernel(
    entry_ref, cover_ref, keep_ref, grad_ref, list_ref, band_ref, out_ref, after, total
):
    step = pl.program_id(0)

    @pl.when(step == 0)
    def _():
        row_ids = lax.broadcasted_iota(jnp.int32, (256, 256), 0)
        column_ids = lax.broadcasted_iota(jnp.int32, (256, 256), 1)
        after[...] = (row_ids > column_ids).astype(jnp.float32).astype(jnp.bfloat16)
        total[...] = jnp.zeros_like(total)

    band = band_ref[0]
    low_ids = lax.broadcasted_iota(jnp.int32, (256, 256), 0)
    high_ids = lax.broadcasted_iota(jnp.int32, (32, 256), 0)

    def one(k, carry):
        tile = step * TILES_STEP + k
        rows = [entry_ref[k, q : q + 1, :] for q in range(9)]
        grads = jnp.concatenate([grad_ref[c, pl.ds(tile, 1), :] for c in range(3)], axis=0)
        colors = jnp.concatenate(rows[6:9], axis=0)
        grads_high = grads.astype(jnp.bfloat16).astype(jnp.float32)
        grads_low = grads - grads_high
        colors_high = colors.astype(jnp.bfloat16).astype(jnp.float32)
        colors_low = colors - colors_high
        blank = jnp.zeros((7, 256), jnp.float32)
        left = jnp.concatenate([grads_high, grads_high, grads_low, blank], axis=0).astype(jnp.bfloat16)
        right = jnp.concatenate([colors_high, colors_low, colors_high, blank], axis=0).astype(jnp.bfloat16)
        shade = mxu(left, right, TN)
        cover = cover_ref[k]
        weight = cover * keep_ref[k]
        weight_high, weight_low = split2(weight)
        both = jnp.concatenate([grads_high, grads_low, blank, blank[0:3]], axis=0).astype(jnp.bfloat16)
        color_grad = mxu(both, weight_high, NN)
        color_grad = color_grad[0:3] + color_grad[3:6] + mxu(both, weight_low, NN)[0:3]
        lit = weight * shade
        lit_high, lit_low = split2(lit)
        behind = mxu(lit_high, after[...], NN) + mxu(lit_low, after[...], NN)
        pull = lit - behind * (cover / (1.0 - cover))
        delta_x, delta_y = tile_deltas(tile, band, rows[0], rows[1])
        sum_0 = pull[0:16]
        sum_y = sum_0 * delta_y[0:1]
        sum_yy = sum_y * delta_y[0:1]
        for i in range(1, 16):
            piece = pull[16 * i : 16 * i + 16]
            piece_y = piece * delta_y[i : i + 1]
            sum_0 = sum_0 + piece
            sum_y = sum_y + piece_y
            sum_yy = sum_yy + piece_y * delta_y[i : i + 1]
        sum_x = sum_0 * delta_x

        def fold(value):
            return jnp.sum(value, axis=0, keepdims=True)

        moment_0 = fold(sum_0)
        moment_x = fold(sum_x)
        moment_xx = fold(sum_x * delta_x)
        moment_y = fold(sum_y)
        moment_xy = fold(sum_y * delta_x)
        moment_yy = fold(sum_yy)
        live = rows[5] > 0.0
        results = [
            rows[2] * moment_x + rows[3] * moment_y,
            rows[4] * moment_y + rows[3] * moment_x,
            -0.5 * moment_xx,
            -moment_xy,
            -0.5 * moment_yy,
            jnp.where(live, moment_0 / jnp.where(live, rows[5], 1.0), 0.0),
            color_grad[0:1],
            color_grad[1:2],
            color_grad[2:3],
        ]
        high, low = slot_place(list_ref[pl.ds(tile, 1), :])
        hot = (low_ids == low).astype(jnp.float32).astype(jnp.bfloat16)
        mask = high_ids == high
        placed = jnp.concatenate([jnp.where(mask, row, 0.0) for row in results], axis=0)
        placed_high, placed_low = split2(placed)
        total[...] += mxu(placed_high, hot, NT) + mxu(placed_low, hot, NT)
        return carry

    lax.fori_loop(0, TILES_STEP, one, 0)

    @pl.when(step == pl.num_programs(0) - 1)
    def _():
        for q in range(9):
            for half in range(2):
                out_ref[32 * half : 32 * half + 32, q, :] = total[
                    32 * q : 32 * q + 32, 128 * half : 128 * half + 128
                ]


def render_backward(entries, cover, keep, grads, lists, band):
    smem = pl.BlockSpec(memory_space=pltpu.SMEM)
    field_spec = pl.BlockSpec((TILES_STEP, 256, 256), lambda i: (i, 0, 0))
    return pl.pallas_call(
        backward_kernel,
        grid=(32 // TILES_STEP,),
        out_shape=jax.ShapeDtypeStruct((64, 9, 128), jnp.float32),
        in_specs=[
            pl.BlockSpec((TILES_STEP, 9, 256), lambda i: (i, 0, 0)),
            field_spec,
            field_spec,
            pl.BlockSpec((3, 32, 256), lambda i: (0, 0, 0)),
            pl.BlockSpec((32, 256), lambda i: (0, 0)),
            smem,
        ],
        out_specs=pl.BlockSpec((64, 9, 128), lambda i: (0, 0, 0)),
        scratch_shapes=[
            pltpu.VMEM((256, 256), jnp.bfloat16),
            pltpu.VMEM((288, 256), jnp.float32),
        ],
        compiler_params=pltpu.CompilerParams(vmem_limit_bytes=VMEM_LIMIT),
        name="render_backward",
    )(entries, cover, keep, grads, lists, band)


def place_kernel(returned_ref, index_ref, count_ref, out_ref, total):
    total[...] = jnp.zeros_like(total)
    low_ids = lax.broadcasted_iota(jnp.int32, (256, 256), 0)
    high_ids = lax.broadcasted_iota(jnp.int32, (64, 256), 0)
    lanes = lax.broadcasted_iota(jnp.int32, (1, 128), 1)

    def place(pair, carry):
        def joined(values):
            return jnp.concatenate(values, axis=1)

        bands = (pair, pair + 32)
        index = joined([index_ref[pl.ds(d, 1), :] for d in bands])
        live = joined([(lanes < count_ref[0, d]).astype(jnp.int32) for d in bands])
        high = jnp.where(live > 0, (index >> 7) & 63, -1)
        low = (index & 127) + ((index >> 13) << 7)
        hot = (low_ids == low).astype(jnp.float32).astype(jnp.bfloat16)
        mask = high_ids == high
        placed = jnp.concatenate(
            [
                jnp.where(mask, joined([returned_ref[d, q : q + 1, :] for d in bands]), 0.0)
                for q in range(9)
            ],
            axis=0,
        )
        placed_high, placed_low = split2(placed)
        total[...] += mxu(placed_high, hot, NT) + mxu(placed_low, hot, NT)
        return carry

    lax.fori_loop(0, 32, place, 0, unroll=2)
    for q in range(9):
        for half in range(2):
            out_ref[q, 64 * half : 64 * half + 64, :] = total[
                64 * q : 64 * q + 64, 128 * half : 128 * half + 128
            ]


def place_gradients(returned, send_index, send_count):
    vmem = pl.BlockSpec(memory_space=pltpu.VMEM)
    return pl.pallas_call(
        place_kernel,
        out_shape=jax.ShapeDtypeStruct((9, 128, 128), jnp.float32),
        in_specs=[vmem, vmem, pl.BlockSpec(memory_space=pltpu.SMEM)],
        out_specs=vmem,
        scratch_shapes=[pltpu.VMEM((576, 256), jnp.float32)],
        compiler_params=pltpu.CompilerParams(vmem_limit_bytes=VMEM_LIMIT),
        name="place_gradients",
    )(returned, send_index, send_count)


RATES = [0.016] * 3 + [0.005] * 3 + [0.001] * 4 + [0.05] + [0.0025] * 3 + [0.000125] * 45


def update_kernel(
    params_ref, first_ref, second_ref, own_ref, other_ref, view_ref, shear_ref, offset_ref, center_ref,
    params_out, first_out, second_out, dense,
):
    spread_rows(params_ref, dense)
    rows = [dense[8 * r : 8 * r + 8, :] for r in range(59)]
    refs = (shear_ref, offset_ref, center_ref)
    cameras = [camera_of(refs, 0), camera_of(refs, 1)]
    _, pull_back = jax.vjp(lambda *values: project_rows(values, cameras), *rows)
    is_first = view_ref[0] == 0
    own = [own_ref[q] for q in range(9)]
    other = [other_ref[q] for q in range(9)]
    gradient = pull_back(
        [
            [jnp.where(is_first, a, b) for a, b in zip(own, other)],
            [jnp.where(is_first, b, a) for a, b in zip(own, other)],
        ]
    )
    for r in range(59):
        dense[8 * r : 8 * r + 8, :] = gradient[r]
    for first in range(0, 59, 8):
        size = min(8, 59 - first)
        row_ids = lax.broadcasted_iota(jnp.int32, (size, 128), 0)
        rate = jnp.full((size, 128), RATES[first], jnp.float32)
        for r in range(1, size):
            if RATES[first + r] != RATES[first + r - 1]:
                rate = jnp.where(row_ids >= r, RATES[first + r], rate)
        for c in range(8):
            here = (slice(first, first + size), pl.ds(128 * c, 128))
            grad = dense[pl.ds(8 * first + c, size, stride=8), :]
            new_first = 0.9 * first_ref[here] + 0.1 * grad
            new_second = 0.999 * second_ref[here] + 0.001 * grad * grad
            corrected = new_first / (1.0 - 0.9**STEP_COUNT)
            scale = jnp.sqrt(new_second / (1.0 - 0.999**STEP_COUNT)) + 1e-15
            params_out[here] = params_ref[here] - rate * corrected / scale
            first_out[here] = new_first
            second_out[here] = new_second


def update(params, first_moment, second_moment, own, other, view, shear, offset, center):
    smem = pl.BlockSpec(memory_space=pltpu.SMEM)
    block = pl.BlockSpec((59, 1024), lambda i: (0, i))
    grads = pl.BlockSpec((9, 8, 128), lambda i: (0, i, 0))
    shape = jax.ShapeDtypeStruct(params.shape, jnp.float32)
    return pl.pallas_call(
        update_kernel,
        grid=(16,),
        out_shape=(shape, shape, shape),
        in_specs=[block, block, block, grads, grads, smem, smem, smem, smem],
        out_specs=(block, block, block),
        scratch_shapes=[pltpu.VMEM((59 * 8, 128), jnp.float32)],
        compiler_params=pltpu.CompilerParams(vmem_limit_bytes=VMEM_LIMIT),
        name="update",
    )(params, first_moment, second_moment, own, other, view, shear, offset, center)


def gaussian_blur(planes):
    taps = window_taps()
    rows_out = planes.shape[1] - 10
    vertical = taps[0] * planes[:, 0:rows_out]
    for position in range(1, 11):
        vertical = vertical + taps[position] * planes[:, position : position + rows_out]
    image_width = planes.shape[2]
    padded = jnp.pad(vertical, ((0, 0), (0, 0), (5, 5)))
    result = taps[0] * padded[:, :, 0:image_width]
    for position in range(1, 11):
        result = result + taps[position] * padded[:, :, position : position + image_width]
    return result


def ssim_map(level_x, level_y, energy_x, energy_y, product_xy):
    upper = (2.0 * level_x * level_y + 0.0001) * (2.0 * (product_xy - level_x * level_y) + 0.0009)
    lower = (level_x * level_x + level_y * level_y + 0.0001) * (
        energy_x - level_x * level_x + (energy_y - level_y * level_y) + 0.0009
    )
    return upper / lower


def window_stats(widened):
    shown = widened[0:3]
    truth = widened[3:6]
    mean_x = gaussian_blur(shown)
    mean_y = gaussian_blur(truth)
    power_x = gaussian_blur(shown * shown)
    power_y = gaussian_blur(truth * truth)
    cross_xy = gaussian_blur(shown * truth)
    return (mean_x, mean_y, power_x, power_y, cross_xy)


def shards(
    params,
    first_moment,
    second_moment,
    target,
    view_shear,
    view_offset,
    cam_center,
    background,
    send_index,
    send_count,
    tile_list,
    tile_count,
):
    view_index = lax.axis_index("view")
    band_index = lax.axis_index("tile")
    band_total = lax.axis_size("tile")

    def own_first(values):
        return jnp.where(view_index == 0, values, values[::-1])

    shear, offset, center = own_first(view_shear), own_first(view_offset), own_first(cam_center)
    backdrop = own_first(background)[0]
    band = band_index.astype(jnp.int32).reshape(1)
    outgoing = project_and_pick(params, send_index[0], shear, offset, center)
    incoming = exchange(outgoing, 0)
    shown, entries, cover, keep = render_forward(
        incoming, tile_list[0, 0], tile_count, band, backdrop
    )
    image_band = shown.reshape(3, 32, 16, 16).transpose(0, 2, 1, 3).reshape(3, 16, 512)
    frame_band = target[0]
    image_width = frame_band.shape[2]
    stacked = jnp.concatenate([image_band, frame_band], axis=0)
    widened = extended(stacked, (("tile", 1),), 5)
    mean_x, mean_y, power_x, power_y, cross_xy = window_stats(widened)
    similarity, ssim_back = jax.vjp(
        lambda level_x, energy_x, product_xy: ssim_map(
            level_x, mean_y, energy_x, power_y, product_xy
        ),
        mean_x,
        power_x,
        cross_xy,
    )
    grad_mean, grad_power, grad_cross = ssim_back(jnp.full_like(similarity, -0.8))
    spread = extended(
        jnp.concatenate([grad_mean, grad_power, grad_cross], axis=0), (("tile", 1),), 5
    )
    blurred = gaussian_blur(spread)
    difference = image_band - frame_band
    smooth = jnp.sqrt(difference * difference + 0.0001)
    loss_part = jnp.sum(0.2 * smooth + 0.8 * (1.0 - similarity))
    pixel_grad = (
        0.2 * difference / smooth
        + blurred[0:3]
        + 2.0 * image_band * blurred[3:6]
        + frame_band * blurred[6:9]
    )
    mean_loss = lax.psum(loss_part, ("view", "tile")) / (
        lax.axis_size("view") * 3 * 16 * band_total * image_width
    )
    grad_tiles = pixel_grad.reshape(3, 16, 32, 16).transpose(0, 2, 1, 3).reshape(3, 32, 256)
    slot_grad = render_backward(entries, cover, keep, grad_tiles, tile_list[0, 0], band)
    returned = exchange(slot_grad, 1)
    own_grad = place_gradients(returned, send_index[0], send_count)
    other_grad = lax.ppermute(own_grad, "view", [(0, 1), (1, 0)])
    new_params, new_first, new_second = update(
        params, first_moment, second_moment, own_grad, other_grad,
        view_index.astype(jnp.int32).reshape(1), view_shear, view_offset, cam_center,
    )
    return (new_params, new_first, new_second, mean_loss)


def solution(mesh):
    placed = (
        P(None, "tile"),
        P(None, "tile"),
        P(None, "tile"),
        P("view", None, "tile", None),
        P(),
        P(),
        P(),
        P(),
        P("tile", None, None),
        P("tile", None),
        P("view", "tile", None, None),
        P("tile", None),
    )
    return jax.shard_map(
        shards,
        mesh=mesh,
        in_specs=placed,
        out_specs=(P(None, "tile"), P(None, "tile"), P(None, "tile"), P()),
        check_vma=False,
    )
```

```python
import functools
import math

import jax
import jax.numpy as jnp
from jax import lax
from jax.experimental import pallas as pl
from jax.experimental.pallas import tpu as pltpu
from jax.sharding import PartitionSpec as P

STEP_COUNT = 20
LIST = 256


def extended(block, sides, width):
    for axis, dim in sides:
        count = lax.axis_size(axis)
        forward = [(i, i + 1) for i in range(count - 1)]
        backward = [(target, source) for source, target in forward]
        low = lax.ppermute(
            lax.slice_in_dim(block, block.shape[dim] - width, None, axis=dim), axis, forward
        )
        high = lax.ppermute(lax.slice_in_dim(block, 0, width, axis=dim), axis, backward)
        block = jnp.concatenate([low, block, high], axis=dim)
    return block


def window_taps():
    raw_taps = [math.exp(-(position - 5) * (position - 5) / 4.5) for position in range(11)]
    return [element / sum(raw_taps) for element in raw_taps]


def harmonics(unit_x, unit_y, unit_z):
    square_x = unit_x * unit_x
    square_y = unit_y * unit_y
    square_z = unit_z * unit_z
    return [
        0.28209479177387814 * jnp.ones_like(unit_x),
        -0.4886025119029199 * unit_y,
        0.4886025119029199 * unit_z,
        -0.4886025119029199 * unit_x,
        1.0925484305920792 * unit_x * unit_y,
        -1.0925484305920792 * unit_y * unit_z,
        0.31539156525252005 * (2.0 * square_z - square_x - square_y),
        -1.0925484305920792 * unit_x * unit_z,
        0.5462742152960396 * (square_x - square_y),
        -0.5900435899266435 * unit_y * (3.0 * square_x - square_y),
        2.890611442640554 * unit_x * unit_y * unit_z,
        -0.4570457994644658 * unit_y * (4.0 * square_z - square_x - square_y),
        0.3731763325901154 * unit_z * (2.0 * square_z - 3.0 * square_x - 3.0 * square_y),
        -0.4570457994644658 * unit_x * (4.0 * square_z - square_x - square_y),
        1.445305721320277 * unit_z * (square_x - square_y),
        -0.5900435899266435 * unit_x * (square_x - 3.0 * square_y),
    ]


MESH = pl.DeviceIdType.MESH
VMEM_LIMIT = 56 * 1024 * 1024
NN = (((1,), (0,)), ((), ()))
NT = (((1,), (1,)), ((), ()))
TN = (((0,), (0,)), ((), ()))


def mxu(left, right, dims):
    return lax.dot_general(left, right, dims, preferred_element_type=jnp.float32)


def split2(value):
    high = value.astype(jnp.bfloat16)
    low = (value - high.astype(jnp.float32)).astype(jnp.bfloat16)
    return high, low


def split3(value):
    high = value.astype(jnp.bfloat16)
    rest = value - high.astype(jnp.float32)
    middle = rest.astype(jnp.bfloat16)
    low = (rest - middle.astype(jnp.float32)).astype(jnp.bfloat16)
    return high, middle, low


def project_rows(rows, cameras):
    pos_x, pos_y, pos_z = rows[0:3]
    scales = [jnp.exp(row) for row in rows[3:6]]
    quat_w, quat_x, quat_y, quat_z = rows[6:10]
    norm = 1.0 / jnp.sqrt(
        quat_w * quat_w + quat_x * quat_x + quat_y * quat_y + quat_z * quat_z
    )
    quat_w, quat_x, quat_y, quat_z = quat_w * norm, quat_x * norm, quat_y * norm, quat_z * norm
    rotation = [
        [
            1.0 - 2.0 * (quat_y * quat_y + quat_z * quat_z),
            2.0 * (quat_x * quat_y - quat_w * quat_z),
            2.0 * (quat_x * quat_z + quat_w * quat_y),
        ],
        [
            2.0 * (quat_x * quat_y + quat_w * quat_z),
            1.0 - 2.0 * (quat_x * quat_x + quat_z * quat_z),
            2.0 * (quat_y * quat_z - quat_w * quat_x),
        ],
        [
            2.0 * (quat_x * quat_z - quat_w * quat_y),
            2.0 * (quat_y * quat_z + quat_w * quat_x),
            1.0 - 2.0 * (quat_x * quat_x + quat_y * quat_y),
        ],
    ]
    opacity = 1.0 / (1.0 + jnp.exp(-rows[10]))
    records = []
    for shear_x, shear_y, offset_x, offset_y, center_x, center_y, center_z in cameras:
        first = [(rotation[0][k] + shear_x * rotation[2][k]) * scales[k] for k in range(3)]
        second = [(rotation[1][k] + shear_y * rotation[2][k]) * scales[k] for k in range(3)]
        cov_xx = first[0] * first[0] + first[1] * first[1] + first[2] * first[2] + 0.3
        cov_yy = second[0] * second[0] + second[1] * second[1] + second[2] * second[2] + 0.3
        cov_xy = first[0] * second[0] + first[1] * second[1] + first[2] * second[2]
        inverse = 1.0 / (cov_xx * cov_yy - cov_xy * cov_xy)
        toward_x = pos_x - center_x
        toward_y = pos_y - center_y
        toward_z = pos_z - center_z
        shrink = 1.0 / jnp.sqrt(toward_x * toward_x + toward_y * toward_y + toward_z * toward_z)
        basis = harmonics(toward_x * shrink, toward_y * shrink, toward_z * shrink)
        colors = []
        for c in range(3):
            total = basis[0] * rows[11 + c]
            for k in range(1, 16):
                total = total + basis[k] * rows[11 + 3 * k + c]
            colors.append(0.5 + total)
        records.append(
            [
                pos_x + shear_x * pos_z + offset_x,
                pos_y + shear_y * pos_z + offset_y,
                cov_yy * inverse,
                -cov_xy * inverse,
                cov_xx * inverse,
                opacity,
                *colors,
            ]
        )
    return records


def camera_of(refs, view):
    shear_ref, offset_ref, center_ref = refs
    return (
        shear_ref[view, 0],
        shear_ref[view, 1],
        offset_ref[view, 0],
        offset_ref[view, 1],
        center_ref[view, 0],
        center_ref[view, 1],
        center_ref[view, 2],
    )


BLOCK = 4096


def dense_rows(source_ref, sub):
    count = source_ref.shape[0]
    columns = pl.ds(pl.multiple_of(1024 * sub, 1024), 1024)
    rows = []
    for first in range(0, count, 8):
        size = min(8, count - first)
        block = source_ref[first : first + size, columns].reshape(size, 8, 128)
        rows += [block[r] for r in range(size)]
    return rows


def project_kernel(
    params_ref, index_ref, view_ref, shear_ref, offset_ref, center_ref, out_ref, table, high_parts, low_parts
):
    step = pl.program_id(0)
    camera = camera_of((shear_ref, offset_ref, center_ref), view_ref[0])

    def part(sub, carry):
        record = project_rows(dense_rows(params_ref, sub), [camera])[0]
        first = pl.multiple_of(step * (BLOCK // 128) + 8 * sub, 8)
        for q in range(9):
            table[q, pl.ds(first, 8), :] = record[q]
        return carry

    lax.fori_loop(0, BLOCK // 1024, part, 0, unroll=2)

    @pl.when(step == pl.num_programs(0) - 1)
    def _():
        for q in range(9):
            for half in range(2):
                store_parts(
                    table[q, 64 * half : 64 * half + 64, :],
                    high_parts, low_parts, q, pl.ds(128 * half, 128),
                )
        low_ids = lax.broadcasted_iota(jnp.int32, (256, 256), 0)
        high_ids = lax.broadcasted_iota(jnp.int32, (64, 256), 0)

        def pick(pair, carry):
            index = jnp.concatenate(
                [index_ref[pl.ds(pair, 1), :], index_ref[pl.ds(pair + 32, 1), :]], axis=1
            )
            high = (index >> 7) & 63
            low = (index & 127) + ((index >> 13) << 7)
            rows = pick_rows(high_parts, low_parts, one_hot(low_ids, low), high_ids == high)
            for q in range(9):
                out_ref[pair, q : q + 1, :] = rows[q][:, 0:128]
                out_ref[pair + 32, q : q + 1, :] = rows[q][:, 128:256]
            return carry

        lax.fori_loop(0, 32, pick, 0, unroll=4)


def project_and_pick(params, send_index, view, shear, offset, center):
    smem = pl.BlockSpec(memory_space=pltpu.SMEM)
    return pl.pallas_call(
        project_kernel,
        grid=(16384 // BLOCK,),
        out_shape=jax.ShapeDtypeStruct((64, 9, 128), jnp.float32),
        in_specs=[
            pl.BlockSpec((59, BLOCK), lambda i: (0, i)),
            pl.BlockSpec((64, 128), lambda i: (0, 0)),
            smem,
            smem,
            smem,
            smem,
        ],
        out_specs=pl.BlockSpec((64, 9, 128), lambda i: (0, 0, 0)),
        scratch_shapes=[
            pltpu.VMEM((9, 128, 128), jnp.float32),
            pltpu.VMEM((576, 512), jnp.bfloat16),
            pltpu.VMEM((128, 256), jnp.bfloat16),
        ],
        compiler_params=pltpu.CompilerParams(vmem_limit_bytes=VMEM_LIMIT),
        name="project_and_pick",
    )(params, send_index, view, shear, offset, center)


def axis_peers(me, stride):
    place = lax.rem(me // stride, 4)
    return [me + (lax.rem(place + j, 4) - place) * stride for j in range(1, 4)]


def signal_all(semaphore, peers):
    for peer in peers:
        pl.semaphore_signal(semaphore, inc=1, device_id={"tile": peer}, device_id_type=MESH)


def exchange_kernel(in_ref, out_ref, send_sem, recv_sem, local_sem, plane_sem, cube_sem):
    total = lax.axis_size("tile")
    me = lax.axis_index("tile")
    barrier = pltpu.get_barrier_semaphore()
    lines = [axis_peers(me, stride) for stride in (1, 4, 16)]
    for line in lines:
        signal_all(barrier, line)
    own = pltpu.make_async_copy(in_ref.at[me], out_ref.at[me], local_sem)
    own.start()
    pl.semaphore_wait(barrier, 9)
    signal_all(plane_sem, lines[1])
    pl.semaphore_wait(plane_sem, 3)
    signal_all(cube_sem, lines[2])
    pl.semaphore_wait(cube_sem, 3)

    def copy_to(p):
        peer = lax.rem(me + p, total)
        return pltpu.make_async_remote_copy(
            src_ref=in_ref.at[peer],
            dst_ref=out_ref.at[me],
            send_sem=send_sem.at[p],
            recv_sem=recv_sem.at[p],
            device_id={"tile": peer},
            device_id_type=MESH,
        )

    def send(p, carry):
        copy_to(p).start()
        return carry

    def finish(p, carry):
        copy_to(p).wait()
        return carry

    lax.fori_loop(1, total, send, 0)
    own.wait()
    lax.fori_loop(1, total, finish, 0)


def exchange(blocks, collective_id):
    vmem = pl.BlockSpec(memory_space=pltpu.VMEM)
    total = blocks.shape[0]
    return pl.pallas_call(
        exchange_kernel,
        out_shape=jax.ShapeDtypeStruct(blocks.shape, blocks.dtype),
        in_specs=[vmem],
        out_specs=vmem,
        scratch_shapes=[
            pltpu.SemaphoreType.DMA((total,)),
            pltpu.SemaphoreType.DMA((total,)),
            pltpu.SemaphoreType.DMA,
            pltpu.SemaphoreType.REGULAR,
            pltpu.SemaphoreType.REGULAR,
        ],
        compiler_params=pltpu.CompilerParams(
            collective_id=collective_id, has_side_effects=True, vmem_limit_bytes=VMEM_LIMIT
        ),
        name="exchange",
    )(blocks)


TILES_STEP = 8
CHUNK = 16
UNROLL = 4


def slot_place(index):
    return (index >> 7) & 31, (index & 127) + ((index >> 12) << 7)


def one_hot(ids, values):
    return (ids == values).astype(jnp.float32).astype(jnp.bfloat16)


def store_parts(rows, high_parts, low_parts, q, columns):
    count = rows.shape[0]
    high, middle, low = split3(rows)
    here = pl.ds(count * q, count)
    width = columns.size
    high_parts[here, columns] = high
    high_parts[here, pl.ds(columns.start + 256, width)] = middle
    if q < 2:
        low_parts[here, columns] = low


def both_parts(value, right, dims):
    sums = mxu(jnp.concatenate(split2(value), axis=0), right, dims)
    return sums[: value.shape[0]] + sums[value.shape[0] :]


def pick_rows(high_parts, low_parts, hot, mask):
    count = mask.shape[0]
    found = mxu(high_parts[...], jnp.concatenate([hot, hot], axis=0), NN)
    found_low = mxu(low_parts[...], hot, NN)
    rows = []
    for q in range(9):
        part = found[count * q : count * q + count]
        if q < 2:
            part = part + found_low[count * q : count * q + count]
        rows.append(jnp.sum(jnp.where(mask, part, 0.0), axis=0, keepdims=True))
    return rows


def tile_deltas(tile, band, u_row, w_row):
    offsets = lax.broadcasted_iota(jnp.int32, (16, 256), 0)
    pixel_x = (offsets + 16 * tile).astype(jnp.float32) + 0.5
    pixel_y = (offsets + 16 * band).astype(jnp.float32) + 0.5
    return pixel_x - u_row, pixel_y - w_row


def forward_kernel(
    slots_ref, list_ref, count_ref, band_ref, view_ref, back_ref,
    image_ref, entry_ref, cover_ref, keep_ref,
    high_parts, low_parts, before, picked, total,
):
    step = pl.program_id(0)
    view = view_ref[0]
    band = band_ref[0]
    lanes = lax.broadcasted_iota(jnp.int32, (1, 256), 1)

    @pl.when(step == 0)
    def _():
        for q in range(9):
            for half in range(2):
                store_parts(
                    slots_ref[32 * half : 32 * half + 32, q, :],
                    high_parts, low_parts, q, pl.ds(128 * half, 128),
                )
        row_ids = lax.broadcasted_iota(jnp.int32, (256, 256), 0)
        column_ids = lax.broadcasted_iota(jnp.int32, (256, 256), 1)
        before[...] = (row_ids < column_ids).astype(jnp.float32).astype(jnp.bfloat16)
        total[...] = jnp.zeros_like(total)
        high_ids = lax.broadcasted_iota(jnp.int32, (32, 256), 0)

        def pick(tile, carry):
            high, low = slot_place(list_ref[pl.ds(tile, 1), :])
            rows = pick_rows(high_parts, low_parts, one_hot(row_ids, low), high_ids == high)
            rows[5] = jnp.where(lanes < count_ref[0, tile], rows[5], 0.0)
            for c in range(3):
                rows[6 + c] = rows[6 + c] - back_ref[view, c]
            for q in range(9):
                picked[tile, q : q + 1, :] = rows[q]
            return carry

        lax.fori_loop(0, 32, pick, 0, unroll=4)

    color_ids = lax.broadcasted_iota(jnp.int32, (128, 256), 0)

    def one(k, carry):
        tile = step * TILES_STEP + k
        rows = [picked[tile, q : q + 1, :] for q in range(9)]
        for q in range(9):
            entry_ref[k, q : q + 1, :] = rows[q]
        delta_x, delta_y = tile_deltas(tile, band, rows[0], rows[1])
        along_x = -0.5 * rows[2] * delta_x * delta_x
        mixed = -rows[3] * delta_x
        along_y = -0.5 * rows[4] * delta_y * delta_y
        colors = jnp.zeros((128, 256), jnp.float32)
        for c in range(3):
            colors = jnp.where(color_ids == 3 * tile + c, rows[6 + c], colors)
        colors = jnp.concatenate(split2(colors), axis=0)
        for first in range(0, 16, CHUNK):
            pieces = []
            for i in range(first, first + CHUNK):
                exponent = along_x + (mixed * delta_y[i : i + 1] + along_y[i : i + 1])
                pieces.append(rows[5] * jnp.exp(exponent))
            cover = jnp.concatenate(pieces, axis=0)
            keep = jnp.exp(both_parts(jnp.log(1.0 - cover), before[...], NN))
            here = slice(16 * first, 16 * (first + CHUNK))
            cover_ref[k, here] = cover
            keep_ref[k, here] = keep
            shown = mxu(jnp.concatenate(split2(cover * keep), axis=0), colors, NT)
            size = 16 * CHUNK
            total[here] += shown[0:size, 0:128] + shown[0:size, 128:256] + shown[size:, 0:128]
        return carry

    lax.fori_loop(0, TILES_STEP, one, 0, unroll=UNROLL)

    @pl.when(step == pl.num_programs(0) - 1)
    def _():
        image_ref[...] = jnp.transpose(total[...])


def render_forward(slots, lists, counts, band, view, back):
    smem = pl.BlockSpec(memory_space=pltpu.SMEM)
    field = jax.ShapeDtypeStruct((32, 256, 256), jnp.float32)
    field_spec = pl.BlockSpec((TILES_STEP, 256, 256), lambda i: (i, 0, 0))
    return pl.pallas_call(
        forward_kernel,
        grid=(32 // TILES_STEP,),
        out_shape=(
            jax.ShapeDtypeStruct((128, 256), jnp.float32),
            jax.ShapeDtypeStruct((32, 9, 256), jnp.float32),
            field,
            field,
        ),
        in_specs=[
            pl.BlockSpec((64, slots.shape[1], 128), lambda i: (0, 0, 0)),
            pl.BlockSpec((32, 256), lambda i: (0, 0)),
            smem,
            smem,
            smem,
            smem,
        ],
        out_specs=(
            pl.BlockSpec((128, 256), lambda i: (0, 0)),
            pl.BlockSpec((TILES_STEP, 9, 256), lambda i: (i, 0, 0)),
            field_spec,
            field_spec,
        ),
        scratch_shapes=[
            pltpu.VMEM((288, 512), jnp.bfloat16),
            pltpu.VMEM((64, 256), jnp.bfloat16),
            pltpu.VMEM((256, 256), jnp.bfloat16),
            pltpu.VMEM((32, 9, 256), jnp.float32),
            pltpu.VMEM((256, 128), jnp.float32),
        ],
        compiler_params=pltpu.CompilerParams(vmem_limit_bytes=VMEM_LIMIT),
        name="render_forward",
    )(slots, lists, counts, band, view, back)


def backward_kernel(
    entry_ref, cover_ref, keep_ref, grad_ref, list_ref, band_ref, loss_ref, out_ref,
    after, total, results, high_weights, low_weights,
):
    step = pl.program_id(0)

    @pl.when(step == 0)
    def _():
        row_ids = lax.broadcasted_iota(jnp.int32, (256, 256), 0)
        column_ids = lax.broadcasted_iota(jnp.int32, (256, 256), 1)
        after[...] = (row_ids > column_ids).astype(jnp.float32).astype(jnp.bfloat16)

    band = band_ref[0]

    def fold(value):
        return jnp.sum(value, axis=0, keepdims=True)

    def one(k, carry):
        tile = step * TILES_STEP + k
        rows = [entry_ref[k, q : q + 1, :] for q in range(9)]
        grads = jnp.concatenate([grad_ref[c, pl.ds(tile, 1), :] for c in range(3)], axis=0)
        colors = jnp.concatenate(rows[6:9], axis=0)
        grads_high = grads.astype(jnp.bfloat16).astype(jnp.float32)
        grads_low = grads - grads_high
        colors_high = colors.astype(jnp.bfloat16).astype(jnp.float32)
        colors_low = colors - colors_high
        blank = jnp.zeros((7, 256), jnp.float32)
        left = jnp.concatenate([grads_high, grads_high, grads_low, blank], axis=0).astype(jnp.bfloat16)
        right = jnp.concatenate([colors_high, colors_low, colors_high, blank], axis=0).astype(jnp.bfloat16)
        both = jnp.concatenate([grads_high, grads_low, blank, blank[0:3]], axis=0).astype(jnp.bfloat16)
        delta_x, delta_y = tile_deltas(tile, band, rows[0], rows[1])
        sum_0 = jnp.zeros((16, 256), jnp.float32)
        sum_y = sum_0
        sum_yy = sum_0
        for first in range(0, 16, CHUNK):
            here = slice(16 * first, 16 * (first + CHUNK))
            shade = mxu(left[:, here], right, TN)
            cover = cover_ref[k, here]
            weight = cover * keep_ref[k, here]
            weight_high, weight_low = split2(weight)
            high_weights[k % 2, here] = weight_high
            low_weights[k % 2, here] = weight_low
            lit = weight * shade
            behind = both_parts(lit, after[...], NN)
            pull = lit - behind * (cover / (1.0 - cover))
            for i in range(CHUNK):
                piece = pull[16 * i : 16 * i + 16]
                level = delta_y[first + i : first + i + 1]
                piece_y = piece * level
                sum_0 = sum_0 + piece
                sum_y = sum_y + piece_y
                sum_yy = sum_yy + piece_y * level
        color_grad = mxu(both, high_weights[k % 2], NN)
        color_grad = color_grad[0:3] + color_grad[3:6] + mxu(both, low_weights[k % 2], NN)[0:3]
        sum_x = sum_0 * delta_x
        moment_0 = fold(sum_0)
        moment_x = fold(sum_x)
        moment_xx = fold(sum_x * delta_x)
        moment_y = fold(sum_y)
        moment_xy = fold(sum_y * delta_x)
        moment_yy = fold(sum_yy)
        live = rows[5] > 0.0
        values = [
            rows[2] * moment_x + rows[3] * moment_y,
            rows[4] * moment_y + rows[3] * moment_x,
            -0.5 * moment_xx,
            -moment_xy,
            -0.5 * moment_yy,
            jnp.where(live, moment_0 / jnp.where(live, rows[5], 1.0), 0.0),
            color_grad[0:1],
            color_grad[1:2],
            color_grad[2:3],
        ]
        for q in range(9):
            results[tile, q : q + 1, :] = values[q]
        return carry

    lax.fori_loop(0, TILES_STEP, one, 0, unroll=UNROLL)

    @pl.when(step == pl.num_programs(0) - 1)
    def _():
        low_ids = lax.broadcasted_iota(jnp.int32, (256, 256), 0)
        high_ids = lax.broadcasted_iota(jnp.int32, (32, 256), 0)
        total[...] = jnp.zeros_like(total)

        def place(tile, carry):
            high, low = slot_place(list_ref[pl.ds(tile, 1), :])
            place_rows([results[tile, q : q + 1, :] for q in range(9)], total, one_hot(low_ids, low), high_ids == high)
            return carry

        lax.fori_loop(0, 32, place, 0, unroll=4)
        for q in range(9):
            for half in range(2):
                out_ref[32 * half : 32 * half + 32, q, :] = total[
                    32 * q : 32 * q + 32, 128 * half : 128 * half + 128
                ]
        out_ref[:, 9, :] = jnp.broadcast_to(loss_ref[...], (64, 128))


def place_rows(rows, total, hot, mask):
    count = mask.shape[0]
    high_rows, low_rows = [], []
    for row in rows:
        high = row.astype(jnp.bfloat16).astype(jnp.float32)
        high_rows.append(jnp.where(mask, high, 0.0))
        low_rows.append(jnp.where(mask, row - high, 0.0))
    placed = jnp.concatenate(high_rows + low_rows, axis=0).astype(jnp.bfloat16)
    sums = mxu(placed, hot, NT)
    total[...] += sums[: 9 * count] + sums[9 * count :]


def render_backward(entries, cover, keep, grads, lists, band, loss):
    smem = pl.BlockSpec(memory_space=pltpu.SMEM)
    field_spec = pl.BlockSpec((TILES_STEP, 256, 256), lambda i: (i, 0, 0))
    return pl.pallas_call(
        backward_kernel,
        grid=(32 // TILES_STEP,),
        out_shape=jax.ShapeDtypeStruct((64, 10, 128), jnp.float32),
        in_specs=[
            pl.BlockSpec((TILES_STEP, 9, 256), lambda i: (i, 0, 0)),
            field_spec,
            field_spec,
            pl.BlockSpec((3, 32, 256), lambda i: (0, 0, 0)),
            pl.BlockSpec((32, 256), lambda i: (0, 0)),
            smem,
            pl.BlockSpec((1, 128), lambda i: (0, 0)),
        ],
        out_specs=pl.BlockSpec((64, 10, 128), lambda i: (0, 0, 0)),
        scratch_shapes=[
            pltpu.VMEM((256, 256), jnp.bfloat16),
            pltpu.VMEM((288, 256), jnp.float32),
            pltpu.VMEM((32, 9, 256), jnp.float32),
            pltpu.VMEM((2, 256, 256), jnp.bfloat16),
            pltpu.VMEM((2, 256, 256), jnp.bfloat16),
        ],
        compiler_params=pltpu.CompilerParams(vmem_limit_bytes=VMEM_LIMIT),
        name="render_backward",
    )(entries, cover, keep, grads, lists, band, loss)
def place_kernel(returned_ref, index_ref, count_ref, out_ref, total):
    total[...] = jnp.zeros_like(total)
    low_ids = lax.broadcasted_iota(jnp.int32, (256, 256), 0)
    high_ids = lax.broadcasted_iota(jnp.int32, (64, 256), 0)
    lanes = lax.broadcasted_iota(jnp.int32, (1, 128), 1)

    def place(pair, carry):
        def joined(values):
            return jnp.concatenate(values, axis=1)

        bands = (pair, pair + 32)
        index = joined([index_ref[pl.ds(d, 1), :] for d in bands])
        live = joined([(lanes < count_ref[0, d]).astype(jnp.int32) for d in bands])
        high = jnp.where(live > 0, (index >> 7) & 63, -1)
        low = (index & 127) + ((index >> 13) << 7)
        rows = [joined([returned_ref[d, q : q + 1, :] for d in bands]) for q in range(9)]
        place_rows(rows, total, one_hot(low_ids, low), high_ids == high)
        return carry

    lax.fori_loop(0, 32, place, 0, unroll=4)
    for q in range(9):
        for half in range(2):
            out_ref[q, 64 * half : 64 * half + 64, :] = total[
                64 * q : 64 * q + 64, 128 * half : 128 * half + 128
            ]
    loss = jnp.sum(returned_ref[:, 9, :], axis=0, keepdims=True)
    out_ref[9] = jnp.broadcast_to(loss, (128, 128))


def place_gradients(returned, send_index, send_count):
    vmem = pl.BlockSpec(memory_space=pltpu.VMEM)
    return pl.pallas_call(
        place_kernel,
        out_shape=jax.ShapeDtypeStruct((10, 128, 128), jnp.float32),
        in_specs=[vmem, vmem, pl.BlockSpec(memory_space=pltpu.SMEM)],
        out_specs=vmem,
        scratch_shapes=[pltpu.VMEM((576, 256), jnp.float32)],
        compiler_params=pltpu.CompilerParams(vmem_limit_bytes=VMEM_LIMIT),
        name="place_gradients",
    )(returned, send_index, send_count)


RATES = [0.016] * 3 + [0.005] * 3 + [0.001] * 4 + [0.05] + [0.0025] * 3 + [0.000125] * 45
LOSS_TERMS = 2 * 3 * 1024 * 512


def update_kernel(
    params_ref, first_ref, second_ref, own_ref, other_ref, view_ref, shear_ref, offset_ref, center_ref,
    params_out, first_out, second_out, loss_out, dense,
):
    refs = (shear_ref, offset_ref, center_ref)
    cameras = [camera_of(refs, 0), camera_of(refs, 1)]
    is_first = view_ref[0] == 0
    loss_out[...] = (own_ref[9, 0:1, 0:1] + other_ref[9, 0:1, 0:1]) / LOSS_TERMS

    def part(sub, carry):
        rows = dense_rows(params_ref, sub)
        _, pull_back = jax.vjp(lambda *values: project_rows(values, cameras), *rows)
        here = pl.ds(pl.multiple_of(8 * sub, 8), 8)
        own = [own_ref[q, here, :] for q in range(9)]
        other = [other_ref[q, here, :] for q in range(9)]
        gradient = pull_back(
            [
                [jnp.where(is_first, a, b) for a, b in zip(own, other)],
                [jnp.where(is_first, b, a) for a, b in zip(own, other)],
            ]
        )
        for r in range(59):
            dense[8 * r : 8 * r + 8, :] = gradient[r]
        for first in range(0, 59, 8):
            size = min(8, 59 - first)
            row_ids = lax.broadcasted_iota(jnp.int32, (size, 128), 0)
            rate = jnp.full((size, 128), RATES[first], jnp.float32)
            for r in range(1, size):
                if RATES[first + r] != RATES[first + r - 1]:
                    rate = jnp.where(row_ids >= r, RATES[first + r], rate)
            rate = rate / (1.0 - 0.9**STEP_COUNT)
            for c in range(8):
                columns = pl.ds(pl.multiple_of(1024 * sub + 128 * c, 128), 128)
                here = (slice(first, first + size), columns)
                grad = dense[pl.ds(8 * first + c, size, stride=8), :]
                new_first = 0.9 * first_ref[here] + 0.1 * grad
                new_second = 0.999 * second_ref[here] + 0.001 * grad * grad
                scale = jnp.sqrt(new_second * (1.0 / (1.0 - 0.999**STEP_COUNT))) + 1e-15
                params_out[here] = params_ref[here] - rate * new_first / scale
                first_out[here] = new_first
                second_out[here] = new_second
        return carry

    lax.fori_loop(0, BLOCK // 1024, part, 0)


def update(params, first_moment, second_moment, own, other, view, shear, offset, center):
    smem = pl.BlockSpec(memory_space=pltpu.SMEM)
    block = pl.BlockSpec((59, BLOCK), lambda i: (0, i))
    grads = pl.BlockSpec((10, BLOCK // 128, 128), lambda i: (0, i, 0))
    shape = jax.ShapeDtypeStruct(params.shape, jnp.float32)
    return pl.pallas_call(
        update_kernel,
        grid=(16384 // BLOCK,),
        out_shape=(shape, shape, shape, jax.ShapeDtypeStruct((1, 1), jnp.float32)),
        in_specs=[block, block, block, grads, grads, smem, smem, smem, smem],
        out_specs=(block, block, block, pl.BlockSpec((1, 1), lambda i: (0, 0))),
        scratch_shapes=[pltpu.VMEM((59 * 8, 128), jnp.float32)],
        compiler_params=pltpu.CompilerParams(vmem_limit_bytes=VMEM_LIMIT),
        name="update",
    )(params, first_moment, second_moment, own, other, view, shear, offset, center)


def gaussian_blur(planes):
    taps = window_taps()
    rows_out = planes.shape[1] - 10
    vertical = taps[0] * planes[:, 0:rows_out]
    for position in range(1, 11):
        vertical = vertical + taps[position] * planes[:, position : position + rows_out]
    image_width = planes.shape[2]
    padded = jnp.pad(vertical, ((0, 0), (0, 0), (5, 5)))
    result = taps[0] * padded[:, :, 0:image_width]
    for position in range(1, 11):
        result = result + taps[position] * padded[:, :, position : position + image_width]
    return result


def ssim_map(level_x, level_y, energy_x, energy_y, product_xy):
    upper = (2.0 * level_x * level_y + 0.0001) * (2.0 * (product_xy - level_x * level_y) + 0.0009)
    lower = (level_x * level_x + level_y * level_y + 0.0001) * (
        energy_x - level_x * level_x + (energy_y - level_y * level_y) + 0.0009
    )
    return upper / lower


def window_stats(widened):
    shown = widened[0:3]
    truth = widened[3:6]
    mean_x = gaussian_blur(shown)
    mean_y = gaussian_blur(truth)
    power_x = gaussian_blur(shown * shown)
    power_y = gaussian_blur(truth * truth)
    cross_xy = gaussian_blur(shown * truth)
    return (mean_x, mean_y, power_x, power_y, cross_xy)


def shards(
    params,
    first_moment,
    second_moment,
    target,
    view_shear,
    view_offset,
    cam_center,
    background,
    send_index,
    send_count,
    tile_list,
    tile_count,
):
    view_index = lax.axis_index("view")
    band_index = lax.axis_index("tile")

    view = view_index.astype(jnp.int32).reshape(1)
    band = band_index.astype(jnp.int32).reshape(1)
    backdrop = lax.dynamic_index_in_dim(background, view_index, 0, keepdims=False)
    outgoing = project_and_pick(params, send_index[0], view, view_shear, view_offset, cam_center)
    incoming = exchange(outgoing, 0)
    shown, entries, cover, keep = render_forward(
        incoming, tile_list[0, 0], tile_count, band, view, background
    )
    image_band = shown[:96].reshape(32, 3, 16, 16).transpose(1, 2, 0, 3).reshape(3, 16, 512)
    image_band = image_band + backdrop[:, None, None]
    frame_band = target[0]
    stacked = jnp.concatenate([image_band, frame_band], axis=0)
    widened = extended(stacked, (("tile", 1),), 5)
    mean_x, mean_y, power_x, power_y, cross_xy = window_stats(widened)
    similarity, ssim_back = jax.vjp(
        lambda level_x, energy_x, product_xy: ssim_map(
            level_x, mean_y, energy_x, power_y, product_xy
        ),
        mean_x,
        power_x,
        cross_xy,
    )
    grad_mean, grad_power, grad_cross = ssim_back(jnp.full_like(similarity, -0.8))
    spread = extended(
        jnp.concatenate([grad_mean, grad_power, grad_cross], axis=0), (("tile", 1),), 5
    )
    blurred = gaussian_blur(spread)
    difference = image_band - frame_band
    smooth = jnp.sqrt(difference * difference + 0.0001)
    loss_part = jnp.sum(0.2 * smooth + 0.8 * (1.0 - similarity))
    pixel_grad = (
        0.2 * difference / smooth
        + blurred[0:3]
        + 2.0 * image_band * blurred[3:6]
        + frame_band * blurred[6:9]
    )
    grad_tiles = pixel_grad.reshape(3, 16, 32, 16).transpose(0, 2, 1, 3).reshape(3, 32, 256)
    loss_row = jnp.broadcast_to(loss_part, (1, 128))
    slot_grad = render_backward(entries, cover, keep, grad_tiles, tile_list[0, 0], band, loss_row)
    returned = exchange(slot_grad, 1)
    own_grad = place_gradients(returned, send_index[0], send_count)
    other_grad = lax.ppermute(own_grad, "view", [(0, 1), (1, 0)])
    new_params, new_first, new_second, mean_loss = update(
        params, first_moment, second_moment, own_grad, other_grad, view, view_shear, view_offset, cam_center
    )
    return (new_params, new_first, new_second, mean_loss[0, 0])


def solution(mesh):
    placed = (
        P(None, "tile"),
        P(None, "tile"),
        P(None, "tile"),
        P("view", None, "tile", None),
        P(),
        P(),
        P(),
        P(),
        P("tile", None, None),
        P("tile", None),
        P("view", "tile", None, None),
        P("tile", None),
    )
    return jax.shard_map(
        shards,
        mesh=mesh,
        in_specs=placed,
        out_specs=(P(None, "tile"), P(None, "tile"), P(None, "tile"), P()),
        check_vma=False,
    )
```

```python
import functools
import math

import jax
import jax.numpy as jnp
from jax import lax
from jax.experimental import pallas as pl
from jax.experimental.pallas import tpu as pltpu
from jax.sharding import PartitionSpec as P

STEP_COUNT = 20
LIST = 256


def window_taps():
    raw_taps = [math.exp(-(position - 5) * (position - 5) / 4.5) for position in range(11)]
    return [element / sum(raw_taps) for element in raw_taps]


def harmonics(unit_x, unit_y, unit_z):
    square_x = unit_x * unit_x
    square_y = unit_y * unit_y
    square_z = unit_z * unit_z
    return [
        0.28209479177387814 * jnp.ones_like(unit_x),
        -0.4886025119029199 * unit_y,
        0.4886025119029199 * unit_z,
        -0.4886025119029199 * unit_x,
        1.0925484305920792 * unit_x * unit_y,
        -1.0925484305920792 * unit_y * unit_z,
        0.31539156525252005 * (2.0 * square_z - square_x - square_y),
        -1.0925484305920792 * unit_x * unit_z,
        0.5462742152960396 * (square_x - square_y),
        -0.5900435899266435 * unit_y * (3.0 * square_x - square_y),
        2.890611442640554 * unit_x * unit_y * unit_z,
        -0.4570457994644658 * unit_y * (4.0 * square_z - square_x - square_y),
        0.3731763325901154 * unit_z * (2.0 * square_z - 3.0 * square_x - 3.0 * square_y),
        -0.4570457994644658 * unit_x * (4.0 * square_z - square_x - square_y),
        1.445305721320277 * unit_z * (square_x - square_y),
        -0.5900435899266435 * unit_x * (square_x - 3.0 * square_y),
    ]


MESH = pl.DeviceIdType.MESH
VMEM_LIMIT = 56 * 1024 * 1024
NN = (((1,), (0,)), ((), ()))
NT = (((1,), (1,)), ((), ()))
TN = (((0,), (0,)), ((), ()))


def mxu(left, right, dims):
    return lax.dot_general(left, right, dims, preferred_element_type=jnp.float32)


def split2(value):
    high = value.astype(jnp.bfloat16)
    low = (value - high.astype(jnp.float32)).astype(jnp.bfloat16)
    return high, low


def split3(value):
    high = value.astype(jnp.bfloat16)
    rest = value - high.astype(jnp.float32)
    middle = rest.astype(jnp.bfloat16)
    low = (rest - middle.astype(jnp.float32)).astype(jnp.bfloat16)
    return high, middle, low


def project_rows(rows, cameras):
    pos_x, pos_y, pos_z = rows[0:3]
    scales = [jnp.exp(row) for row in rows[3:6]]
    quat_w, quat_x, quat_y, quat_z = rows[6:10]
    norm = 1.0 / jnp.sqrt(
        quat_w * quat_w + quat_x * quat_x + quat_y * quat_y + quat_z * quat_z
    )
    quat_w, quat_x, quat_y, quat_z = quat_w * norm, quat_x * norm, quat_y * norm, quat_z * norm
    rotation = [
        [
            1.0 - 2.0 * (quat_y * quat_y + quat_z * quat_z),
            2.0 * (quat_x * quat_y - quat_w * quat_z),
            2.0 * (quat_x * quat_z + quat_w * quat_y),
        ],
        [
            2.0 * (quat_x * quat_y + quat_w * quat_z),
            1.0 - 2.0 * (quat_x * quat_x + quat_z * quat_z),
            2.0 * (quat_y * quat_z - quat_w * quat_x),
        ],
        [
            2.0 * (quat_x * quat_z - quat_w * quat_y),
            2.0 * (quat_y * quat_z + quat_w * quat_x),
            1.0 - 2.0 * (quat_x * quat_x + quat_y * quat_y),
        ],
    ]
    opacity = 1.0 / (1.0 + jnp.exp(-rows[10]))
    records = []
    for shear_x, shear_y, offset_x, offset_y, center_x, center_y, center_z in cameras:
        first = [(rotation[0][k] + shear_x * rotation[2][k]) * scales[k] for k in range(3)]
        second = [(rotation[1][k] + shear_y * rotation[2][k]) * scales[k] for k in range(3)]
        cov_xx = first[0] * first[0] + first[1] * first[1] + first[2] * first[2] + 0.3
        cov_yy = second[0] * second[0] + second[1] * second[1] + second[2] * second[2] + 0.3
        cov_xy = first[0] * second[0] + first[1] * second[1] + first[2] * second[2]
        inverse = 1.0 / (cov_xx * cov_yy - cov_xy * cov_xy)
        toward_x = pos_x - center_x
        toward_y = pos_y - center_y
        toward_z = pos_z - center_z
        shrink = 1.0 / jnp.sqrt(toward_x * toward_x + toward_y * toward_y + toward_z * toward_z)
        basis = harmonics(toward_x * shrink, toward_y * shrink, toward_z * shrink)
        colors = []
        for c in range(3):
            total = basis[0] * rows[11 + c]
            for k in range(1, 16):
                total = total + basis[k] * rows[11 + 3 * k + c]
            colors.append(0.5 + total)
        records.append(
            [
                pos_x + shear_x * pos_z + offset_x,
                pos_y + shear_y * pos_z + offset_y,
                cov_yy * inverse,
                -cov_xy * inverse,
                cov_xx * inverse,
                opacity,
                *colors,
            ]
        )
    return records


def camera_of(refs, view):
    shear_ref, offset_ref, center_ref = refs
    return (
        shear_ref[view, 0],
        shear_ref[view, 1],
        offset_ref[view, 0],
        offset_ref[view, 1],
        center_ref[view, 0],
        center_ref[view, 1],
        center_ref[view, 2],
    )


BLOCK = 4096


def dense_rows(source_ref, sub):
    count = source_ref.shape[0]
    columns = pl.ds(pl.multiple_of(1024 * sub, 1024), 1024)
    rows = []
    for first in range(0, count, 8):
        size = min(8, count - first)
        block = source_ref[first : first + size, columns].reshape(size, 8, 128)
        rows += [block[r] for r in range(size)]
    return rows


def axis_peers(me, stride):
    place = lax.rem(me // stride, 4)
    return [me + (lax.rem(place + j, 4) - place) * stride for j in range(1, 4)]


def signal_all(semaphore, peers):
    for peer in peers:
        pl.semaphore_signal(semaphore, inc=1, device_id={"tile": peer}, device_id_type=MESH)


def greet_all(step, semaphores):
    plane_sem, cube_sem = semaphores
    me = lax.axis_index("tile")
    lines = [axis_peers(me, stride) for stride in (1, 4, 16)]
    barrier = pltpu.get_barrier_semaphore()

    @pl.when(step == 0)
    def _():
        for line in lines:
            signal_all(barrier, line)

    @pl.when(step == 1)
    def _():
        pl.semaphore_wait(barrier, 9)
        signal_all(plane_sem, lines[1])

    @pl.when(step == 2)
    def _():
        pl.semaphore_wait(plane_sem, 3)
        signal_all(cube_sem, lines[2])

    @pl.when(step == 3)
    def _():
        pl.semaphore_wait(cube_sem, 3)


def block_copy(outgoing, incoming, send_sem, recv_sem, peer):
    me = lax.axis_index("tile")
    return pltpu.make_async_remote_copy(
        src_ref=outgoing.at[peer],
        dst_ref=incoming.at[me],
        send_sem=send_sem.at[peer],
        recv_sem=recv_sem.at[me],
        device_id={"tile": peer},
        device_id_type=MESH,
    )


def send_block(outgoing, incoming, send_sem, recv_sem, peer):
    @pl.when(peer != lax.axis_index("tile"))
    def _():
        block_copy(outgoing, incoming, send_sem, recv_sem, peer).start()


def finish_blocks(outgoing, incoming, send_sem, recv_sem):
    me = lax.axis_index("tile")
    incoming[me] = outgoing[me]

    def finish(p, carry):
        peer = lax.rem(me + p, 64)
        block_copy(outgoing, incoming, send_sem, recv_sem, peer).wait_send()
        pltpu.make_async_remote_copy(
            src_ref=outgoing.at[peer],
            dst_ref=incoming.at[peer],
            send_sem=send_sem.at[peer],
            recv_sem=recv_sem.at[peer],
            device_id={"tile": peer},
            device_id_type=MESH,
        ).wait_recv()
        return carry

    lax.fori_loop(1, 64, finish, 0)


def exchange_scratch(rows):
    return [
        pltpu.VMEM((64, rows, 128), jnp.float32),
        pltpu.VMEM((64, rows, 128), jnp.float32),
        pltpu.SemaphoreType.DMA((64,)),
        pltpu.SemaphoreType.DMA((64,)),
        pltpu.SemaphoreType.REGULAR,
        pltpu.SemaphoreType.REGULAR,
    ]


def project_kernel(
    params_ref, index_ref, view_ref, shear_ref, offset_ref, center_ref, out_ref,
    table, high_parts, low_parts, outgoing, incoming, send_sem, recv_sem, *greetings,
):
    step = pl.program_id(0)
    greet_all(step, greetings)
    camera = camera_of((shear_ref, offset_ref, center_ref), view_ref[0])

    def part(sub, carry):
        record = project_rows(dense_rows(params_ref, sub), [camera])[0]
        first = pl.multiple_of(step * (BLOCK // 128) + 8 * sub, 8)
        for q in range(9):
            table[q, pl.ds(first, 8), :] = record[q]
        return carry

    lax.fori_loop(0, BLOCK // 1024, part, 0, unroll=2)

    @pl.when(step == pl.num_programs(0) - 1)
    def _():
        for q in range(9):
            for half in range(2):
                store_parts(
                    table[q, 64 * half : 64 * half + 64, :],
                    high_parts, low_parts, q, pl.ds(128 * half, 128),
                )
        low_ids = lax.broadcasted_iota(jnp.int32, (256, 256), 0)
        high_ids = lax.broadcasted_iota(jnp.int32, (64, 256), 0)

        def pick(pair, carry):
            index = jnp.concatenate(
                [index_ref[pl.ds(pair, 1), :], index_ref[pl.ds(pair + 32, 1), :]], axis=1
            )
            high = (index >> 7) & 63
            low = (index & 127) + ((index >> 13) << 7)
            rows = pick_rows(high_parts, low_parts, one_hot(low_ids, low), high_ids == high)
            for q in range(9):
                outgoing[pair, q : q + 1, :] = rows[q][:, 0:128]
                outgoing[pair + 32, q : q + 1, :] = rows[q][:, 128:256]
            return carry

        me = lax.axis_index("tile")

        def group(part, carry):
            first = lax.rem(part + me, 4) * 8
            lax.fori_loop(0, 8, lambda k, carry: pick(first + k, carry), 0, unroll=4)

            def send(k, carry):
                for peer in (first + k, first + k + 32):
                    send_block(outgoing, incoming, send_sem, recv_sem, peer)
                return carry

            lax.fori_loop(0, 8, send, 0)
            return carry

        lax.fori_loop(0, 4, group, 0)
        finish_blocks(outgoing, incoming, send_sem, recv_sem)
        out_ref[...] = incoming[...]


def project_and_pick(params, send_index, view, shear, offset, center):
    smem = pl.BlockSpec(memory_space=pltpu.SMEM)
    return pl.pallas_call(
        project_kernel,
        grid=(16384 // BLOCK,),
        out_shape=jax.ShapeDtypeStruct((64, 9, 128), jnp.float32),
        in_specs=[
            pl.BlockSpec((59, BLOCK), lambda i: (0, i)),
            pl.BlockSpec((64, 128), lambda i: (0, 0)),
            smem,
            smem,
            smem,
            smem,
        ],
        out_specs=pl.BlockSpec((64, 9, 128), lambda i: (0, 0, 0)),
        scratch_shapes=[
            pltpu.VMEM((9, 128, 128), jnp.float32),
            pltpu.VMEM((576, 512), jnp.bfloat16),
            pltpu.VMEM((128, 256), jnp.bfloat16),
            *exchange_scratch(9),
        ],
        compiler_params=pltpu.CompilerParams(
            collective_id=0, has_side_effects=True, vmem_limit_bytes=VMEM_LIMIT
        ),
        name="project_and_pick",
    )(params, send_index, view, shear, offset, center)


def halo_kernel(planes_ref, low_ref, high_ref, low_send, high_send, send_sem, recv_sem):
    total = lax.axis_size("tile")
    me = lax.axis_index("tile")
    following, previous = lax.rem(me + 1, total), lax.rem(me + total - 1, total)
    barrier = pltpu.get_barrier_semaphore()
    signal_all(barrier, (following, previous))
    low_send[...] = planes_ref[:, 6:16, :]
    high_send[...] = planes_ref[:, 0:10, :]
    pl.semaphore_wait(barrier, 2)
    copies = [
        pltpu.make_async_remote_copy(
            src_ref=source,
            dst_ref=target,
            send_sem=send_sem.at[k],
            recv_sem=recv_sem.at[k],
            device_id={"tile": peer},
            device_id_type=MESH,
        )
        for k, (source, target, peer) in enumerate(
            ((low_send, low_ref, following), (high_send, high_ref, previous))
        )
    ]
    for copy in copies:
        copy.start()
    for copy in copies:
        copy.wait()


def halo_rows(planes):
    vmem = pl.BlockSpec(memory_space=pltpu.VMEM)
    part = (planes.shape[0], 10, planes.shape[2])
    shape = jax.ShapeDtypeStruct(part, jnp.float32)
    return pl.pallas_call(
        halo_kernel,
        out_shape=(shape, shape),
        in_specs=[vmem],
        out_specs=(vmem, vmem),
        scratch_shapes=[
            pltpu.VMEM(part, jnp.float32),
            pltpu.VMEM(part, jnp.float32),
            pltpu.SemaphoreType.DMA((2,)),
            pltpu.SemaphoreType.DMA((2,)),
        ],
        compiler_params=pltpu.CompilerParams(
            collective_id=2, has_side_effects=True, vmem_limit_bytes=VMEM_LIMIT
        ),
        name="halo_rows",
    )(planes)


TILES_STEP = 8
CHUNK = 16
UNROLL = 4


def slot_place(index):
    return (index >> 7) & 31, (index & 127) + ((index >> 12) << 7)


def one_hot(ids, values):
    return (ids == values).astype(jnp.float32).astype(jnp.bfloat16)


def store_parts(rows, high_parts, low_parts, q, columns):
    count = rows.shape[0]
    high, middle, low = split3(rows)
    here = pl.ds(count * q, count)
    width = columns.size
    high_parts[here, columns] = high
    high_parts[here, pl.ds(columns.start + 256, width)] = middle
    if q < 2:
        low_parts[here, columns] = low


def both_parts(value, right, dims):
    sums = mxu(jnp.concatenate(split2(value), axis=0), right, dims)
    return sums[: value.shape[0]] + sums[value.shape[0] :]


def pick_rows(high_parts, low_parts, hot, mask):
    count = mask.shape[0]
    found = mxu(high_parts[...], jnp.concatenate([hot, hot], axis=0), NN)
    found_low = mxu(low_parts[...], hot, NN)
    rows = []
    for q in range(9):
        part = found[count * q : count * q + count]
        if q < 2:
            part = part + found_low[count * q : count * q + count]
        rows.append(jnp.sum(jnp.where(mask, part, 0.0), axis=0, keepdims=True))
    return rows


def tile_deltas(tile, band, u_row, w_row):
    offsets = lax.broadcasted_iota(jnp.int32, (16, 256), 0)
    pixel_x = (offsets + 16 * tile).astype(jnp.float32) + 0.5
    pixel_y = (offsets + 16 * band).astype(jnp.float32) + 0.5
    return pixel_x - u_row, pixel_y - w_row


def forward_kernel(
    slots_ref, list_ref, count_ref, band_ref, view_ref, back_ref,
    image_ref, entry_ref, cover_ref, keep_ref,
    high_parts, low_parts, before, picked, total,
):
    step = pl.program_id(0)
    view = view_ref[0]
    band = band_ref[0]
    lanes = lax.broadcasted_iota(jnp.int32, (1, 256), 1)

    @pl.when(step == 0)
    def _():
        for q in range(9):
            for half in range(2):
                store_parts(
                    slots_ref[32 * half : 32 * half + 32, q, :],
                    high_parts, low_parts, q, pl.ds(128 * half, 128),
                )
        row_ids = lax.broadcasted_iota(jnp.int32, (256, 256), 0)
        column_ids = lax.broadcasted_iota(jnp.int32, (256, 256), 1)
        before[...] = (row_ids < column_ids).astype(jnp.float32).astype(jnp.bfloat16)
        total[...] = jnp.zeros_like(total)
        high_ids = lax.broadcasted_iota(jnp.int32, (32, 256), 0)

        def pick(tile, carry):
            high, low = slot_place(list_ref[pl.ds(tile, 1), :])
            rows = pick_rows(high_parts, low_parts, one_hot(row_ids, low), high_ids == high)
            rows[5] = jnp.where(lanes < count_ref[0, tile], rows[5], 0.0)
            for c in range(3):
                rows[6 + c] = rows[6 + c] - back_ref[view, c]
            for q in range(9):
                picked[tile, q : q + 1, :] = rows[q]
            return carry

        lax.fori_loop(0, 32, pick, 0, unroll=4)

    color_ids = lax.broadcasted_iota(jnp.int32, (128, 256), 0)

    def one(k, carry):
        tile = step * TILES_STEP + k
        rows = [picked[tile, q : q + 1, :] for q in range(9)]
        for q in range(9):
            entry_ref[k, q : q + 1, :] = rows[q]
        delta_x, delta_y = tile_deltas(tile, band, rows[0], rows[1])
        along_x = -0.5 * rows[2] * delta_x * delta_x
        mixed = -rows[3] * delta_x
        along_y = -0.5 * rows[4] * delta_y * delta_y
        colors = jnp.zeros((128, 256), jnp.float32)
        for c in range(3):
            colors = jnp.where(color_ids == 3 * tile + c, rows[6 + c], colors)
        colors = jnp.concatenate(split2(colors), axis=0)
        for first in range(0, 16, CHUNK):
            pieces = []
            for i in range(first, first + CHUNK):
                exponent = along_x + (mixed * delta_y[i : i + 1] + along_y[i : i + 1])
                pieces.append(rows[5] * jnp.exp(exponent))
            cover = jnp.concatenate(pieces, axis=0)
            keep = jnp.exp(both_parts(jnp.log(1.0 - cover), before[...], NN))
            here = slice(16 * first, 16 * (first + CHUNK))
            cover_ref[k, here] = cover
            keep_ref[k, here] = keep
            shown = mxu(jnp.concatenate(split2(cover * keep), axis=0), colors, NT)
            size = 16 * CHUNK
            total[here] += shown[0:size, 0:128] + shown[0:size, 128:256] + shown[size:, 0:128]
        return carry

    lax.fori_loop(0, TILES_STEP, one, 0, unroll=UNROLL)

    @pl.when(step == pl.num_programs(0) - 1)
    def _():
        image_ref[...] = jnp.transpose(total[...])


def render_forward(slots, lists, counts, band, view, back):
    smem = pl.BlockSpec(memory_space=pltpu.SMEM)
    field = jax.ShapeDtypeStruct((32, 256, 256), jnp.float32)
    field_spec = pl.BlockSpec((TILES_STEP, 256, 256), lambda i: (i, 0, 0))
    return pl.pallas_call(
        forward_kernel,
        grid=(32 // TILES_STEP,),
        out_shape=(
            jax.ShapeDtypeStruct((128, 256), jnp.float32),
            jax.ShapeDtypeStruct((32, 9, 256), jnp.float32),
            field,
            field,
        ),
        in_specs=[
            pl.BlockSpec((64, slots.shape[1], 128), lambda i: (0, 0, 0)),
            pl.BlockSpec((32, 256), lambda i: (0, 0)),
            smem,
            smem,
            smem,
            smem,
        ],
        out_specs=(
            pl.BlockSpec((128, 256), lambda i: (0, 0)),
            pl.BlockSpec((TILES_STEP, 9, 256), lambda i: (i, 0, 0)),
            field_spec,
            field_spec,
        ),
        scratch_shapes=[
            pltpu.VMEM((288, 512), jnp.bfloat16),
            pltpu.VMEM((64, 256), jnp.bfloat16),
            pltpu.VMEM((256, 256), jnp.bfloat16),
            pltpu.VMEM((32, 9, 256), jnp.float32),
            pltpu.VMEM((256, 128), jnp.float32),
        ],
        compiler_params=pltpu.CompilerParams(vmem_limit_bytes=VMEM_LIMIT),
        name="render_forward",
    )(slots, lists, counts, band, view, back)


def backward_kernel(
    entry_ref, cover_ref, keep_ref, grad_ref, list_ref, band_ref, loss_ref, out_ref,
    after, total, results, high_weights, low_weights, outgoing, incoming, send_sem, recv_sem, *greetings,
):
    step = pl.program_id(0)
    greet_all(step, greetings)

    @pl.when(step == 0)
    def _():
        row_ids = lax.broadcasted_iota(jnp.int32, (256, 256), 0)
        column_ids = lax.broadcasted_iota(jnp.int32, (256, 256), 1)
        after[...] = (row_ids > column_ids).astype(jnp.float32).astype(jnp.bfloat16)

    band = band_ref[0]

    def fold(value):
        return jnp.sum(value, axis=0, keepdims=True)

    def one(k, carry):
        tile = step * TILES_STEP + k
        rows = [entry_ref[k, q : q + 1, :] for q in range(9)]
        grads = jnp.concatenate([grad_ref[c, pl.ds(tile, 1), :] for c in range(3)], axis=0)
        colors = jnp.concatenate(rows[6:9], axis=0)
        grads_high = grads.astype(jnp.bfloat16).astype(jnp.float32)
        grads_low = grads - grads_high
        colors_high = colors.astype(jnp.bfloat16).astype(jnp.float32)
        colors_low = colors - colors_high
        blank = jnp.zeros((7, 256), jnp.float32)
        left = jnp.concatenate([grads_high, grads_high, grads_low, blank], axis=0).astype(jnp.bfloat16)
        right = jnp.concatenate([colors_high, colors_low, colors_high, blank], axis=0).astype(jnp.bfloat16)
        both = jnp.concatenate([grads_high, grads_low, blank, blank[0:3]], axis=0).astype(jnp.bfloat16)
        delta_x, delta_y = tile_deltas(tile, band, rows[0], rows[1])
        sum_0 = jnp.zeros((16, 256), jnp.float32)
        sum_y = sum_0
        sum_yy = sum_0
        for first in range(0, 16, CHUNK):
            here = slice(16 * first, 16 * (first + CHUNK))
            shade = mxu(left[:, here], right, TN)
            cover = cover_ref[k, here]
            weight = cover * keep_ref[k, here]
            weight_high, weight_low = split2(weight)
            high_weights[k % 2, here] = weight_high
            low_weights[k % 2, here] = weight_low
            lit = weight * shade
            behind = both_parts(lit, after[...], NN)
            pull = lit - behind * (cover / (1.0 - cover))
            for i in range(CHUNK):
                piece = pull[16 * i : 16 * i + 16]
                level = delta_y[first + i : first + i + 1]
                piece_y = piece * level
                sum_0 = sum_0 + piece
                sum_y = sum_y + piece_y
                sum_yy = sum_yy + piece_y * level
        color_grad = mxu(both, high_weights[k % 2], NN)
        color_grad = color_grad[0:3] + color_grad[3:6] + mxu(both, low_weights[k % 2], NN)[0:3]
        sum_x = sum_0 * delta_x
        moment_0 = fold(sum_0)
        moment_x = fold(sum_x)
        moment_xx = fold(sum_x * delta_x)
        moment_y = fold(sum_y)
        moment_xy = fold(sum_y * delta_x)
        moment_yy = fold(sum_yy)
        live = rows[5] > 0.0
        values = [
            rows[2] * moment_x + rows[3] * moment_y,
            rows[4] * moment_y + rows[3] * moment_x,
            -0.5 * moment_xx,
            -moment_xy,
            -0.5 * moment_yy,
            jnp.where(live, moment_0 / jnp.where(live, rows[5], 1.0), 0.0),
            color_grad[0:1],
            color_grad[1:2],
            color_grad[2:3],
        ]
        for q in range(9):
            results[tile, q : q + 1, :] = values[q]
        return carry

    lax.fori_loop(0, TILES_STEP, one, 0, unroll=UNROLL)

    @pl.when(step == pl.num_programs(0) - 1)
    def _():
        low_ids = lax.broadcasted_iota(jnp.int32, (256, 256), 0)
        high_ids = lax.broadcasted_iota(jnp.int32, (32, 256), 0)
        total[...] = jnp.zeros_like(total)

        def place(tile, carry):
            high, low = slot_place(list_ref[pl.ds(tile, 1), :])
            place_rows([results[tile, q : q + 1, :] for q in range(9)], total, one_hot(low_ids, low), high_ids == high)
            return carry

        lax.fori_loop(0, 32, place, 0, unroll=4)
        for q in range(9):
            for half in range(2):
                outgoing[32 * half : 32 * half + 32, q, :] = total[
                    32 * q : 32 * q + 32, 128 * half : 128 * half + 128
                ]
        outgoing[:, 9, :] = jnp.broadcast_to(loss_ref[...], (64, 128))
        me = lax.axis_index("tile")

        def send(p, carry):
            block_copy(outgoing, incoming, send_sem, recv_sem, lax.rem(me + p, 64)).start()
            return carry

        lax.fori_loop(1, 64, send, 0)
        finish_blocks(outgoing, incoming, send_sem, recv_sem)
        out_ref[...] = incoming[...]


def place_rows(rows, total, hot, mask):
    count = mask.shape[0]
    high_rows, low_rows = [], []
    for row in rows:
        high = row.astype(jnp.bfloat16).astype(jnp.float32)
        high_rows.append(jnp.where(mask, high, 0.0))
        low_rows.append(jnp.where(mask, row - high, 0.0))
    placed = jnp.concatenate(high_rows + low_rows, axis=0).astype(jnp.bfloat16)
    sums = mxu(placed, hot, NT)
    total[...] += sums[: 9 * count] + sums[9 * count :]


def render_backward(entries, cover, keep, grads, lists, band, loss):
    smem = pl.BlockSpec(memory_space=pltpu.SMEM)
    field_spec = pl.BlockSpec((TILES_STEP, 256, 256), lambda i: (i, 0, 0))
    return pl.pallas_call(
        backward_kernel,
        grid=(32 // TILES_STEP,),
        out_shape=jax.ShapeDtypeStruct((64, 10, 128), jnp.float32),
        in_specs=[
            pl.BlockSpec((TILES_STEP, 9, 256), lambda i: (i, 0, 0)),
            field_spec,
            field_spec,
            pl.BlockSpec((3, 32, 256), lambda i: (0, 0, 0)),
            pl.BlockSpec((32, 256), lambda i: (0, 0)),
            smem,
            pl.BlockSpec((1, 128), lambda i: (0, 0)),
        ],
        out_specs=pl.BlockSpec((64, 10, 128), lambda i: (0, 0, 0)),
        scratch_shapes=[
            pltpu.VMEM((256, 256), jnp.bfloat16),
            pltpu.VMEM((288, 256), jnp.float32),
            pltpu.VMEM((32, 9, 256), jnp.float32),
            pltpu.VMEM((2, 256, 256), jnp.bfloat16),
            pltpu.VMEM((2, 256, 256), jnp.bfloat16),
            *exchange_scratch(10),
        ],
        compiler_params=pltpu.CompilerParams(
            collective_id=1, has_side_effects=True, vmem_limit_bytes=VMEM_LIMIT
        ),
        name="render_backward",
    )(entries, cover, keep, grads, lists, band, loss)
def place_kernel(returned_ref, index_ref, count_ref, out_ref, total):
    total[...] = jnp.zeros_like(total)
    low_ids = lax.broadcasted_iota(jnp.int32, (256, 256), 0)
    high_ids = lax.broadcasted_iota(jnp.int32, (64, 256), 0)
    lanes = lax.broadcasted_iota(jnp.int32, (1, 128), 1)

    def place(pair, carry):
        def joined(values):
            return jnp.concatenate(values, axis=1)

        bands = (pair, pair + 32)
        index = joined([index_ref[pl.ds(d, 1), :] for d in bands])
        live = joined([(lanes < count_ref[0, d]).astype(jnp.int32) for d in bands])
        high = jnp.where(live > 0, (index >> 7) & 63, -1)
        low = (index & 127) + ((index >> 13) << 7)
        rows = [joined([returned_ref[d, q : q + 1, :] for d in bands]) for q in range(9)]
        place_rows(rows, total, one_hot(low_ids, low), high_ids == high)
        return carry

    lax.fori_loop(0, 32, place, 0, unroll=4)
    for q in range(9):
        for half in range(2):
            out_ref[q, 64 * half : 64 * half + 64, :] = total[
                64 * q : 64 * q + 64, 128 * half : 128 * half + 128
            ]
    loss = jnp.sum(returned_ref[:, 9, :], axis=0, keepdims=True)
    out_ref[9] = jnp.broadcast_to(loss, (128, 128))


def place_gradients(returned, send_index, send_count):
    vmem = pl.BlockSpec(memory_space=pltpu.VMEM)
    return pl.pallas_call(
        place_kernel,
        out_shape=jax.ShapeDtypeStruct((10, 128, 128), jnp.float32),
        in_specs=[vmem, vmem, pl.BlockSpec(memory_space=pltpu.SMEM)],
        out_specs=vmem,
        scratch_shapes=[pltpu.VMEM((576, 256), jnp.float32)],
        compiler_params=pltpu.CompilerParams(vmem_limit_bytes=VMEM_LIMIT),
        name="place_gradients",
    )(returned, send_index, send_count)


RATES = [0.016] * 3 + [0.005] * 3 + [0.001] * 4 + [0.05] + [0.0025] * 3 + [0.000125] * 45
LOSS_TERMS = 2 * 3 * 1024 * 512


def update_kernel(
    params_ref, first_ref, second_ref, own_ref, other_ref, view_ref, shear_ref, offset_ref, center_ref,
    params_out, first_out, second_out, loss_out, dense,
):
    refs = (shear_ref, offset_ref, center_ref)
    cameras = [camera_of(refs, 0), camera_of(refs, 1)]
    is_first = view_ref[0] == 0
    loss_out[...] = (own_ref[9, 0:1, 0:1] + other_ref[9, 0:1, 0:1]) / LOSS_TERMS

    def part(sub, carry):
        rows = dense_rows(params_ref, sub)
        _, pull_back = jax.vjp(lambda *values: project_rows(values, cameras), *rows)
        here = pl.ds(pl.multiple_of(8 * sub, 8), 8)
        own = [own_ref[q, here, :] for q in range(9)]
        other = [other_ref[q, here, :] for q in range(9)]
        gradient = pull_back(
            [
                [jnp.where(is_first, a, b) for a, b in zip(own, other)],
                [jnp.where(is_first, b, a) for a, b in zip(own, other)],
            ]
        )
        for r in range(59):
            dense[8 * r : 8 * r + 8, :] = gradient[r]
        for first in range(0, 59, 8):
            size = min(8, 59 - first)
            row_ids = lax.broadcasted_iota(jnp.int32, (size, 128), 0)
            rate = jnp.full((size, 128), RATES[first], jnp.float32)
            for r in range(1, size):
                if RATES[first + r] != RATES[first + r - 1]:
                    rate = jnp.where(row_ids >= r, RATES[first + r], rate)
            rate = rate / (1.0 - 0.9**STEP_COUNT)
            for c in range(8):
                columns = pl.ds(pl.multiple_of(1024 * sub + 128 * c, 128), 128)
                here = (slice(first, first + size), columns)
                grad = dense[pl.ds(8 * first + c, size, stride=8), :]
                new_first = 0.9 * first_ref[here] + 0.1 * grad
                new_second = 0.999 * second_ref[here] + 0.001 * grad * grad
                scale = jnp.sqrt(new_second * (1.0 / (1.0 - 0.999**STEP_COUNT))) + 1e-15
                params_out[here] = params_ref[here] - rate * new_first / scale
                first_out[here] = new_first
                second_out[here] = new_second
        return carry

    lax.fori_loop(0, BLOCK // 1024, part, 0)


def update(params, first_moment, second_moment, own, other, view, shear, offset, center):
    smem = pl.BlockSpec(memory_space=pltpu.SMEM)
    block = pl.BlockSpec((59, BLOCK), lambda i: (0, i))
    grads = pl.BlockSpec((10, BLOCK // 128, 128), lambda i: (0, i, 0))
    shape = jax.ShapeDtypeStruct(params.shape, jnp.float32)
    return pl.pallas_call(
        update_kernel,
        grid=(16384 // BLOCK,),
        out_shape=(shape, shape, shape, jax.ShapeDtypeStruct((1, 1), jnp.float32)),
        in_specs=[block, block, block, grads, grads, smem, smem, smem, smem],
        out_specs=(block, block, block, pl.BlockSpec((1, 1), lambda i: (0, 0))),
        scratch_shapes=[pltpu.VMEM((59 * 8, 128), jnp.float32)],
        compiler_params=pltpu.CompilerParams(vmem_limit_bytes=VMEM_LIMIT),
        name="update",
    )(params, first_moment, second_moment, own, other, view, shear, offset, center)


def gaussian_blur(planes):
    taps = window_taps()
    rows_out = planes.shape[1] - 10
    vertical = taps[0] * planes[:, 0:rows_out]
    for position in range(1, 11):
        vertical = vertical + taps[position] * planes[:, position : position + rows_out]
    image_width = planes.shape[2]
    padded = jnp.pad(vertical, ((0, 0), (0, 0), (5, 5)))
    result = taps[0] * padded[:, :, 0:image_width]
    for position in range(1, 11):
        result = result + taps[position] * padded[:, :, position : position + image_width]
    return result


def ssim_map(level_x, level_y, energy_x, energy_y, product_xy):
    upper = (2.0 * level_x * level_y + 0.0001) * (2.0 * (product_xy - level_x * level_y) + 0.0009)
    lower = (level_x * level_x + level_y * level_y + 0.0001) * (
        energy_x - level_x * level_x + (energy_y - level_y * level_y) + 0.0009
    )
    return upper / lower


def window_stats(widened):
    shown = widened[0:3]
    truth = widened[3:6]
    mean_x = gaussian_blur(shown)
    mean_y = gaussian_blur(truth)
    power_x = gaussian_blur(shown * shown)
    power_y = gaussian_blur(truth * truth)
    cross_xy = gaussian_blur(shown * truth)
    return (mean_x, mean_y, power_x, power_y, cross_xy)


def shards(
    params,
    first_moment,
    second_moment,
    target,
    view_shear,
    view_offset,
    cam_center,
    background,
    send_index,
    send_count,
    tile_list,
    tile_count,
):
    view_index = lax.axis_index("view")
    band_index = lax.axis_index("tile")

    view = view_index.astype(jnp.int32).reshape(1)
    band = band_index.astype(jnp.int32).reshape(1)
    backdrop = lax.dynamic_index_in_dim(background, view_index, 0, keepdims=False)
    incoming = project_and_pick(params, send_index[0], view, view_shear, view_offset, cam_center)
    shown, entries, cover, keep = render_forward(
        incoming, tile_list[0, 0], tile_count, band, view, background
    )
    image_band = shown[:96].reshape(32, 3, 16, 16).transpose(1, 2, 0, 3).reshape(3, 16, 512)
    image_band = image_band + backdrop[:, None, None]
    frame_band = target[0]
    stacked = jnp.concatenate([image_band, frame_band], axis=0)
    low, high = halo_rows(stacked)
    last_band = lax.axis_size("tile") - 1
    low = jnp.where(band_index > 0, low, 0.0)
    high = jnp.where(band_index < last_band, high, 0.0)
    widened = jnp.concatenate([low, stacked, high], axis=1)
    mean_x, mean_y, power_x, power_y, cross_xy = window_stats(widened)
    similarity, ssim_back = jax.vjp(
        lambda level_x, energy_x, product_xy: ssim_map(
            level_x, mean_y, energy_x, power_y, product_xy
        ),
        mean_x,
        power_x,
        cross_xy,
    )
    rows = jnp.arange(26, dtype=jnp.int32) - 5 + 16 * band_index
    inside = (rows >= 0) & (rows < 16 * (last_band + 1))
    seed = jnp.where(inside, -0.8, 0.0)[None, :, None]
    spread = jnp.concatenate(ssim_back(jnp.broadcast_to(seed, similarity.shape)), axis=0)
    similarity = similarity[:, 5:21]
    blurred = gaussian_blur(spread)
    difference = image_band - frame_band
    smooth = jnp.sqrt(difference * difference + 0.0001)
    loss_part = jnp.sum(0.2 * smooth + 0.8 * (1.0 - similarity))
    pixel_grad = (
        0.2 * difference / smooth
        + blurred[0:3]
        + 2.0 * image_band * blurred[3:6]
        + frame_band * blurred[6:9]
    )
    grad_tiles = pixel_grad.reshape(3, 16, 32, 16).transpose(0, 2, 1, 3).reshape(3, 32, 256)
    loss_row = jnp.broadcast_to(loss_part, (1, 128))
    returned = render_backward(entries, cover, keep, grad_tiles, tile_list[0, 0], band, loss_row)
    own_grad = place_gradients(returned, send_index[0], send_count)
    other_grad = lax.ppermute(own_grad, "view", [(0, 1), (1, 0)])
    new_params, new_first, new_second, mean_loss = update(
        params, first_moment, second_moment, own_grad, other_grad, view, view_shear, view_offset, cam_center
    )
    return (new_params, new_first, new_second, mean_loss[0, 0])


def solution(mesh):
    placed = (
        P(None, "tile"),
        P(None, "tile"),
        P(None, "tile"),
        P("view", None, "tile", None),
        P(),
        P(),
        P(),
        P(),
        P("tile", None, None),
        P("tile", None),
        P("view", "tile", None, None),
        P("tile", None),
    )
    return jax.shard_map(
        shards,
        mesh=mesh,
        in_specs=placed,
        out_specs=(P(None, "tile"), P(None, "tile"), P(None, "tile"), P()),
        check_vma=False,
    )
```

```python
import functools
import math

import jax
import jax.numpy as jnp
from jax import lax
from jax.experimental import pallas as pl
from jax.experimental.pallas import tpu as pltpu
from jax.sharding import PartitionSpec as P

STEP_COUNT = 20
LIST = 256


def window_taps():
    raw_taps = [math.exp(-(position - 5) * (position - 5) / 4.5) for position in range(11)]
    return [element / sum(raw_taps) for element in raw_taps]


def harmonics(unit_x, unit_y, unit_z):
    square_x = unit_x * unit_x
    square_y = unit_y * unit_y
    square_z = unit_z * unit_z
    return [
        0.28209479177387814 * jnp.ones_like(unit_x),
        -0.4886025119029199 * unit_y,
        0.4886025119029199 * unit_z,
        -0.4886025119029199 * unit_x,
        1.0925484305920792 * unit_x * unit_y,
        -1.0925484305920792 * unit_y * unit_z,
        0.31539156525252005 * (2.0 * square_z - square_x - square_y),
        -1.0925484305920792 * unit_x * unit_z,
        0.5462742152960396 * (square_x - square_y),
        -0.5900435899266435 * unit_y * (3.0 * square_x - square_y),
        2.890611442640554 * unit_x * unit_y * unit_z,
        -0.4570457994644658 * unit_y * (4.0 * square_z - square_x - square_y),
        0.3731763325901154 * unit_z * (2.0 * square_z - 3.0 * square_x - 3.0 * square_y),
        -0.4570457994644658 * unit_x * (4.0 * square_z - square_x - square_y),
        1.445305721320277 * unit_z * (square_x - square_y),
        -0.5900435899266435 * unit_x * (square_x - 3.0 * square_y),
    ]


def ssim_map(level_x, level_y, energy_x, energy_y, product_xy):
    upper = (2.0 * level_x * level_y + 0.0001) * (2.0 * (product_xy - level_x * level_y) + 0.0009)
    lower = (level_x * level_x + level_y * level_y + 0.0001) * (
        energy_x - level_x * level_x + (energy_y - level_y * level_y) + 0.0009
    )
    return upper / lower


MESH = pl.DeviceIdType.MESH
VMEM_LIMIT = 56 * 1024 * 1024
NN = (((1,), (0,)), ((), ()))
NT = (((1,), (1,)), ((), ()))
TN = (((0,), (0,)), ((), ()))


def mxu(left, right, dims):
    return lax.dot_general(left, right, dims, preferred_element_type=jnp.float32)


def split2(value):
    high = value.astype(jnp.bfloat16)
    low = (value - high.astype(jnp.float32)).astype(jnp.bfloat16)
    return high, low


def split3(value):
    high = value.astype(jnp.bfloat16)
    rest = value - high.astype(jnp.float32)
    middle = rest.astype(jnp.bfloat16)
    low = (rest - middle.astype(jnp.float32)).astype(jnp.bfloat16)
    return high, middle, low


def project_rows(rows, cameras):
    pos_x, pos_y, pos_z = rows[0:3]
    scales = [jnp.exp(row) for row in rows[3:6]]
    quat_w, quat_x, quat_y, quat_z = rows[6:10]
    norm = 1.0 / jnp.sqrt(
        quat_w * quat_w + quat_x * quat_x + quat_y * quat_y + quat_z * quat_z
    )
    quat_w, quat_x, quat_y, quat_z = quat_w * norm, quat_x * norm, quat_y * norm, quat_z * norm
    rotation = [
        [
            1.0 - 2.0 * (quat_y * quat_y + quat_z * quat_z),
            2.0 * (quat_x * quat_y - quat_w * quat_z),
            2.0 * (quat_x * quat_z + quat_w * quat_y),
        ],
        [
            2.0 * (quat_x * quat_y + quat_w * quat_z),
            1.0 - 2.0 * (quat_x * quat_x + quat_z * quat_z),
            2.0 * (quat_y * quat_z - quat_w * quat_x),
        ],
        [
            2.0 * (quat_x * quat_z - quat_w * quat_y),
            2.0 * (quat_y * quat_z + quat_w * quat_x),
            1.0 - 2.0 * (quat_x * quat_x + quat_y * quat_y),
        ],
    ]
    opacity = 1.0 / (1.0 + jnp.exp(-rows[10]))
    records = []
    for shear_x, shear_y, offset_x, offset_y, center_x, center_y, center_z in cameras:
        first = [(rotation[0][k] + shear_x * rotation[2][k]) * scales[k] for k in range(3)]
        second = [(rotation[1][k] + shear_y * rotation[2][k]) * scales[k] for k in range(3)]
        cov_xx = first[0] * first[0] + first[1] * first[1] + first[2] * first[2] + 0.3
        cov_yy = second[0] * second[0] + second[1] * second[1] + second[2] * second[2] + 0.3
        cov_xy = first[0] * second[0] + first[1] * second[1] + first[2] * second[2]
        inverse = 1.0 / (cov_xx * cov_yy - cov_xy * cov_xy)
        toward_x = pos_x - center_x
        toward_y = pos_y - center_y
        toward_z = pos_z - center_z
        shrink = 1.0 / jnp.sqrt(toward_x * toward_x + toward_y * toward_y + toward_z * toward_z)
        basis = harmonics(toward_x * shrink, toward_y * shrink, toward_z * shrink)
        colors = []
        for c in range(3):
            total = basis[0] * rows[11 + c]
            for k in range(1, 16):
                total = total + basis[k] * rows[11 + 3 * k + c]
            colors.append(0.5 + total)
        records.append(
            [
                pos_x + shear_x * pos_z + offset_x,
                pos_y + shear_y * pos_z + offset_y,
                cov_yy * inverse,
                -cov_xy * inverse,
                cov_xx * inverse,
                opacity,
                *colors,
            ]
        )
    return records


def camera_of(refs, view):
    shear_ref, offset_ref, center_ref = refs
    return (
        shear_ref[view, 0],
        shear_ref[view, 1],
        offset_ref[view, 0],
        offset_ref[view, 1],
        center_ref[view, 0],
        center_ref[view, 1],
        center_ref[view, 2],
    )


BLOCK = 4096


def dense_rows(source_ref, sub):
    count = source_ref.shape[0]
    columns = pl.ds(pl.multiple_of(1024 * sub, 1024), 1024)
    rows = []
    for first in range(0, count, 8):
        size = min(8, count - first)
        block = source_ref[first : first + size, columns].reshape(size, 8, 128)
        rows += [block[r] for r in range(size)]
    return rows


def axis_peers(me, stride):
    place = lax.rem(me // stride, 4)
    return [me + (lax.rem(place + j, 4) - place) * stride for j in range(1, 4)]


def signal_all(semaphore, peers):
    for peer in peers:
        pl.semaphore_signal(semaphore, inc=1, device_id={"tile": peer}, device_id_type=MESH)


def greet_all(step, semaphores):
    plane_sem, cube_sem = semaphores
    me = lax.axis_index("tile")
    lines = [axis_peers(me, stride) for stride in (1, 4, 16)]
    barrier = pltpu.get_barrier_semaphore()

    @pl.when(step == 0)
    def _():
        for line in lines:
            signal_all(barrier, line)

    @pl.when(step == 1)
    def _():
        pl.semaphore_wait(barrier, 9)
        signal_all(plane_sem, lines[1])

    @pl.when(step == 2)
    def _():
        pl.semaphore_wait(plane_sem, 3)
        signal_all(cube_sem, lines[2])

    @pl.when(step == 3)
    def _():
        pl.semaphore_wait(cube_sem, 3)


def block_copy(outgoing, incoming, send_sem, recv_sem, peer):
    me = lax.axis_index("tile")
    return pltpu.make_async_remote_copy(
        src_ref=outgoing.at[peer],
        dst_ref=incoming.at[me],
        send_sem=send_sem.at[peer],
        recv_sem=recv_sem.at[me],
        device_id={"tile": peer},
        device_id_type=MESH,
    )


def send_block(outgoing, incoming, send_sem, recv_sem, peer):
    @pl.when(peer != lax.axis_index("tile"))
    def _():
        block_copy(outgoing, incoming, send_sem, recv_sem, peer).start()


def finish_blocks(outgoing, incoming, send_sem, recv_sem):
    me = lax.axis_index("tile")
    incoming[me] = outgoing[me]

    def finish(p, carry):
        peer = lax.rem(me + p, 64)
        block_copy(outgoing, incoming, send_sem, recv_sem, peer).wait_send()
        pltpu.make_async_remote_copy(
            src_ref=outgoing.at[peer],
            dst_ref=incoming.at[peer],
            send_sem=send_sem.at[peer],
            recv_sem=recv_sem.at[peer],
            device_id={"tile": peer},
            device_id_type=MESH,
        ).wait_recv()
        return carry

    lax.fori_loop(1, 64, finish, 0)


def exchange_scratch(rows):
    return [
        pltpu.VMEM((64, rows, 128), jnp.float32),
        pltpu.VMEM((64, rows, 128), jnp.float32),
        pltpu.SemaphoreType.DMA((64,)),
        pltpu.SemaphoreType.DMA((64,)),
        pltpu.SemaphoreType.REGULAR,
        pltpu.SemaphoreType.REGULAR,
    ]


def project_kernel(
    params_ref, index_ref, view_ref, shear_ref, offset_ref, center_ref, out_ref,
    table, high_parts, low_parts, outgoing, incoming, send_sem, recv_sem, *greetings,
):
    step = pl.program_id(0)
    greet_all(step, greetings)
    camera = camera_of((shear_ref, offset_ref, center_ref), view_ref[0])

    def part(sub, carry):
        record = project_rows(dense_rows(params_ref, sub), [camera])[0]
        first = pl.multiple_of(step * (BLOCK // 128) + 8 * sub, 8)
        for q in range(9):
            table[q, pl.ds(first, 8), :] = record[q]
        return carry

    lax.fori_loop(0, BLOCK // 1024, part, 0, unroll=2)

    @pl.when(step == pl.num_programs(0) - 1)
    def _():
        for q in range(9):
            for half in range(2):
                store_parts(
                    table[q, 64 * half : 64 * half + 64, :],
                    high_parts, low_parts, q, pl.ds(128 * half, 128),
                )
        low_ids = lax.broadcasted_iota(jnp.int32, (256, 256), 0)
        high_ids = lax.broadcasted_iota(jnp.int32, (64, 256), 0)

        def pick(pair, carry):
            index = jnp.concatenate(
                [index_ref[pl.ds(pair, 1), :], index_ref[pl.ds(pair + 32, 1), :]], axis=1
            )
            high = (index >> 7) & 63
            low = (index & 127) + ((index >> 13) << 7)
            rows = pick_rows(high_parts, low_parts, one_hot(low_ids, low), high_ids == high)
            for q in range(9):
                outgoing[pair, q : q + 1, :] = rows[q][:, 0:128]
                outgoing[pair + 32, q : q + 1, :] = rows[q][:, 128:256]
            return carry

        me = lax.axis_index("tile")

        def group(part, carry):
            first = lax.rem(part + me, 4) * 8
            lax.fori_loop(0, 8, lambda k, carry: pick(first + k, carry), 0, unroll=4)

            def send(k, carry):
                for peer in (first + k, first + k + 32):
                    send_block(outgoing, incoming, send_sem, recv_sem, peer)
                return carry

            lax.fori_loop(0, 8, send, 0)
            return carry

        lax.fori_loop(0, 4, group, 0)
        finish_blocks(outgoing, incoming, send_sem, recv_sem)
        out_ref[...] = incoming[...]


def project_and_pick(params, send_index, view, shear, offset, center):
    smem = pl.BlockSpec(memory_space=pltpu.SMEM)
    return pl.pallas_call(
        project_kernel,
        grid=(16384 // BLOCK,),
        out_shape=jax.ShapeDtypeStruct((64, 9, 128), jnp.float32),
        in_specs=[
            pl.BlockSpec((59, BLOCK), lambda i: (0, i)),
            pl.BlockSpec((64, 128), lambda i: (0, 0)),
            smem,
            smem,
            smem,
            smem,
        ],
        out_specs=pl.BlockSpec((64, 9, 128), lambda i: (0, 0, 0)),
        scratch_shapes=[
            pltpu.VMEM((9, 128, 128), jnp.float32),
            pltpu.VMEM((576, 512), jnp.bfloat16),
            pltpu.VMEM((128, 256), jnp.bfloat16),
            *exchange_scratch(9),
        ],
        compiler_params=pltpu.CompilerParams(
            collective_id=0, has_side_effects=True, vmem_limit_bytes=VMEM_LIMIT
        ),
        name="project_and_pick",
    )(params, send_index, view, shear, offset, center)


def slot_place(index):
    return (index >> 7) & 31, (index & 127) + ((index >> 12) << 7)


def one_hot(ids, values):
    return (ids == values).astype(jnp.float32).astype(jnp.bfloat16)


def store_parts(rows, high_parts, low_parts, q, columns):
    count = rows.shape[0]
    high, middle, low = split3(rows)
    here = pl.ds(count * q, count)
    width = columns.size
    high_parts[here, columns] = high
    high_parts[here, pl.ds(columns.start + 256, width)] = middle
    if q < 2:
        low_parts[here, columns] = low


def both_parts(value, right, dims):
    sums = mxu(jnp.concatenate(split2(value), axis=0), right, dims)
    return sums[: value.shape[0]] + sums[value.shape[0] :]


def pick_rows(high_parts, low_parts, hot, mask):
    count = mask.shape[0]
    found = mxu(high_parts[...], jnp.concatenate([hot, hot], axis=0), NN)
    found_low = mxu(low_parts[...], hot, NN)
    rows = []
    for q in range(9):
        part = found[count * q : count * q + count]
        if q < 2:
            part = part + found_low[count * q : count * q + count]
        rows.append(jnp.sum(jnp.where(mask, part, 0.0), axis=0, keepdims=True))
    return rows


def place_rows(rows, total, hot, mask):
    count = mask.shape[0]
    high_rows, low_rows = [], []
    for row in rows:
        high = row.astype(jnp.bfloat16).astype(jnp.float32)
        high_rows.append(jnp.where(mask, high, 0.0))
        low_rows.append(jnp.where(mask, row - high, 0.0))
    placed = jnp.concatenate(high_rows + low_rows, axis=0).astype(jnp.bfloat16)
    sums = mxu(placed, hot, NT)
    total[...] += sums[: 9 * count] + sums[9 * count :]


def tile_deltas(tile, band, u_row, w_row):
    offsets = lax.broadcasted_iota(jnp.int32, (16, 256), 0)
    pixel_x = (offsets + 16 * tile).astype(jnp.float32) + 0.5
    pixel_y = (offsets + 16 * band).astype(jnp.float32) + 0.5
    return pixel_x - u_row, pixel_y - w_row


def forward_tile(tile, band, picked, before, cover_ref, keep_ref, total):
    rows = [picked[tile, q : q + 1, :] for q in range(9)]
    delta_x, delta_y = tile_deltas(tile, band, rows[0], rows[1])
    along_x = -0.5 * rows[2] * delta_x * delta_x
    mixed = -rows[3] * delta_x
    along_y = -0.5 * rows[4] * delta_y * delta_y
    color_ids = lax.broadcasted_iota(jnp.int32, (128, 256), 0)
    colors = jnp.zeros((128, 256), jnp.float32)
    for c in range(3):
        colors = jnp.where(color_ids == 3 * tile + c, rows[6 + c], colors)
    colors = jnp.concatenate(split2(colors), axis=0)
    pieces = []
    for i in range(16):
        exponent = along_x + (mixed * delta_y[i : i + 1] + along_y[i : i + 1])
        pieces.append(rows[5] * jnp.exp(exponent))
    cover = jnp.concatenate(pieces, axis=0)
    keep = jnp.exp(both_parts(jnp.log(1.0 - cover), before[...], NN))
    cover_ref[tile] = cover
    keep_ref[tile] = keep
    shown = mxu(jnp.concatenate(split2(cover * keep), axis=0), colors, NT)
    total[...] += shown[0:256, 0:128] + shown[0:256, 128:256] + shown[256:512, 0:128]


def backward_tile(tile, slot, band, picked, after, cover_ref, keep_ref, grad_ref, results, high_weights, low_weights):
    rows = [picked[tile, q : q + 1, :] for q in range(9)]
    grads = jnp.concatenate([grad_ref[pl.ds(3 * tile + c, 1), :] for c in range(3)], axis=0)
    colors = jnp.concatenate(rows[6:9], axis=0)
    grads_high = grads.astype(jnp.bfloat16).astype(jnp.float32)
    grads_low = grads - grads_high
    colors_high = colors.astype(jnp.bfloat16).astype(jnp.float32)
    colors_low = colors - colors_high
    blank = jnp.zeros((7, 256), jnp.float32)
    left = jnp.concatenate([grads_high, grads_high, grads_low, blank], axis=0).astype(jnp.bfloat16)
    right = jnp.concatenate([colors_high, colors_low, colors_high, blank], axis=0).astype(jnp.bfloat16)
    both = jnp.concatenate([grads_high, grads_low, blank, blank[0:3]], axis=0).astype(jnp.bfloat16)
    delta_x, delta_y = tile_deltas(tile, band, rows[0], rows[1])
    shade = mxu(left, right, TN)
    cover = cover_ref[tile]
    weight = cover * keep_ref[tile]
    weight_high, weight_low = split2(weight)
    high_weights[slot] = weight_high
    low_weights[slot] = weight_low
    lit = weight * shade
    behind = both_parts(lit, after[...], NN)
    pull = lit - behind * (cover / (1.0 - cover))
    sum_0 = jnp.zeros((16, 256), jnp.float32)
    sum_y = sum_0
    sum_yy = sum_0
    for i in range(16):
        piece = pull[16 * i : 16 * i + 16]
        level = delta_y[i : i + 1]
        piece_y = piece * level
        sum_0 = sum_0 + piece
        sum_y = sum_y + piece_y
        sum_yy = sum_yy + piece_y * level
    color_grad = mxu(both, high_weights[slot], NN)
    color_grad = color_grad[0:3] + color_grad[3:6] + mxu(both, low_weights[slot], NN)[0:3]
    sum_x = sum_0 * delta_x

    def fold(value):
        return jnp.sum(value, axis=0, keepdims=True)

    moment_x = fold(sum_x)
    moment_y = fold(sum_y)
    live = rows[5] > 0.0
    values = [
        rows[2] * moment_x + rows[3] * moment_y,
        rows[4] * moment_y + rows[3] * moment_x,
        -0.5 * fold(sum_x * delta_x),
        -fold(sum_y * delta_x),
        -0.5 * fold(sum_yy),
        jnp.where(live, fold(sum_0) / jnp.where(live, rows[5], 1.0), 0.0),
        color_grad[0:1],
        color_grad[1:2],
        color_grad[2:3],
    ]
    for q in range(9):
        results[tile, q : q + 1, :] = values[q]


def blurred_down(planes, count):
    taps = window_taps()
    result = taps[5] * planes[5 : 5 + count]
    for k in range(5):
        result = result + taps[k] * (planes[k : k + count] + planes[10 - k : 10 - k + count])
    return result


def blurred_across(planes, spread):
    taps = window_taps()
    spread[:, 0:8, :] = pltpu.roll(planes[:, 8:16], 3, 2)
    spread[:, 8:24, :] = planes
    spread[:, 24:32, :] = pltpu.roll(planes[:, 0:8], 125, 2)
    result = taps[5] * planes
    for k in range(5):
        result = result + taps[k] * (spread[:, 3 + k : 19 + k, :] + spread[:, 13 - k : 29 - k, :])
    return result


def window_step(band, last_band, image_ref, truth_ref, grad_ref, spread):
    image = image_ref[...].reshape(36, 16, 128)
    truth = truth_ref[...].reshape(36, 16, 128)
    stage = lax.broadcasted_iota(jnp.int32, (36, 16, 128), 0) - 10 + 16 * band
    within = (stage >= 0) & (stage < 16 * (last_band + 1))
    image = jnp.where(within, image, 0.0)
    truth = jnp.where(within, truth, 0.0)
    stats = []
    for k, plane in enumerate((image, truth, image * image, truth * truth, image * truth)):
        stats.append(blurred_across(blurred_down(plane, 26), spread.at[k]))
    mean_x, mean_y, power_x, power_y, cross_xy = stats
    similarity, ssim_back = jax.vjp(
        lambda level_x, energy_x, product_xy: ssim_map(
            level_x, mean_y, energy_x, power_y, product_xy
        ),
        mean_x,
        power_x,
        cross_xy,
    )
    lanes = lax.broadcasted_iota(jnp.int32, (26, 16, 128), 2)
    counted = within[5:31] & (lanes < 96)
    pulled = []
    for k, plane in enumerate(ssim_back(jnp.where(counted, -0.8, 0.0))):
        pulled.append(blurred_across(blurred_down(plane, 16), spread.at[k, 0:16]))
    shown = image[10:26]
    wanted = truth[10:26]
    difference = shown - wanted
    smooth = jnp.sqrt(difference * difference + 0.0001)
    loss = jnp.where(lanes[0:16] < 96, 0.2 * smooth + 0.8 * (1.0 - similarity[5:21]), 0.0)
    pixel_grad = 0.2 * difference / smooth + pulled[0] + 2.0 * shown * pulled[1] + wanted * pulled[2]
    grad_ref[...] = jnp.transpose(pixel_grad.reshape(256, 128))
    return jnp.sum(jnp.sum(loss, axis=0), axis=0, keepdims=True)


def render_kernel(
    slots_ref, list_ref, count_ref, view_ref, back_ref, target_ref, index_ref, sent_ref,
    own_ref, other_ref,
    high_parts, low_parts, before, after, picked, cover_ref, keep_ref, results, total, slot_total, owner_total,
    target_rows, image_ref, truth_ref, grad_ref, spread, high_weights, low_weights,
    outgoing, incoming, send_sem, recv_sem, plane_sem, cube_sem, halo_send, halo_recv, swap_send, swap_recv,
):
    me = lax.axis_index("tile")
    pair = 1 - lax.axis_index("view")
    band = me
    last_band = lax.axis_size("tile") - 1
    view = view_ref[0]
    barrier = pltpu.get_barrier_semaphore()
    lines = [axis_peers(me, stride) for stride in (1, 4, 16)]
    for line in lines:
        signal_all(barrier, line)
    pl.semaphore_signal(barrier, inc=1, device_id={"view": pair}, device_id_type=MESH)

    for q in range(9):
        for half in range(2):
            store_parts(
                slots_ref[32 * half : 32 * half + 32, q, :], high_parts, low_parts, q, pl.ds(128 * half, 128)
            )
    row_ids = lax.broadcasted_iota(jnp.int32, (256, 256), 0)
    column_ids = lax.broadcasted_iota(jnp.int32, (256, 256), 1)
    before[...] = (row_ids < column_ids).astype(jnp.float32).astype(jnp.bfloat16)
    after[...] = (row_ids > column_ids).astype(jnp.float32).astype(jnp.bfloat16)
    own_pixels = slice(160, 416)
    target_rows[0:96, :] = target_ref[...]
    target_rows[96:128, :] = jnp.zeros((32, 256), jnp.float32)
    truth_ref[own_pixels, :] = jnp.transpose(target_rows[...])
    lanes = lax.broadcasted_iota(jnp.int32, (1, 256), 1)
    high_ids = lax.broadcasted_iota(jnp.int32, (32, 256), 0)

    def pick(tile, carry):
        high, low = slot_place(list_ref[pl.ds(tile, 1), :])
        low_ids = lax.broadcasted_iota(jnp.int32, (256, 256), 0)
        rows = pick_rows(high_parts, low_parts, one_hot(low_ids, low), high_ids == high)
        rows[5] = jnp.where(lanes < count_ref[0, tile], rows[5], 0.0)
        for c in range(3):
            rows[6 + c] = rows[6 + c] - back_ref[view, c]
        for q in range(9):
            picked[tile, q : q + 1, :] = rows[q]
        return carry

    lax.fori_loop(0, 32, pick, 0, unroll=4)
    pl.semaphore_wait(barrier, 10)
    signal_all(plane_sem, lines[1])
    total[...] = jnp.zeros_like(total)

    def forward(tile, carry):
        forward_tile(tile, band, picked, before, cover_ref, keep_ref, total)
        return carry

    lax.fori_loop(0, 12, forward, 0, unroll=4)
    pl.semaphore_wait(plane_sem, 3)
    signal_all(cube_sem, lines[2])
    lax.fori_loop(12, 24, forward, 0, unroll=4)
    pl.semaphore_wait(cube_sem, 3)

    following, previous = lax.rem(me + 1, 64), lax.rem(me + 63, 64)

    def halo(field, k, peer, source, target):
        return pltpu.make_async_remote_copy(
            src_ref=field.at[pl.ds(source, 160), :],
            dst_ref=field.at[pl.ds(target, 160), :],
            send_sem=halo_send.at[k],
            recv_sem=halo_recv.at[k],
            device_id={"tile": peer},
            device_id_type=MESH,
        )

    copies = [halo(truth_ref, 0, following, 256, 0), halo(truth_ref, 1, previous, 160, 416)]
    for copy in copies:
        copy.start()
    lax.fori_loop(24, 32, forward, 0, unroll=4)
    color_lanes = lax.broadcasted_iota(jnp.int32, (1, 128), 1)
    backdrop = jnp.zeros((1, 128), jnp.float32)
    for c in range(3):
        here = (lax.rem(color_lanes, 3) == c) & (color_lanes < 96)
        backdrop = jnp.where(here, back_ref[view, c], backdrop)
    image_ref[own_pixels, :] = total[...] + backdrop
    shown = [halo(image_ref, 2, following, 256, 0), halo(image_ref, 3, previous, 160, 416)]
    for copy in shown:
        copy.start()
    for copy in copies + shown:
        copy.wait()
    loss = window_step(band, last_band, image_ref, truth_ref, grad_ref, spread)

    def backward(group, carry):
        for slot in range(4):
            backward_tile(
                4 * group + slot, slot, band, picked, after, cover_ref, keep_ref, grad_ref, results,
                high_weights, low_weights,
            )
        return carry

    lax.fori_loop(0, 8, backward, 0)
    slot_total[...] = jnp.zeros_like(slot_total)

    def place_slots(tile, carry):
        high, low = slot_place(list_ref[pl.ds(tile, 1), :])
        low_ids = lax.broadcasted_iota(jnp.int32, (256, 256), 0)
        rows = [results[tile, q : q + 1, :] for q in range(9)]
        place_rows(rows, slot_total, one_hot(low_ids, low), high_ids == high)
        return carry

    lax.fori_loop(0, 32, place_slots, 0, unroll=4)
    for q in range(9):
        for half in range(2):
            outgoing[32 * half : 32 * half + 32, q, :] = slot_total[
                32 * q : 32 * q + 32, 128 * half : 128 * half + 128
            ]
    outgoing[:, 9, :] = jnp.broadcast_to(loss, (64, 128))

    def send(p, carry):
        block_copy(outgoing, incoming, send_sem, recv_sem, lax.rem(me + p, 64)).start()
        return carry

    lax.fori_loop(1, 64, send, 0)
    owner_total[...] = jnp.zeros_like(owner_total)
    owner_ids = lax.broadcasted_iota(jnp.int32, (64, 256), 0)
    finish_blocks(outgoing, incoming, send_sem, recv_sem)

    def place_owned(first, carry):
        def joined(values):
            return jnp.concatenate(values, axis=1)

        bands = (first, first + 32)
        index = joined([index_ref[pl.ds(d, 1), :] for d in bands])
        live = joined([(color_lanes < sent_ref[0, d]).astype(jnp.int32) for d in bands])
        high = jnp.where(live > 0, (index >> 7) & 63, -1)
        low = (index & 127) + ((index >> 13) << 7)
        low_ids = lax.broadcasted_iota(jnp.int32, (256, 256), 0)
        rows = [joined([incoming[d, q : q + 1, :] for d in bands]) for q in range(9)]
        place_rows(rows, owner_total, one_hot(low_ids, low), owner_ids == high)
        return carry

    lax.fori_loop(0, 32, place_owned, 0, unroll=4)
    for q in range(9):
        for half in range(2):
            own_ref[q, 64 * half : 64 * half + 64, :] = owner_total[
                64 * q : 64 * q + 64, 128 * half : 128 * half + 128
            ]
    losses = jnp.sum(incoming[:, 9, :], axis=0, keepdims=True)
    own_ref[9] = jnp.broadcast_to(losses, (128, 128))
    swap = pltpu.make_async_remote_copy(
        src_ref=own_ref,
        dst_ref=other_ref,
        send_sem=swap_send,
        recv_sem=swap_recv,
        device_id={"view": pair},
        device_id_type=MESH,
    )
    swap.start()
    swap.wait()


def render_step(slots, lists, counts, view, back, target_tiles, send_index, send_count):
    smem = pl.BlockSpec(memory_space=pltpu.SMEM)
    vmem = pl.BlockSpec(memory_space=pltpu.VMEM)
    shape = jax.ShapeDtypeStruct((10, 128, 128), jnp.float32)
    f32, bf16 = jnp.float32, jnp.bfloat16
    return pl.pallas_call(
        render_kernel,
        out_shape=(shape, shape),
        in_specs=[vmem, vmem, smem, smem, smem, vmem, vmem, smem],
        out_specs=(vmem, vmem),
        scratch_shapes=[
            pltpu.VMEM((288, 512), bf16),
            pltpu.VMEM((64, 256), bf16),
            pltpu.VMEM((256, 256), bf16),
            pltpu.VMEM((256, 256), bf16),
            pltpu.VMEM((32, 9, 256), f32),
            pltpu.VMEM((32, 256, 256), f32),
            pltpu.VMEM((32, 256, 256), f32),
            pltpu.VMEM((32, 9, 256), f32),
            pltpu.VMEM((256, 128), f32),
            pltpu.VMEM((288, 256), f32),
            pltpu.VMEM((576, 256), f32),
            pltpu.VMEM((128, 256), f32),
            pltpu.VMEM((576, 128), f32),
            pltpu.VMEM((576, 128), f32),
            pltpu.VMEM((128, 256), f32),
            pltpu.VMEM((5, 26, 32, 128), f32),
            pltpu.VMEM((4, 256, 256), bf16),
            pltpu.VMEM((4, 256, 256), bf16),
            *exchange_scratch(10),
            pltpu.SemaphoreType.DMA((4,)),
            pltpu.SemaphoreType.DMA((4,)),
            pltpu.SemaphoreType.DMA,
            pltpu.SemaphoreType.DMA,
        ],
        compiler_params=pltpu.CompilerParams(
            collective_id=1, has_side_effects=True, vmem_limit_bytes=VMEM_LIMIT
        ),
        name="render_step",
    )(slots, lists, counts, view, back, target_tiles, send_index, send_count)


RATES = [0.016] * 3 + [0.005] * 3 + [0.001] * 4 + [0.05] + [0.0025] * 3 + [0.000125] * 45
LOSS_TERMS = 2 * 3 * 1024 * 512


def update_kernel(
    params_ref, first_ref, second_ref, own_ref, other_ref, view_ref, shear_ref, offset_ref, center_ref,
    params_out, first_out, second_out, loss_out, dense,
):
    refs = (shear_ref, offset_ref, center_ref)
    cameras = [camera_of(refs, 0), camera_of(refs, 1)]
    is_first = view_ref[0] == 0
    losses = own_ref[9, 0:1, :] + other_ref[9, 0:1, :]
    loss_out[...] = jnp.sum(losses, axis=1, keepdims=True) / LOSS_TERMS

    def part(sub, carry):
        rows = dense_rows(params_ref, sub)
        _, pull_back = jax.vjp(lambda *values: project_rows(values, cameras), *rows)
        here = pl.ds(pl.multiple_of(8 * sub, 8), 8)
        own = [own_ref[q, here, :] for q in range(9)]
        other = [other_ref[q, here, :] for q in range(9)]
        gradient = pull_back(
            [
                [jnp.where(is_first, a, b) for a, b in zip(own, other)],
                [jnp.where(is_first, b, a) for a, b in zip(own, other)],
            ]
        )
        for r in range(59):
            dense[8 * r : 8 * r + 8, :] = gradient[r]
        for first in range(0, 59, 8):
            size = min(8, 59 - first)
            row_ids = lax.broadcasted_iota(jnp.int32, (size, 128), 0)
            rate = jnp.full((size, 128), RATES[first], jnp.float32)
            for r in range(1, size):
                if RATES[first + r] != RATES[first + r - 1]:
                    rate = jnp.where(row_ids >= r, RATES[first + r], rate)
            rate = rate / (1.0 - 0.9**STEP_COUNT)
            for c in range(8):
                columns = pl.ds(pl.multiple_of(1024 * sub + 128 * c, 128), 128)
                here = (slice(first, first + size), columns)
                grad = dense[pl.ds(8 * first + c, size, stride=8), :]
                new_first = 0.9 * first_ref[here] + 0.1 * grad
                new_second = 0.999 * second_ref[here] + 0.001 * grad * grad
                scale = jnp.sqrt(new_second * (1.0 / (1.0 - 0.999**STEP_COUNT))) + 1e-15
                params_out[here] = params_ref[here] - rate * new_first / scale
                first_out[here] = new_first
                second_out[here] = new_second
        return carry

    lax.fori_loop(0, BLOCK // 1024, part, 0)


def update(params, first_moment, second_moment, own, other, view, shear, offset, center):
    smem = pl.BlockSpec(memory_space=pltpu.SMEM)
    block = pl.BlockSpec((59, BLOCK), lambda i: (0, i))
    grads = pl.BlockSpec((10, BLOCK // 128, 128), lambda i: (0, i, 0))
    shape = jax.ShapeDtypeStruct(params.shape, jnp.float32)
    return pl.pallas_call(
        update_kernel,
        grid=(16384 // BLOCK,),
        out_shape=(shape, shape, shape, jax.ShapeDtypeStruct((1, 1), jnp.float32)),
        in_specs=[block, block, block, grads, grads, smem, smem, smem, smem],
        out_specs=(block, block, block, pl.BlockSpec((1, 1), lambda i: (0, 0))),
        scratch_shapes=[pltpu.VMEM((59 * 8, 128), jnp.float32)],
        compiler_params=pltpu.CompilerParams(vmem_limit_bytes=VMEM_LIMIT),
        name="update",
    )(params, first_moment, second_moment, own, other, view, shear, offset, center)


def shards(
    params,
    first_moment,
    second_moment,
    target,
    view_shear,
    view_offset,
    cam_center,
    background,
    send_index,
    send_count,
    tile_list,
    tile_count,
):
    view_index = lax.axis_index("view")
    view = view_index.astype(jnp.int32).reshape(1)
    incoming = project_and_pick(params, send_index[0], view, view_shear, view_offset, cam_center)
    target_tiles = target[0].reshape(3, 16, 32, 16).transpose(2, 0, 1, 3).reshape(96, 256)
    own_grad, other_grad = render_step(
        incoming, tile_list[0, 0], tile_count, view, background, target_tiles, send_index[0], send_count
    )
    new_params, new_first, new_second, mean_loss = update(
        params, first_moment, second_moment, own_grad, other_grad, view, view_shear, view_offset, cam_center
    )
    return (new_params, new_first, new_second, mean_loss[0, 0])


def solution(mesh):
    placed = (
        P(None, "tile"),
        P(None, "tile"),
        P(None, "tile"),
        P("view", None, "tile", None),
        P(),
        P(),
        P(),
        P(),
        P("tile", None, None),
        P("tile", None),
        P("view", "tile", None, None),
        P("tile", None),
    )
    return jax.shard_map(
        shards,
        mesh=mesh,
        in_specs=placed,
        out_specs=(P(None, "tile"), P(None, "tile"), P(None, "tile"), P()),
        check_vma=False,
    )
```

```python
import functools
import math

import jax
import jax.numpy as jnp
from jax import lax
from jax.experimental import pallas as pl
from jax.experimental.pallas import tpu as pltpu
from jax.sharding import PartitionSpec as P

STEP_COUNT = 20
LIST = 256


def window_taps():
    raw_taps = [math.exp(-(position - 5) * (position - 5) / 4.5) for position in range(11)]
    return [element / sum(raw_taps) for element in raw_taps]


def harmonics(unit_x, unit_y, unit_z):
    square_x = unit_x * unit_x
    square_y = unit_y * unit_y
    square_z = unit_z * unit_z
    return [
        0.28209479177387814 * jnp.ones_like(unit_x),
        -0.4886025119029199 * unit_y,
        0.4886025119029199 * unit_z,
        -0.4886025119029199 * unit_x,
        1.0925484305920792 * unit_x * unit_y,
        -1.0925484305920792 * unit_y * unit_z,
        0.31539156525252005 * (2.0 * square_z - square_x - square_y),
        -1.0925484305920792 * unit_x * unit_z,
        0.5462742152960396 * (square_x - square_y),
        -0.5900435899266435 * unit_y * (3.0 * square_x - square_y),
        2.890611442640554 * unit_x * unit_y * unit_z,
        -0.4570457994644658 * unit_y * (4.0 * square_z - square_x - square_y),
        0.3731763325901154 * unit_z * (2.0 * square_z - 3.0 * square_x - 3.0 * square_y),
        -0.4570457994644658 * unit_x * (4.0 * square_z - square_x - square_y),
        1.445305721320277 * unit_z * (square_x - square_y),
        -0.5900435899266435 * unit_x * (square_x - 3.0 * square_y),
    ]


def ssim_map(level_x, level_y, energy_x, energy_y, product_xy):
    upper = (2.0 * level_x * level_y + 0.0001) * (2.0 * (product_xy - level_x * level_y) + 0.0009)
    lower = (level_x * level_x + level_y * level_y + 0.0001) * (
        energy_x - level_x * level_x + (energy_y - level_y * level_y) + 0.0009
    )
    return upper / lower


MESH = pl.DeviceIdType.MESH
MIB = 1024 * 1024
NN = (((1,), (0,)), ((), ()))
NT = (((1,), (1,)), ((), ()))
TN = (((0,), (0,)), ((), ()))


def mxu(left, right, dims):
    return lax.dot_general(left, right, dims, preferred_element_type=jnp.float32)


def split2(value):
    high = value.astype(jnp.bfloat16)
    low = (value - high.astype(jnp.float32)).astype(jnp.bfloat16)
    return high, low


def split3(value):
    high = value.astype(jnp.bfloat16)
    rest = value - high.astype(jnp.float32)
    middle = rest.astype(jnp.bfloat16)
    low = (rest - middle.astype(jnp.float32)).astype(jnp.bfloat16)
    return high, middle, low


def project_rows(rows, cameras):
    pos_x, pos_y, pos_z = rows[0:3]
    scales = [jnp.exp(row) for row in rows[3:6]]
    quat_w, quat_x, quat_y, quat_z = rows[6:10]
    norm = 1.0 / jnp.sqrt(
        quat_w * quat_w + quat_x * quat_x + quat_y * quat_y + quat_z * quat_z
    )
    quat_w, quat_x, quat_y, quat_z = quat_w * norm, quat_x * norm, quat_y * norm, quat_z * norm
    rotation = [
        [
            1.0 - 2.0 * (quat_y * quat_y + quat_z * quat_z),
            2.0 * (quat_x * quat_y - quat_w * quat_z),
            2.0 * (quat_x * quat_z + quat_w * quat_y),
        ],
        [
            2.0 * (quat_x * quat_y + quat_w * quat_z),
            1.0 - 2.0 * (quat_x * quat_x + quat_z * quat_z),
            2.0 * (quat_y * quat_z - quat_w * quat_x),
        ],
        [
            2.0 * (quat_x * quat_z - quat_w * quat_y),
            2.0 * (quat_y * quat_z + quat_w * quat_x),
            1.0 - 2.0 * (quat_x * quat_x + quat_y * quat_y),
        ],
    ]
    opacity = 1.0 / (1.0 + jnp.exp(-rows[10]))
    records = []
    for shear_x, shear_y, offset_x, offset_y, center_x, center_y, center_z in cameras:
        first = [(rotation[0][k] + shear_x * rotation[2][k]) * scales[k] for k in range(3)]
        second = [(rotation[1][k] + shear_y * rotation[2][k]) * scales[k] for k in range(3)]
        cov_xx = first[0] * first[0] + first[1] * first[1] + first[2] * first[2] + 0.3
        cov_yy = second[0] * second[0] + second[1] * second[1] + second[2] * second[2] + 0.3
        cov_xy = first[0] * second[0] + first[1] * second[1] + first[2] * second[2]
        inverse = 1.0 / (cov_xx * cov_yy - cov_xy * cov_xy)
        toward_x = pos_x - center_x
        toward_y = pos_y - center_y
        toward_z = pos_z - center_z
        shrink = 1.0 / jnp.sqrt(toward_x * toward_x + toward_y * toward_y + toward_z * toward_z)
        basis = harmonics(toward_x * shrink, toward_y * shrink, toward_z * shrink)
        colors = []
        for c in range(3):
            total = basis[0] * rows[11 + c]
            for k in range(1, 16):
                total = total + basis[k] * rows[11 + 3 * k + c]
            colors.append(0.5 + total)
        records.append(
            [
                pos_x + shear_x * pos_z + offset_x,
                pos_y + shear_y * pos_z + offset_y,
                cov_yy * inverse,
                -cov_xy * inverse,
                cov_xx * inverse,
                opacity,
                *colors,
            ]
        )
    return records


def camera_of(refs, view):
    shear_ref, offset_ref, center_ref = refs
    return (
        shear_ref[view, 0],
        shear_ref[view, 1],
        offset_ref[view, 0],
        offset_ref[view, 1],
        center_ref[view, 0],
        center_ref[view, 1],
        center_ref[view, 2],
    )


BLOCK = 4096


def dense_rows(source_ref, sub):
    count = source_ref.shape[0]
    columns = pl.ds(pl.multiple_of(1024 * sub, 1024), 1024)
    rows = []
    for first in range(0, count, 8):
        size = min(8, count - first)
        block = source_ref[first : first + size, columns].reshape(size, 8, 128)
        rows += [block[r] for r in range(size)]
    return rows


def axis_peers(me, stride):
    place = lax.rem(me // stride, 4)
    return [me + (lax.rem(place + j, 4) - place) * stride for j in range(1, 4)]


def signal_all(semaphore, peers):
    for peer in peers:
        pl.semaphore_signal(semaphore, inc=1, device_id={"tile": peer}, device_id_type=MESH)


def greet_all(step, semaphores):
    plane_sem, cube_sem = semaphores
    me = lax.axis_index("tile")
    lines = [axis_peers(me, stride) for stride in (1, 4, 16)]
    barrier = pltpu.get_barrier_semaphore()

    @pl.when(step == 0)
    def _():
        for line in lines:
            signal_all(barrier, line)

    @pl.when(step == 1)
    def _():
        pl.semaphore_wait(barrier, 9)
        signal_all(plane_sem, lines[1])

    @pl.when(step == 2)
    def _():
        pl.semaphore_wait(plane_sem, 3)
        signal_all(cube_sem, lines[2])

    @pl.when(step == 3)
    def _():
        pl.semaphore_wait(cube_sem, 3)


def block_copy(outgoing, incoming, send_sem, recv_sem, peer):
    me = lax.axis_index("tile")
    return pltpu.make_async_remote_copy(
        src_ref=outgoing.at[peer],
        dst_ref=incoming.at[me],
        send_sem=send_sem,
        recv_sem=recv_sem,
        device_id={"tile": peer},
        device_id_type=MESH,
    )


def send_block(outgoing, incoming, send_sem, recv_sem, peer):
    @pl.when(peer != lax.axis_index("tile"))
    def _():
        block_copy(outgoing, incoming, send_sem, recv_sem, peer).start()


def finish_blocks(outgoing, incoming, send_sem, recv_sem):
    me = lax.axis_index("tile")
    pltpu.make_async_remote_copy(
        src_ref=outgoing.at[0:63],
        dst_ref=incoming.at[0:63],
        send_sem=send_sem,
        recv_sem=recv_sem,
        device_id={"tile": lax.rem(me + 1, 64)},
        device_id_type=MESH,
    ).wait()
    incoming[me] = outgoing[me]


def exchange_scratch(rows):
    return [
        pltpu.VMEM((64, rows, 128), jnp.float32),
        pltpu.VMEM((64, rows, 128), jnp.float32),
        pltpu.SemaphoreType.DMA,
        pltpu.SemaphoreType.DMA,
        pltpu.SemaphoreType.REGULAR,
        pltpu.SemaphoreType.REGULAR,
    ]


def project_kernel(
    params_ref, index_ref, view_ref, shear_ref, offset_ref, center_ref, out_ref,
    table, high_parts, low_parts, outgoing, incoming, send_sem, recv_sem, *greetings,
):
    step = pl.program_id(0)
    greet_all(step, greetings)
    camera = camera_of((shear_ref, offset_ref, center_ref), view_ref[0])

    def part(sub, carry):
        record = project_rows(dense_rows(params_ref, sub), [camera])[0]
        first = pl.multiple_of(step * (BLOCK // 128) + 8 * sub, 8)
        for q in range(9):
            table[q, pl.ds(first, 8), :] = record[q]
        return carry

    lax.fori_loop(0, BLOCK // 1024, part, 0, unroll=2)

    @pl.when(step == pl.num_programs(0) - 1)
    def _():
        for q in range(9):
            for half in range(2):
                store_parts(
                    table[q, 64 * half : 64 * half + 64, :],
                    high_parts, low_parts, q, pl.ds(128 * half, 128),
                )
        low_ids = lax.broadcasted_iota(jnp.int32, (256, 256), 0)
        high_ids = lax.broadcasted_iota(jnp.int32, (64, 256), 0)

        def pick(pair, carry):
            index = jnp.concatenate(
                [index_ref[pl.ds(pair, 1), :], index_ref[pl.ds(pair + 32, 1), :]], axis=1
            )
            high = (index >> 7) & 63
            low = (index & 127) + ((index >> 13) << 7)
            rows = pick_rows(high_parts, low_parts, one_hot(low_ids, low), high_ids == high)
            for q in range(9):
                outgoing[pair, q : q + 1, :] = rows[q][:, 0:128]
                outgoing[pair + 32, q : q + 1, :] = rows[q][:, 128:256]
            return carry

        me = lax.axis_index("tile")

        def group(part, carry):
            first = lax.rem(part + me, 4) * 8
            lax.fori_loop(0, 8, lambda k, carry: pick(first + k, carry), 0, unroll=4)

            def send(k, carry):
                for peer in (first + k, first + k + 32):
                    send_block(outgoing, incoming, send_sem, recv_sem, peer)
                return carry

            lax.fori_loop(0, 8, send, 0)
            return carry

        lax.fori_loop(0, 4, group, 0)
        finish_blocks(outgoing, incoming, send_sem, recv_sem)
        out_ref[...] = incoming[...]


def project_and_pick(params, send_index, view, shear, offset, center):
    smem = pl.BlockSpec(memory_space=pltpu.SMEM)
    return pl.pallas_call(
        project_kernel,
        grid=(16384 // BLOCK,),
        out_shape=jax.ShapeDtypeStruct((64, 9, 128), jnp.float32),
        in_specs=[
            pl.BlockSpec((59, BLOCK), lambda i: (0, i)),
            pl.BlockSpec((64, 128), lambda i: (0, 0)),
            smem,
            smem,
            smem,
            smem,
        ],
        out_specs=pl.BlockSpec((64, 9, 128), lambda i: (0, 0, 0)),
        scratch_shapes=[
            pltpu.VMEM((9, 128, 128), jnp.float32),
            pltpu.VMEM((576, 512), jnp.bfloat16),
            pltpu.VMEM((128, 256), jnp.bfloat16),
            *exchange_scratch(9),
        ],
        compiler_params=pltpu.CompilerParams(
            collective_id=0, has_side_effects=True, vmem_limit_bytes=56 * MIB
        ),
        name="project_and_pick",
    )(params, send_index, view, shear, offset, center)


def slot_place(index):
    return (index >> 7) & 31, (index & 127) + ((index >> 12) << 7)


def one_hot(ids, values):
    return (ids == values).astype(jnp.float32).astype(jnp.bfloat16)


def store_parts(rows, high_parts, low_parts, q, columns):
    count = rows.shape[0]
    high, middle, low = split3(rows)
    here = pl.ds(count * q, count)
    width = columns.size
    high_parts[here, columns] = high
    high_parts[here, pl.ds(columns.start + 256, width)] = middle
    if q < 2:
        low_parts[here, columns] = low


def both_parts(value, right, dims):
    sums = mxu(jnp.concatenate(split2(value), axis=0), right, dims)
    return sums[: value.shape[0]] + sums[value.shape[0] :]


def pick_rows(high_parts, low_parts, hot, mask):
    count = mask.shape[0]
    found = mxu(high_parts[...], jnp.concatenate([hot, hot], axis=0), NN)
    found_low = mxu(low_parts[...], hot, NN)
    rows = []
    for q in range(9):
        part = found[count * q : count * q + count]
        if q < 2:
            part = part + found_low[count * q : count * q + count]
        rows.append(jnp.sum(jnp.where(mask, part, 0.0), axis=0, keepdims=True))
    return rows


def place_rows(rows, total, hot, mask):
    count = mask.shape[0]
    high_rows, low_rows = [], []
    for row in rows:
        high = row.astype(jnp.bfloat16).astype(jnp.float32)
        high_rows.append(jnp.where(mask, high, 0.0))
        low_rows.append(jnp.where(mask, row - high, 0.0))
    placed = jnp.concatenate(high_rows + low_rows, axis=0).astype(jnp.bfloat16)
    sums = mxu(placed, hot, NT)
    total[...] += sums[: 9 * count] + sums[9 * count :]


def tile_deltas(tile, band, u_row, w_row):
    offsets = lax.broadcasted_iota(jnp.int32, (16, 256), 0)
    pixel_x = (offsets + 16 * tile).astype(jnp.float32) + 0.5
    pixel_y = (offsets + 16 * band).astype(jnp.float32) + 0.5
    return pixel_x - u_row, pixel_y - w_row


def forward_tile(tile, band, picked, before, cover_ref, keep_ref, total):
    rows = [picked[tile, q : q + 1, :] for q in range(9)]
    delta_x, delta_y = tile_deltas(tile, band, rows[0], rows[1])
    along_x = -0.5 * rows[2] * delta_x * delta_x
    mixed = -rows[3] * delta_x
    along_y = -0.5 * rows[4] * delta_y * delta_y
    color_ids = lax.broadcasted_iota(jnp.int32, (128, 256), 0)
    colors = jnp.zeros((128, 256), jnp.float32)
    for c in range(3):
        colors = jnp.where(color_ids == 3 * tile + c, rows[6 + c], colors)
    colors = jnp.concatenate(split2(colors), axis=0)
    pieces = []
    for i in range(16):
        exponent = along_x + (mixed * delta_y[i : i + 1] + along_y[i : i + 1])
        pieces.append(rows[5] * jnp.exp(exponent))
    cover = jnp.concatenate(pieces, axis=0)
    keep = jnp.exp(both_parts(jnp.log(1.0 - cover), before[...], NN))
    cover_ref[tile] = cover
    keep_ref[tile] = keep
    shown = mxu((cover * keep).astype(jnp.bfloat16), colors, NT)
    total[...] += shown[:, 0:128] + shown[:, 128:256]


def backward_tile(tile, band, picked, after, cover_ref, keep_ref, grad_ref, results):
    rows = [picked[tile, q : q + 1, :] for q in range(9)]
    grads = jnp.concatenate([grad_ref[pl.ds(3 * tile + c, 1), :] for c in range(3)], axis=0)
    colors = jnp.concatenate(rows[6:9], axis=0)
    grads_high = grads.astype(jnp.bfloat16).astype(jnp.float32)
    grads_low = grads - grads_high
    colors_high = colors.astype(jnp.bfloat16).astype(jnp.float32)
    colors_low = colors - colors_high
    blank = jnp.zeros((7, 256), jnp.float32)
    left = jnp.concatenate([grads_high, grads_high, grads_low, blank], axis=0).astype(jnp.bfloat16)
    right = jnp.concatenate([colors_high, colors_low, colors_high, blank], axis=0).astype(jnp.bfloat16)
    both = jnp.concatenate([grads_high, grads_low, blank, blank[0:3]], axis=0).astype(jnp.bfloat16)
    delta_x, delta_y = tile_deltas(tile, band, rows[0], rows[1])
    shade = mxu(left, right, TN)
    weight = keep_ref[tile]
    lit = weight * shade
    behind = mxu(lit.astype(jnp.bfloat16), after[...], NN)
    pull = lit - behind * cover_ref[tile]
    sum_0 = jnp.zeros((16, 256), jnp.float32)
    sum_y = sum_0
    sum_yy = sum_0
    for i in range(16):
        piece = pull[16 * i : 16 * i + 16]
        level = delta_y[i : i + 1]
        piece_y = piece * level
        sum_0 = sum_0 + piece
        sum_y = sum_y + piece_y
        sum_yy = sum_yy + piece_y * level
    color_grad = mxu(both, weight.astype(jnp.bfloat16), NN)
    color_grad = color_grad[0:3] + color_grad[3:6]
    sum_x = sum_0 * delta_x

    def fold(value):
        return jnp.sum(value, axis=0, keepdims=True)

    moment_x = fold(sum_x)
    moment_y = fold(sum_y)
    live = rows[5] > 0.0
    values = [
        rows[2] * moment_x + rows[3] * moment_y,
        rows[4] * moment_y + rows[3] * moment_x,
        -0.5 * fold(sum_x * delta_x),
        -fold(sum_y * delta_x),
        -0.5 * fold(sum_yy),
        jnp.where(live, fold(sum_0) / jnp.where(live, rows[5], 1.0), 0.0),
        color_grad[0:1],
        color_grad[1:2],
        color_grad[2:3],
    ]
    for q in range(9):
        results[tile, q : q + 1, :] = values[q]


def blurred_down(planes, count):
    taps = window_taps()
    result = taps[5] * planes[5 : 5 + count]
    for k in range(5):
        result = result + taps[k] * (planes[k : k + count] + planes[10 - k : 10 - k + count])
    return result


def blurred_across(planes, spread):
    taps = window_taps()
    spread[:, 0:8, :] = pltpu.roll(planes[:, 8:16], 3, 2)
    spread[:, 8:24, :] = planes
    spread[:, 24:32, :] = pltpu.roll(planes[:, 0:8], 125, 2)
    result = taps[5] * planes
    for k in range(5):
        result = result + taps[k] * (spread[:, 3 + k : 19 + k, :] + spread[:, 13 - k : 29 - k, :])
    return result


def rows_within(field_ref, band, last_band):
    rows = lax.broadcasted_iota(jnp.int32, (36, 16, 128), 0) - 10 + 16 * band
    within = (rows >= 0) & (rows < 16 * (last_band + 1))
    return jnp.where(within, field_ref[...].reshape(36, 16, 128), 0.0), within


def window_of(plane, spread):
    return blurred_across(blurred_down(plane, 26), spread)


def truth_step(band, last_band, truth_ref, spread, truth_stats):
    truth, _ = rows_within(truth_ref, band, last_band)
    truth_stats[0] = window_of(truth, spread.at[0])
    truth_stats[1] = window_of(truth * truth, spread.at[1])


def window_step(band, last_band, image_ref, truth_ref, grad_ref, spread, truth_stats):
    image, within = rows_within(image_ref, band, last_band)
    truth, _ = rows_within(truth_ref, band, last_band)
    mean_x = window_of(image, spread.at[0])
    power_x = window_of(image * image, spread.at[1])
    cross_xy = window_of(image * truth, spread.at[2])
    mean_y, power_y = truth_stats[0], truth_stats[1]
    similarity, ssim_back = jax.vjp(
        lambda level_x, energy_x, product_xy: ssim_map(
            level_x, mean_y, energy_x, power_y, product_xy
        ),
        mean_x,
        power_x,
        cross_xy,
    )
    lanes = lax.broadcasted_iota(jnp.int32, (26, 16, 128), 2)
    counted = within[5:31] & (lanes < 96)
    pulled = []
    for k, plane in enumerate(ssim_back(jnp.where(counted, -0.8, 0.0))):
        pulled.append(blurred_across(blurred_down(plane, 16), spread.at[k, 0:16]))
    shown = image[10:26]
    wanted = truth[10:26]
    difference = shown - wanted
    smooth = jnp.sqrt(difference * difference + 0.0001)
    loss = jnp.where(lanes[0:16] < 96, 0.2 * smooth + 0.8 * (1.0 - similarity[5:21]), 0.0)
    pixel_grad = 0.2 * difference / smooth + pulled[0] + 2.0 * shown * pulled[1] + wanted * pulled[2]
    grad_ref[...] = jnp.transpose(pixel_grad.reshape(256, 128))
    return jnp.sum(jnp.sum(loss, axis=0), axis=0, keepdims=True)


def render_kernel(
    slots_ref, list_ref, count_ref, view_ref, back_ref, target_ref, index_ref, sent_ref,
    own_ref, other_ref,
    high_parts, low_parts, before, after, picked, cover_ref, keep_ref, results, total, slot_total, owner_total,
    target_rows, image_ref, truth_ref, grad_ref, spread, truth_stats,
    outgoing, incoming, send_sem, recv_sem, plane_sem, cube_sem, halo_send, halo_recv, swap_send, swap_recv,
):
    me = lax.axis_index("tile")
    pair = 1 - lax.axis_index("view")
    band = me
    last_band = lax.axis_size("tile") - 1
    view = view_ref[0]
    barrier = pltpu.get_barrier_semaphore()
    lines = [axis_peers(me, stride) for stride in (1, 4, 16)]
    for line in lines:
        signal_all(barrier, line)
    pl.semaphore_signal(barrier, inc=1, device_id={"view": pair}, device_id_type=MESH)

    for q in range(9):
        for half in range(2):
            store_parts(
                slots_ref[32 * half : 32 * half + 32, q, :], high_parts, low_parts, q, pl.ds(128 * half, 128)
            )
    row_ids = lax.broadcasted_iota(jnp.int32, (256, 256), 0)
    column_ids = lax.broadcasted_iota(jnp.int32, (256, 256), 1)
    before[...] = (row_ids < column_ids).astype(jnp.float32).astype(jnp.bfloat16)
    after[...] = (row_ids > column_ids).astype(jnp.float32).astype(jnp.bfloat16)
    own_pixels = slice(160, 416)
    target_rows[0:96, :] = target_ref[...]
    target_rows[96:128, :] = jnp.zeros((32, 256), jnp.float32)
    truth_ref[own_pixels, :] = jnp.transpose(target_rows[...])
    lanes = lax.broadcasted_iota(jnp.int32, (1, 256), 1)
    high_ids = lax.broadcasted_iota(jnp.int32, (32, 256), 0)

    def pick(tile, carry):
        high, low = slot_place(list_ref[pl.ds(tile, 1), :])
        low_ids = lax.broadcasted_iota(jnp.int32, (256, 256), 0)
        rows = pick_rows(high_parts, low_parts, one_hot(low_ids, low), high_ids == high)
        rows[5] = jnp.where(lanes < count_ref[0, tile], rows[5], 0.0)
        for c in range(3):
            rows[6 + c] = rows[6 + c] - back_ref[view, c]
        for q in range(9):
            picked[tile, q : q + 1, :] = rows[q]
        return carry

    lax.fori_loop(0, 32, pick, 0, unroll=4)
    pl.semaphore_wait(barrier, 10)
    signal_all(plane_sem, lines[1])
    total[...] = jnp.zeros_like(total)

    def forward(tile, carry):
        forward_tile(tile, band, picked, before, cover_ref, keep_ref, total)
        return carry

    lax.fori_loop(0, 12, forward, 0, unroll=4)
    pl.semaphore_wait(plane_sem, 3)
    signal_all(cube_sem, lines[2])
    lax.fori_loop(12, 24, forward, 0, unroll=4)
    pl.semaphore_wait(cube_sem, 3)

    following, previous = lax.rem(me + 1, 64), lax.rem(me + 63, 64)

    def halo(field, k, peer, source, target):
        return pltpu.make_async_remote_copy(
            src_ref=field.at[pl.ds(source, 160), :],
            dst_ref=field.at[pl.ds(target, 160), :],
            send_sem=halo_send.at[k],
            recv_sem=halo_recv.at[k],
            device_id={"tile": peer},
            device_id_type=MESH,
        )

    copies = [halo(truth_ref, 0, following, 256, 0), halo(truth_ref, 1, previous, 160, 416)]
    for copy in copies:
        copy.start()
    lax.fori_loop(24, 32, forward, 0, unroll=4)
    color_lanes = lax.broadcasted_iota(jnp.int32, (1, 128), 1)
    backdrop = jnp.zeros((1, 128), jnp.float32)
    for c in range(3):
        here = (lax.rem(color_lanes, 3) == c) & (color_lanes < 96)
        backdrop = jnp.where(here, back_ref[view, c], backdrop)
    image_ref[own_pixels, :] = total[...] + backdrop
    shown = [halo(image_ref, 2, following, 256, 0), halo(image_ref, 3, previous, 160, 416)]
    for copy in shown:
        copy.start()
    for copy in copies:
        copy.wait()
    truth_step(band, last_band, truth_ref, spread, truth_stats)

    def prepare(tile, carry):
        cover = cover_ref[tile]
        keep_ref[tile] = cover * keep_ref[tile]
        cover_ref[tile] = cover / (1.0 - cover)
        return carry

    lax.fori_loop(0, 32, prepare, 0, unroll=2)
    for copy in shown:
        copy.wait()
    loss = window_step(band, last_band, image_ref, truth_ref, grad_ref, spread, truth_stats)

    def backward(group, carry):
        for slot in range(4):
            backward_tile(
                4 * group + slot, band, picked, after, cover_ref, keep_ref, grad_ref, results
            )
        return carry

    lax.fori_loop(0, 8, backward, 0)
    slot_total[...] = jnp.zeros_like(slot_total)

    def joined(values):
        return jnp.concatenate(values, axis=1)

    def place_slots(tile, carry):
        tiles = (tile, tile + 16)
        high, low = slot_place(joined([list_ref[pl.ds(t, 1), :] for t in tiles]))
        low_ids = lax.broadcasted_iota(jnp.int32, (256, 512), 0)
        slot_ids = lax.broadcasted_iota(jnp.int32, (32, 512), 0)
        rows = [joined([results[t, q : q + 1, :] for t in tiles]) for q in range(9)]
        place_rows(rows, slot_total, one_hot(low_ids, low), slot_ids == high)
        return carry

    lax.fori_loop(0, 16, place_slots, 0, unroll=4)
    for q in range(9):
        for half in range(2):
            outgoing[32 * half : 32 * half + 32, q, :] = slot_total[
                32 * q : 32 * q + 32, 128 * half : 128 * half + 128
            ]
    outgoing[:, 9, :] = jnp.broadcast_to(loss, (64, 128))

    def send(p, carry):
        block_copy(outgoing, incoming, send_sem, recv_sem, lax.rem(me + p, 64)).start()
        return carry

    lax.fori_loop(1, 64, send, 0)
    owner_total[...] = jnp.zeros_like(owner_total)
    owner_ids = lax.broadcasted_iota(jnp.int32, (64, 512), 0)
    finish_blocks(outgoing, incoming, send_sem, recv_sem)

    def place_owned(first, carry):
        bands = (first, first + 16, first + 32, first + 48)
        index = joined([index_ref[pl.ds(d, 1), :] for d in bands])
        live = joined([(color_lanes < sent_ref[0, d]).astype(jnp.int32) for d in bands])
        high = jnp.where(live > 0, (index >> 7) & 63, -1)
        low = (index & 127) + ((index >> 13) << 7)
        low_ids = lax.broadcasted_iota(jnp.int32, (256, 512), 0)
        rows = [joined([incoming[d, q : q + 1, :] for d in bands]) for q in range(9)]
        place_rows(rows, owner_total, one_hot(low_ids, low), owner_ids == high)
        return carry

    lax.fori_loop(0, 16, place_owned, 0, unroll=4)
    for q in range(9):
        for half in range(2):
            own_ref[q, 64 * half : 64 * half + 64, :] = owner_total[
                64 * q : 64 * q + 64, 128 * half : 128 * half + 128
            ]
    losses = jnp.sum(incoming[:, 9, :], axis=0, keepdims=True)
    own_ref[9] = jnp.broadcast_to(losses, (128, 128))
    swap = pltpu.make_async_remote_copy(
        src_ref=own_ref,
        dst_ref=other_ref,
        send_sem=swap_send,
        recv_sem=swap_recv,
        device_id={"view": pair},
        device_id_type=MESH,
    )
    swap.start()
    swap.wait()


def render_step(slots, lists, counts, view, back, target_tiles, send_index, send_count):
    smem = pl.BlockSpec(memory_space=pltpu.SMEM)
    vmem = pl.BlockSpec(memory_space=pltpu.VMEM)
    shape = jax.ShapeDtypeStruct((10, 128, 128), jnp.float32)
    f32, bf16 = jnp.float32, jnp.bfloat16
    return pl.pallas_call(
        render_kernel,
        out_shape=(shape, shape),
        in_specs=[vmem, vmem, smem, smem, smem, vmem, vmem, smem],
        out_specs=(vmem, vmem),
        scratch_shapes=[
            pltpu.VMEM((288, 512), bf16),
            pltpu.VMEM((64, 256), bf16),
            pltpu.VMEM((256, 256), bf16),
            pltpu.VMEM((256, 256), bf16),
            pltpu.VMEM((32, 9, 256), f32),
            pltpu.VMEM((32, 256, 256), f32),
            pltpu.VMEM((32, 256, 256), f32),
            pltpu.VMEM((32, 9, 256), f32),
            pltpu.VMEM((256, 128), f32),
            pltpu.VMEM((288, 256), f32),
            pltpu.VMEM((576, 256), f32),
            pltpu.VMEM((128, 256), f32),
            pltpu.VMEM((576, 128), f32),
            pltpu.VMEM((576, 128), f32),
            pltpu.VMEM((128, 256), f32),
            pltpu.VMEM((3, 26, 32, 128), f32),
            pltpu.VMEM((2, 26, 16, 128), f32),
            *exchange_scratch(10),
            pltpu.SemaphoreType.DMA((4,)),
            pltpu.SemaphoreType.DMA((4,)),
            pltpu.SemaphoreType.DMA,
            pltpu.SemaphoreType.DMA,
        ],
        compiler_params=pltpu.CompilerParams(
            collective_id=1, has_side_effects=True, vmem_limit_bytes=34 * MIB
        ),
        cost_estimate=pl.CostEstimate(flops=20_000_000_000, bytes_accessed=4_000_000, transcendentals=7_000_000),
        name="render_step",
    )(slots, lists, counts, view, back, target_tiles, send_index, send_count)


RATES = [0.016] * 3 + [0.005] * 3 + [0.001] * 4 + [0.05] + [0.0025] * 3 + [0.000125] * 45
LOSS_TERMS = 2 * 3 * 1024 * 512


def update_kernel(
    params_ref, first_ref, second_ref, own_ref, other_ref, view_ref, shear_ref, offset_ref, center_ref,
    params_out, first_out, second_out, loss_out, dense,
):
    refs = (shear_ref, offset_ref, center_ref)
    cameras = [camera_of(refs, 0), camera_of(refs, 1)]
    is_first = view_ref[0] == 0
    losses = own_ref[9, 0:1, :] + other_ref[9, 0:1, :]
    loss_out[...] = jnp.sum(losses, axis=1, keepdims=True) / LOSS_TERMS

    def part(sub, carry):
        rows = dense_rows(params_ref, sub)
        _, pull_back = jax.vjp(lambda *values: project_rows(values, cameras), *rows)
        here = pl.ds(pl.multiple_of(8 * sub, 8), 8)
        own = [own_ref[q, here, :] for q in range(9)]
        other = [other_ref[q, here, :] for q in range(9)]
        gradient = pull_back(
            [
                [jnp.where(is_first, a, b) for a, b in zip(own, other)],
                [jnp.where(is_first, b, a) for a, b in zip(own, other)],
            ]
        )
        for r in range(59):
            dense[8 * r : 8 * r + 8, :] = gradient[r]
        for first in range(0, 59, 8):
            size = min(8, 59 - first)
            row_ids = lax.broadcasted_iota(jnp.int32, (size, 128), 0)
            rate = jnp.full((size, 128), RATES[first], jnp.float32)
            for r in range(1, size):
                if RATES[first + r] != RATES[first + r - 1]:
                    rate = jnp.where(row_ids >= r, RATES[first + r], rate)
            rate = rate / (1.0 - 0.9**STEP_COUNT)
            for c in range(8):
                columns = pl.ds(pl.multiple_of(1024 * sub + 128 * c, 128), 128)
                here = (slice(first, first + size), columns)
                grad = dense[pl.ds(8 * first + c, size, stride=8), :]
                new_first = 0.9 * first_ref[here] + 0.1 * grad
                new_second = 0.999 * second_ref[here] + 0.001 * grad * grad
                scale = jnp.sqrt(new_second * (1.0 / (1.0 - 0.999**STEP_COUNT))) + 1e-15
                params_out[here] = params_ref[here] - rate * new_first / scale
                first_out[here] = new_first
                second_out[here] = new_second
        return carry

    lax.fori_loop(0, BLOCK // 1024, part, 0)


def update(params, first_moment, second_moment, own, other, view, shear, offset, center):
    smem = pl.BlockSpec(memory_space=pltpu.SMEM)
    block = pl.BlockSpec((59, BLOCK), lambda i: (0, i))
    grads = pl.BlockSpec((10, BLOCK // 128, 128), lambda i: (0, i, 0))
    shape = jax.ShapeDtypeStruct(params.shape, jnp.float32)
    return pl.pallas_call(
        update_kernel,
        grid=(16384 // BLOCK,),
        out_shape=(shape, shape, shape, jax.ShapeDtypeStruct((1, 1), jnp.float32)),
        in_specs=[block, block, block, grads, grads, smem, smem, smem, smem],
        out_specs=(block, block, block, pl.BlockSpec((1, 1), lambda i: (0, 0))),
        scratch_shapes=[pltpu.VMEM((59 * 8, 128), jnp.float32)],
        compiler_params=pltpu.CompilerParams(vmem_limit_bytes=16 * MIB),
        name="update",
    )(params, first_moment, second_moment, own, other, view, shear, offset, center)


def shards(
    params,
    first_moment,
    second_moment,
    target,
    view_shear,
    view_offset,
    cam_center,
    background,
    send_index,
    send_count,
    tile_list,
    tile_count,
):
    view_index = lax.axis_index("view")
    view = view_index.astype(jnp.int32).reshape(1)
    incoming = project_and_pick(params, send_index[0], view, view_shear, view_offset, cam_center)
    target_tiles = target[0].reshape(3, 16, 32, 16).transpose(2, 0, 1, 3).reshape(96, 256)
    own_grad, other_grad = render_step(
        incoming, tile_list[0, 0], tile_count, view, background, target_tiles, send_index[0], send_count
    )
    new_params, new_first, new_second, mean_loss = update(
        params, first_moment, second_moment, own_grad, other_grad, view, view_shear, view_offset, cam_center
    )
    return (new_params, new_first, new_second, mean_loss[0, 0])


def solution(mesh):
    placed = (
        P(None, "tile"),
        P(None, "tile"),
        P(None, "tile"),
        P("view", None, "tile", None),
        P(),
        P(),
        P(),
        P(),
        P("tile", None, None),
        P("tile", None),
        P("view", "tile", None, None),
        P("tile", None),
    )
    return jax.shard_map(
        shards,
        mesh=mesh,
        in_specs=placed,
        out_specs=(P(None, "tile"), P(None, "tile"), P(None, "tile"), P()),
        check_vma=False,
    )
```

```python
import functools
import math

import jax
import jax.numpy as jnp
from jax import lax
from jax.experimental import pallas as pl
from jax.experimental.pallas import tpu as pltpu
from jax.sharding import PartitionSpec as P

STEP_COUNT = 20
LIST = 256


def window_taps():
    raw_taps = [math.exp(-(position - 5) * (position - 5) / 4.5) for position in range(11)]
    return [element / sum(raw_taps) for element in raw_taps]


def harmonics(unit_x, unit_y, unit_z):
    square_x = unit_x * unit_x
    square_y = unit_y * unit_y
    square_z = unit_z * unit_z
    return [
        0.28209479177387814 * jnp.ones_like(unit_x),
        -0.4886025119029199 * unit_y,
        0.4886025119029199 * unit_z,
        -0.4886025119029199 * unit_x,
        1.0925484305920792 * unit_x * unit_y,
        -1.0925484305920792 * unit_y * unit_z,
        0.31539156525252005 * (2.0 * square_z - square_x - square_y),
        -1.0925484305920792 * unit_x * unit_z,
        0.5462742152960396 * (square_x - square_y),
        -0.5900435899266435 * unit_y * (3.0 * square_x - square_y),
        2.890611442640554 * unit_x * unit_y * unit_z,
        -0.4570457994644658 * unit_y * (4.0 * square_z - square_x - square_y),
        0.3731763325901154 * unit_z * (2.0 * square_z - 3.0 * square_x - 3.0 * square_y),
        -0.4570457994644658 * unit_x * (4.0 * square_z - square_x - square_y),
        1.445305721320277 * unit_z * (square_x - square_y),
        -0.5900435899266435 * unit_x * (square_x - 3.0 * square_y),
    ]


def ssim_map(level_x, level_y, energy_x, energy_y, product_xy):
    upper = (2.0 * level_x * level_y + 0.0001) * (2.0 * (product_xy - level_x * level_y) + 0.0009)
    lower = (level_x * level_x + level_y * level_y + 0.0001) * (
        energy_x - level_x * level_x + (energy_y - level_y * level_y) + 0.0009
    )
    return upper / lower


MESH = pl.DeviceIdType.MESH
MIB = 1024 * 1024
NN = (((1,), (0,)), ((), ()))
NT = (((1,), (1,)), ((), ()))
TN = (((0,), (0,)), ((), ()))


def mxu(left, right, dims):
    return lax.dot_general(left, right, dims, preferred_element_type=jnp.float32)


def split2(value):
    high = value.astype(jnp.bfloat16)
    low = (value - high.astype(jnp.float32)).astype(jnp.bfloat16)
    return high, low


def split3(value):
    high = value.astype(jnp.bfloat16)
    rest = value - high.astype(jnp.float32)
    middle = rest.astype(jnp.bfloat16)
    low = (rest - middle.astype(jnp.float32)).astype(jnp.bfloat16)
    return high, middle, low


def project_rows(rows, cameras):
    pos_x, pos_y, pos_z = rows[0:3]
    scales = [jnp.exp(row) for row in rows[3:6]]
    quat_w, quat_x, quat_y, quat_z = rows[6:10]
    norm = 1.0 / jnp.sqrt(
        quat_w * quat_w + quat_x * quat_x + quat_y * quat_y + quat_z * quat_z
    )
    quat_w, quat_x, quat_y, quat_z = quat_w * norm, quat_x * norm, quat_y * norm, quat_z * norm
    rotation = [
        [
            1.0 - 2.0 * (quat_y * quat_y + quat_z * quat_z),
            2.0 * (quat_x * quat_y - quat_w * quat_z),
            2.0 * (quat_x * quat_z + quat_w * quat_y),
        ],
        [
            2.0 * (quat_x * quat_y + quat_w * quat_z),
            1.0 - 2.0 * (quat_x * quat_x + quat_z * quat_z),
            2.0 * (quat_y * quat_z - quat_w * quat_x),
        ],
        [
            2.0 * (quat_x * quat_z - quat_w * quat_y),
            2.0 * (quat_y * quat_z + quat_w * quat_x),
            1.0 - 2.0 * (quat_x * quat_x + quat_y * quat_y),
        ],
    ]
    opacity = 1.0 / (1.0 + jnp.exp(-rows[10]))
    records = []
    for shear_x, shear_y, offset_x, offset_y, center_x, center_y, center_z in cameras:
        first = [(rotation[0][k] + shear_x * rotation[2][k]) * scales[k] for k in range(3)]
        second = [(rotation[1][k] + shear_y * rotation[2][k]) * scales[k] for k in range(3)]
        cov_xx = first[0] * first[0] + first[1] * first[1] + first[2] * first[2] + 0.3
        cov_yy = second[0] * second[0] + second[1] * second[1] + second[2] * second[2] + 0.3
        cov_xy = first[0] * second[0] + first[1] * second[1] + first[2] * second[2]
        inverse = 1.0 / (cov_xx * cov_yy - cov_xy * cov_xy)
        toward_x = pos_x - center_x
        toward_y = pos_y - center_y
        toward_z = pos_z - center_z
        shrink = 1.0 / jnp.sqrt(toward_x * toward_x + toward_y * toward_y + toward_z * toward_z)
        basis = harmonics(toward_x * shrink, toward_y * shrink, toward_z * shrink)
        colors = []
        for c in range(3):
            total = basis[0] * rows[11 + c]
            for k in range(1, 16):
                total = total + basis[k] * rows[11 + 3 * k + c]
            colors.append(0.5 + total)
        records.append(
            [
                pos_x + shear_x * pos_z + offset_x,
                pos_y + shear_y * pos_z + offset_y,
                cov_yy * inverse,
                -cov_xy * inverse,
                cov_xx * inverse,
                opacity,
                *colors,
            ]
        )
    return records


def camera_of(refs, view):
    shear_ref, offset_ref, center_ref = refs
    return (
        shear_ref[view, 0],
        shear_ref[view, 1],
        offset_ref[view, 0],
        offset_ref[view, 1],
        center_ref[view, 0],
        center_ref[view, 1],
        center_ref[view, 2],
    )


BLOCK = 4096


def dense_rows(source_ref, sub):
    count = source_ref.shape[0]
    columns = pl.ds(pl.multiple_of(1024 * sub, 1024), 1024)
    rows = []
    for first in range(0, count, 8):
        size = min(8, count - first)
        block = source_ref[first : first + size, columns].reshape(size, 8, 128)
        rows += [block[r] for r in range(size)]
    return rows


def axis_peers(me, stride):
    place = lax.rem(me // stride, 4)
    return [me + (lax.rem(place + j, 4) - place) * stride for j in range(1, 4)]


def signal_all(semaphore, peers):
    for peer in peers:
        pl.semaphore_signal(semaphore, inc=1, device_id={"tile": peer}, device_id_type=MESH)


def greet_all(step, semaphores):
    plane_sem, cube_sem = semaphores
    me = lax.axis_index("tile")
    lines = [axis_peers(me, stride) for stride in (1, 4, 16)]
    barrier = pltpu.get_barrier_semaphore()

    @pl.when(step == 0)
    def _():
        for line in lines:
            signal_all(barrier, line)

    @pl.when(step == 1)
    def _():
        pl.semaphore_wait(barrier, 9)
        signal_all(plane_sem, lines[1])

    @pl.when(step == 2)
    def _():
        pl.semaphore_wait(plane_sem, 3)
        signal_all(cube_sem, lines[2])

    @pl.when(step == 3)
    def _():
        pl.semaphore_wait(cube_sem, 3)


def block_copy(outgoing, incoming, send_sem, recv_sem, peer):
    me = lax.axis_index("tile")
    return pltpu.make_async_remote_copy(
        src_ref=outgoing.at[peer],
        dst_ref=incoming.at[me],
        send_sem=send_sem,
        recv_sem=recv_sem,
        device_id={"tile": peer},
        device_id_type=MESH,
    )


def send_block(outgoing, incoming, send_sem, recv_sem, peer):
    @pl.when(peer != lax.axis_index("tile"))
    def _():
        block_copy(outgoing, incoming, send_sem, recv_sem, peer).start()


def finish_blocks(outgoing, incoming, send_sem, recv_sem):
    me = lax.axis_index("tile")
    pltpu.make_async_remote_copy(
        src_ref=outgoing.at[0:63],
        dst_ref=incoming.at[0:63],
        send_sem=send_sem,
        recv_sem=recv_sem,
        device_id={"tile": lax.rem(me + 1, 64)},
        device_id_type=MESH,
    ).wait()
    incoming[me] = outgoing[me]


def exchange_scratch(rows):
    return [
        pltpu.VMEM((64, rows, 128), jnp.float32),
        pltpu.VMEM((64, rows, 128), jnp.float32),
        pltpu.SemaphoreType.DMA,
        pltpu.SemaphoreType.DMA,
        pltpu.SemaphoreType.REGULAR,
        pltpu.SemaphoreType.REGULAR,
    ]


def project_kernel(
    params_ref, index_ref, view_ref, shear_ref, offset_ref, center_ref, out_ref,
    table, high_parts, low_parts, outgoing, incoming, send_sem, recv_sem, *greetings,
):
    step = pl.program_id(0)
    greet_all(step, greetings)
    camera = camera_of((shear_ref, offset_ref, center_ref), view_ref[0])

    def part(sub, carry):
        record = project_rows(dense_rows(params_ref, sub), [camera])[0]
        first = pl.multiple_of(step * (BLOCK // 128) + 8 * sub, 8)
        for q in range(9):
            table[q, pl.ds(first, 8), :] = record[q]
        return carry

    lax.fori_loop(0, BLOCK // 1024, part, 0, unroll=2)

    @pl.when(step == pl.num_programs(0) - 1)
    def _():
        for q in range(9):
            for half in range(2):
                store_parts(
                    table[q, 64 * half : 64 * half + 64, :],
                    high_parts, low_parts, q, pl.ds(128 * half, 128),
                )
        low_ids = lax.broadcasted_iota(jnp.int32, (256, 256), 0)
        high_ids = lax.broadcasted_iota(jnp.int32, (64, 256), 0)

        def pick(pair, carry):
            index = jnp.concatenate(
                [index_ref[pl.ds(pair, 1), :], index_ref[pl.ds(pair + 32, 1), :]], axis=1
            )
            high = (index >> 7) & 63
            low = (index & 127) + ((index >> 13) << 7)
            rows = pick_rows(high_parts, low_parts, one_hot(low_ids, low), high_ids == high)
            for q in range(9):
                outgoing[pair, q : q + 1, :] = rows[q][:, 0:128]
                outgoing[pair + 32, q : q + 1, :] = rows[q][:, 128:256]
            return carry

        me = lax.axis_index("tile")

        def group(part, carry):
            first = lax.rem(part + me, 4) * 8
            lax.fori_loop(0, 8, lambda k, carry: pick(first + k, carry), 0, unroll=4)

            def send(k, carry):
                for peer in (first + k, first + k + 32):
                    send_block(outgoing, incoming, send_sem, recv_sem, peer)
                return carry

            lax.fori_loop(0, 8, send, 0)
            return carry

        lax.fori_loop(0, 4, group, 0)
        finish_blocks(outgoing, incoming, send_sem, recv_sem)
        out_ref[...] = incoming[...]


def project_and_pick(params, send_index, view, shear, offset, center):
    smem = pl.BlockSpec(memory_space=pltpu.SMEM)
    return pl.pallas_call(
        project_kernel,
        grid=(16384 // BLOCK,),
        out_shape=jax.ShapeDtypeStruct((64, 9, 128), jnp.float32),
        in_specs=[
            pl.BlockSpec((59, BLOCK), lambda i: (0, i)),
            pl.BlockSpec((64, 128), lambda i: (0, 0)),
            smem,
            smem,
            smem,
            smem,
        ],
        out_specs=pl.BlockSpec((64, 9, 128), lambda i: (0, 0, 0)),
        scratch_shapes=[
            pltpu.VMEM((9, 128, 128), jnp.float32),
            pltpu.VMEM((576, 512), jnp.bfloat16),
            pltpu.VMEM((128, 256), jnp.bfloat16),
            *exchange_scratch(9),
        ],
        compiler_params=pltpu.CompilerParams(
            collective_id=0, has_side_effects=True, vmem_limit_bytes=56 * MIB
        ),
        name="project_and_pick",
    )(params, send_index, view, shear, offset, center)


def slot_place(index):
    return (index >> 7) & 31, (index & 127) + ((index >> 12) << 7)


def one_hot(ids, values):
    return (ids == values).astype(jnp.float32).astype(jnp.bfloat16)


def store_parts(rows, high_parts, low_parts, q, columns):
    count = rows.shape[0]
    high, middle, low = split3(rows)
    here = pl.ds(count * q, count)
    width = columns.size
    high_parts[here, columns] = high
    high_parts[here, pl.ds(columns.start + 256, width)] = middle
    if q < 2:
        low_parts[here, columns] = low


def both_parts(value, right, dims):
    sums = mxu(jnp.concatenate(split2(value), axis=0), right, dims)
    return sums[: value.shape[0]] + sums[value.shape[0] :]


def pick_rows(high_parts, low_parts, hot, mask):
    count = mask.shape[0]
    found = mxu(high_parts[...], jnp.concatenate([hot, hot], axis=0), NN)
    found_low = mxu(low_parts[...], hot, NN)
    rows = []
    for q in range(9):
        part = found[count * q : count * q + count]
        if q < 2:
            part = part + found_low[count * q : count * q + count]
        rows.append(jnp.sum(jnp.where(mask, part, 0.0), axis=0, keepdims=True))
    return rows


def place_rows(rows, total, hot, mask):
    count = mask.shape[0]
    high_rows, low_rows = [], []
    for row in rows:
        high = row.astype(jnp.bfloat16).astype(jnp.float32)
        high_rows.append(jnp.where(mask, high, 0.0))
        low_rows.append(jnp.where(mask, row - high, 0.0))
    placed = jnp.concatenate(high_rows + low_rows, axis=0).astype(jnp.bfloat16)
    sums = mxu(placed, hot, NT)
    total[...] += sums[: 9 * count] + sums[9 * count :]


def tile_deltas(tile, band, u_row, w_row):
    offsets = lax.broadcasted_iota(jnp.int32, (16, 256), 0)
    pixel_x = (offsets + 16 * tile).astype(jnp.float32) + 0.5
    pixel_y = (offsets + 16 * band).astype(jnp.float32) + 0.5
    return pixel_x - u_row, pixel_y - w_row


def forward_tile(tile, band, picked, before, cover_ref, keep_ref, total):
    rows = [picked[tile, q : q + 1, :] for q in range(9)]
    delta_x, delta_y = tile_deltas(tile, band, rows[0], rows[1])
    along_x = -0.5 * rows[2] * delta_x * delta_x
    mixed = -rows[3] * delta_x
    along_y = -0.5 * rows[4] * delta_y * delta_y
    color_ids = lax.broadcasted_iota(jnp.int32, (128, 256), 0)
    colors = jnp.zeros((128, 256), jnp.float32)
    for c in range(3):
        colors = jnp.where(color_ids == 3 * tile + c, rows[6 + c], colors)
    colors = jnp.concatenate(split2(colors), axis=0)
    pieces = []
    for i in range(16):
        exponent = along_x + (mixed * delta_y[i : i + 1] + along_y[i : i + 1])
        pieces.append(rows[5] * jnp.exp(exponent))
    cover = jnp.concatenate(pieces, axis=0)
    keep = jnp.exp(both_parts(jnp.log(1.0 - cover), before[...], NN))
    cover_ref[tile] = cover
    keep_ref[tile] = keep
    shown = mxu(jnp.concatenate(split2(cover * keep), axis=0), colors, NT)
    total[...] += shown[0:256, 0:128] + shown[0:256, 128:256] + shown[256:512, 0:128]


def backward_tile(tile, band, picked, after, cover_ref, keep_ref, grad_ref, results):
    rows = [picked[tile, q : q + 1, :] for q in range(9)]
    grads = jnp.concatenate([grad_ref[pl.ds(3 * tile + c, 1), :] for c in range(3)], axis=0)
    colors = jnp.concatenate(rows[6:9], axis=0)
    grads_high = grads.astype(jnp.bfloat16).astype(jnp.float32)
    grads_low = grads - grads_high
    colors_high = colors.astype(jnp.bfloat16).astype(jnp.float32)
    colors_low = colors - colors_high
    blank = jnp.zeros((7, 256), jnp.float32)
    left = jnp.concatenate([grads_high, grads_high, grads_low, blank], axis=0).astype(jnp.bfloat16)
    right = jnp.concatenate([colors_high, colors_low, colors_high, blank], axis=0).astype(jnp.bfloat16)
    both = jnp.concatenate([grads_high, grads_low, blank, blank[0:3]], axis=0).astype(jnp.bfloat16)
    delta_x, delta_y = tile_deltas(tile, band, rows[0], rows[1])
    shade = mxu(left, right, TN)
    weight = keep_ref[tile]
    lit = weight * shade
    behind = mxu(lit.astype(jnp.bfloat16), after[...], NN)
    pull = lit - behind * cover_ref[tile]
    sum_0 = jnp.zeros((16, 256), jnp.float32)
    sum_y = sum_0
    sum_yy = sum_0
    for i in range(16):
        piece = pull[16 * i : 16 * i + 16]
        level = delta_y[i : i + 1]
        piece_y = piece * level
        sum_0 = sum_0 + piece
        sum_y = sum_y + piece_y
        sum_yy = sum_yy + piece_y * level
    weight_high, weight_low = split2(weight)
    color_grad = mxu(both, weight_high, NN)
    color_grad = color_grad[0:3] + color_grad[3:6] + mxu(both, weight_low, NN)[0:3]
    sum_x = sum_0 * delta_x

    def fold(value):
        return jnp.sum(value, axis=0, keepdims=True)

    moment_x = fold(sum_x)
    moment_y = fold(sum_y)
    live = rows[5] > 0.0
    values = [
        rows[2] * moment_x + rows[3] * moment_y,
        rows[4] * moment_y + rows[3] * moment_x,
        -0.5 * fold(sum_x * delta_x),
        -fold(sum_y * delta_x),
        -0.5 * fold(sum_yy),
        jnp.where(live, fold(sum_0) / jnp.where(live, rows[5], 1.0), 0.0),
        color_grad[0:1],
        color_grad[1:2],
        color_grad[2:3],
    ]
    for q in range(9):
        results[tile, q : q + 1, :] = values[q]


def blurred_down(planes, count):
    taps = window_taps()
    result = taps[5] * planes[5 : 5 + count]
    for k in range(5):
        result = result + taps[k] * (planes[k : k + count] + planes[10 - k : 10 - k + count])
    return result


def blurred_across(planes, spread):
    taps = window_taps()
    spread[:, 0:8, :] = pltpu.roll(planes[:, 8:16], 3, 2)
    spread[:, 8:24, :] = planes
    spread[:, 24:32, :] = pltpu.roll(planes[:, 0:8], 125, 2)
    result = taps[5] * planes
    for k in range(5):
        result = result + taps[k] * (spread[:, 3 + k : 19 + k, :] + spread[:, 13 - k : 29 - k, :])
    return result


def rows_within(field_ref, band, last_band):
    rows = lax.broadcasted_iota(jnp.int32, (36, 16, 128), 0) - 10 + 16 * band
    within = (rows >= 0) & (rows < 16 * (last_band + 1))
    return jnp.where(within, field_ref[...].reshape(36, 16, 128), 0.0), within


def window_of(plane, spread):
    return blurred_across(blurred_down(plane, 26), spread)


def truth_step(band, last_band, truth_ref, spread, truth_stats):
    truth, _ = rows_within(truth_ref, band, last_band)
    truth_stats[0] = window_of(truth, spread.at[0])
    truth_stats[1] = window_of(truth * truth, spread.at[1])


def window_step(band, last_band, image_ref, truth_ref, grad_ref, spread, truth_stats):
    image, within = rows_within(image_ref, band, last_band)
    truth, _ = rows_within(truth_ref, band, last_band)
    mean_x = window_of(image, spread.at[0])
    power_x = window_of(image * image, spread.at[1])
    cross_xy = window_of(image * truth, spread.at[2])
    mean_y, power_y = truth_stats[0], truth_stats[1]
    similarity, ssim_back = jax.vjp(
        lambda level_x, energy_x, product_xy: ssim_map(
            level_x, mean_y, energy_x, power_y, product_xy
        ),
        mean_x,
        power_x,
        cross_xy,
    )
    lanes = lax.broadcasted_iota(jnp.int32, (26, 16, 128), 2)
    counted = within[5:31] & (lanes < 96)
    pulled = []
    for k, plane in enumerate(ssim_back(jnp.where(counted, -0.8, 0.0))):
        pulled.append(blurred_across(blurred_down(plane, 16), spread.at[k, 0:16]))
    shown = image[10:26]
    wanted = truth[10:26]
    difference = shown - wanted
    smooth = jnp.sqrt(difference * difference + 0.0001)
    loss = jnp.where(lanes[0:16] < 96, 0.2 * smooth + 0.8 * (1.0 - similarity[5:21]), 0.0)
    pixel_grad = 0.2 * difference / smooth + pulled[0] + 2.0 * shown * pulled[1] + wanted * pulled[2]
    grad_ref[...] = jnp.transpose(pixel_grad.reshape(256, 128))
    return jnp.sum(jnp.sum(loss, axis=0), axis=0, keepdims=True)


def render_kernel(
    slots_ref, list_ref, count_ref, view_ref, back_ref, target_ref, index_ref, sent_ref,
    own_ref, other_ref,
    high_parts, low_parts, before, after, picked, cover_ref, keep_ref, results, total, slot_total, owner_total,
    target_rows, image_ref, truth_ref, grad_ref, spread, truth_stats,
    outgoing, incoming, send_sem, recv_sem, plane_sem, cube_sem, halo_send, halo_recv, swap_send, swap_recv,
):
    me = lax.axis_index("tile")
    pair = 1 - lax.axis_index("view")
    band = me
    last_band = lax.axis_size("tile") - 1
    view = view_ref[0]
    barrier = pltpu.get_barrier_semaphore()
    lines = [axis_peers(me, stride) for stride in (1, 4, 16)]
    for line in lines:
        signal_all(barrier, line)
    pl.semaphore_signal(barrier, inc=1, device_id={"view": pair}, device_id_type=MESH)

    for q in range(9):
        for half in range(2):
            store_parts(
                slots_ref[32 * half : 32 * half + 32, q, :], high_parts, low_parts, q, pl.ds(128 * half, 128)
            )
    row_ids = lax.broadcasted_iota(jnp.int32, (256, 256), 0)
    column_ids = lax.broadcasted_iota(jnp.int32, (256, 256), 1)
    before[...] = (row_ids < column_ids).astype(jnp.float32).astype(jnp.bfloat16)
    after[...] = (row_ids > column_ids).astype(jnp.float32).astype(jnp.bfloat16)
    own_pixels = slice(160, 416)
    target_rows[0:96, :] = target_ref[...]
    target_rows[96:128, :] = jnp.zeros((32, 256), jnp.float32)
    truth_ref[own_pixels, :] = jnp.transpose(target_rows[...])
    lanes = lax.broadcasted_iota(jnp.int32, (1, 256), 1)
    high_ids = lax.broadcasted_iota(jnp.int32, (32, 256), 0)

    def pick(tile, carry):
        high, low = slot_place(list_ref[pl.ds(tile, 1), :])
        low_ids = lax.broadcasted_iota(jnp.int32, (256, 256), 0)
        rows = pick_rows(high_parts, low_parts, one_hot(low_ids, low), high_ids == high)
        rows[5] = jnp.where(lanes < count_ref[0, tile], rows[5], 0.0)
        for c in range(3):
            rows[6 + c] = rows[6 + c] - back_ref[view, c]
        for q in range(9):
            picked[tile, q : q + 1, :] = rows[q]
        return carry

    lax.fori_loop(0, 32, pick, 0, unroll=4)
    pl.semaphore_wait(barrier, 10)
    signal_all(plane_sem, lines[1])
    total[...] = jnp.zeros_like(total)

    def forward(tile, carry):
        forward_tile(tile, band, picked, before, cover_ref, keep_ref, total)
        return carry

    lax.fori_loop(0, 12, forward, 0, unroll=4)
    pl.semaphore_wait(plane_sem, 3)
    signal_all(cube_sem, lines[2])
    lax.fori_loop(12, 24, forward, 0, unroll=4)
    pl.semaphore_wait(cube_sem, 3)

    following, previous = lax.rem(me + 1, 64), lax.rem(me + 63, 64)

    def halo(field, k, peer, source, target):
        return pltpu.make_async_remote_copy(
            src_ref=field.at[pl.ds(source, 160), :],
            dst_ref=field.at[pl.ds(target, 160), :],
            send_sem=halo_send.at[k],
            recv_sem=halo_recv.at[k],
            device_id={"tile": peer},
            device_id_type=MESH,
        )

    copies = [halo(truth_ref, 0, following, 256, 0), halo(truth_ref, 1, previous, 160, 416)]
    for copy in copies:
        copy.start()
    lax.fori_loop(24, 32, forward, 0, unroll=4)
    color_lanes = lax.broadcasted_iota(jnp.int32, (1, 128), 1)
    backdrop = jnp.zeros((1, 128), jnp.float32)
    for c in range(3):
        here = (lax.rem(color_lanes, 3) == c) & (color_lanes < 96)
        backdrop = jnp.where(here, back_ref[view, c], backdrop)
    image_ref[own_pixels, :] = total[...] + backdrop
    shown = [halo(image_ref, 2, following, 256, 0), halo(image_ref, 3, previous, 160, 416)]
    for copy in shown:
        copy.start()
    for copy in copies:
        copy.wait()
    truth_step(band, last_band, truth_ref, spread, truth_stats)

    def prepare(tile, carry):
        cover = cover_ref[tile]
        keep_ref[tile] = cover * keep_ref[tile]
        cover_ref[tile] = cover / (1.0 - cover)
        return carry

    lax.fori_loop(0, 32, prepare, 0, unroll=2)
    for copy in shown:
        copy.wait()
    loss = window_step(band, last_band, image_ref, truth_ref, grad_ref, spread, truth_stats)

    def backward(group, carry):
        for slot in range(4):
            backward_tile(
                4 * group + slot, band, picked, after, cover_ref, keep_ref, grad_ref, results
            )
        return carry

    lax.fori_loop(0, 8, backward, 0)
    slot_total[...] = jnp.zeros_like(slot_total)

    def joined(values):
        return jnp.concatenate(values, axis=1)

    def place_slots(tile, carry):
        tiles = (tile, tile + 16)
        high, low = slot_place(joined([list_ref[pl.ds(t, 1), :] for t in tiles]))
        low_ids = lax.broadcasted_iota(jnp.int32, (256, 512), 0)
        slot_ids = lax.broadcasted_iota(jnp.int32, (32, 512), 0)
        rows = [joined([results[t, q : q + 1, :] for t in tiles]) for q in range(9)]
        place_rows(rows, slot_total, one_hot(low_ids, low), slot_ids == high)
        return carry

    lax.fori_loop(0, 16, place_slots, 0, unroll=4)
    for q in range(9):
        for half in range(2):
            outgoing[32 * half : 32 * half + 32, q, :] = slot_total[
                32 * q : 32 * q + 32, 128 * half : 128 * half + 128
            ]
    outgoing[:, 9, :] = jnp.broadcast_to(loss, (64, 128))

    def send(p, carry):
        block_copy(outgoing, incoming, send_sem, recv_sem, lax.rem(me + p, 64)).start()
        return carry

    lax.fori_loop(1, 64, send, 0)
    owner_total[...] = jnp.zeros_like(owner_total)
    owner_ids = lax.broadcasted_iota(jnp.int32, (64, 512), 0)
    finish_blocks(outgoing, incoming, send_sem, recv_sem)

    def place_owned(first, carry):
        bands = (first, first + 16, first + 32, first + 48)
        index = joined([index_ref[pl.ds(d, 1), :] for d in bands])
        live = joined([(color_lanes < sent_ref[0, d]).astype(jnp.int32) for d in bands])
        high = jnp.where(live > 0, (index >> 7) & 63, -1)
        low = (index & 127) + ((index >> 13) << 7)
        low_ids = lax.broadcasted_iota(jnp.int32, (256, 512), 0)
        rows = [joined([incoming[d, q : q + 1, :] for d in bands]) for q in range(9)]
        place_rows(rows, owner_total, one_hot(low_ids, low), owner_ids == high)
        return carry

    lax.fori_loop(0, 16, place_owned, 0, unroll=4)
    for q in range(9):
        for half in range(2):
            own_ref[q, 64 * half : 64 * half + 64, :] = owner_total[
                64 * q : 64 * q + 64, 128 * half : 128 * half + 128
            ]
    losses = jnp.sum(incoming[:, 9, :], axis=0, keepdims=True)
    own_ref[9] = jnp.broadcast_to(losses, (128, 128))
    swap = pltpu.make_async_remote_copy(
        src_ref=own_ref,
        dst_ref=other_ref,
        send_sem=swap_send,
        recv_sem=swap_recv,
        device_id={"view": pair},
        device_id_type=MESH,
    )
    swap.start()
    swap.wait()


def render_step(slots, lists, counts, view, back, target_tiles, send_index, send_count):
    smem = pl.BlockSpec(memory_space=pltpu.SMEM)
    vmem = pl.BlockSpec(memory_space=pltpu.VMEM)
    shape = jax.ShapeDtypeStruct((10, 128, 128), jnp.float32)
    f32, bf16 = jnp.float32, jnp.bfloat16
    return pl.pallas_call(
        render_kernel,
        out_shape=(shape, shape),
        in_specs=[vmem, vmem, smem, smem, smem, vmem, vmem, smem],
        out_specs=(vmem, vmem),
        scratch_shapes=[
            pltpu.VMEM((288, 512), bf16),
            pltpu.VMEM((64, 256), bf16),
            pltpu.VMEM((256, 256), bf16),
            pltpu.VMEM((256, 256), bf16),
            pltpu.VMEM((32, 9, 256), f32),
            pltpu.VMEM((32, 256, 256), f32),
            pltpu.VMEM((32, 256, 256), f32),
            pltpu.VMEM((32, 9, 256), f32),
            pltpu.VMEM((256, 128), f32),
            pltpu.VMEM((288, 256), f32),
            pltpu.VMEM((576, 256), f32),
            pltpu.VMEM((128, 256), f32),
            pltpu.VMEM((576, 128), f32),
            pltpu.VMEM((576, 128), f32),
            pltpu.VMEM((128, 256), f32),
            pltpu.VMEM((3, 26, 32, 128), f32),
            pltpu.VMEM((2, 26, 16, 128), f32),
            *exchange_scratch(10),
            pltpu.SemaphoreType.DMA((4,)),
            pltpu.SemaphoreType.DMA((4,)),
            pltpu.SemaphoreType.DMA,
            pltpu.SemaphoreType.DMA,
        ],
        compiler_params=pltpu.CompilerParams(
            collective_id=1, has_side_effects=True, vmem_limit_bytes=34 * MIB
        ),
        cost_estimate=pl.CostEstimate(flops=20_000_000_000, bytes_accessed=4_000_000, transcendentals=7_000_000),
        name="render_step",
    )(slots, lists, counts, view, back, target_tiles, send_index, send_count)


RATES = [0.016] * 3 + [0.005] * 3 + [0.001] * 4 + [0.05] + [0.0025] * 3 + [0.000125] * 45
LOSS_TERMS = 2 * 3 * 1024 * 512


STAGES = 4


def update_kernel(
    params_ref, first_ref, second_ref, own_ref, other_ref, view_ref, shear_ref, offset_ref, center_ref,
    params_out, first_out, second_out, loss_out, dense, staged, copy_sem,
):
    refs = (shear_ref, offset_ref, center_ref)
    cameras = [camera_of(refs, 0), camera_of(refs, 1)]
    is_first = view_ref[0] == 0
    losses = own_ref[9, 0:1, :] + other_ref[9, 0:1, :]
    loss_out[...] = jnp.sum(losses, axis=1, keepdims=True) / LOSS_TERMS

    def copies(slot, sub):
        columns = pl.ds(pl.multiple_of(1024 * sub, 1024), 1024)
        return [
            pltpu.make_async_copy(staged.at[slot, k], out.at[:, columns], copy_sem.at[slot, k])
            for k, out in enumerate((params_out, first_out, second_out))
        ]

    def part(sub, carry):
        slot = lax.rem(sub, STAGES)

        @pl.when(sub >= STAGES)
        def _():
            for copy in copies(slot, sub - STAGES):
                copy.wait()

        rows = dense_rows(params_ref, sub)
        _, pull_back = jax.vjp(lambda *values: project_rows(values, cameras), *rows)
        here = pl.ds(pl.multiple_of(8 * sub, 8), 8)
        own = [own_ref[q, here, :] for q in range(9)]
        other = [other_ref[q, here, :] for q in range(9)]
        gradient = pull_back(
            [
                [jnp.where(is_first, a, b) for a, b in zip(own, other)],
                [jnp.where(is_first, b, a) for a, b in zip(own, other)],
            ]
        )
        for r in range(59):
            dense[8 * r : 8 * r + 8, :] = gradient[r]
        for first in range(0, 59, 8):
            size = min(8, 59 - first)
            row_ids = lax.broadcasted_iota(jnp.int32, (size, 128), 0)
            rate = jnp.full((size, 128), RATES[first], jnp.float32)
            for r in range(1, size):
                if RATES[first + r] != RATES[first + r - 1]:
                    rate = jnp.where(row_ids >= r, RATES[first + r], rate)
            rate = rate / (1.0 - 0.9**STEP_COUNT)
            for c in range(8):
                columns = pl.ds(pl.multiple_of(1024 * sub + 128 * c, 128), 128)
                here = (slice(first, first + size), columns)
                grad = dense[pl.ds(8 * first + c, size, stride=8), :]
                new_first = 0.9 * first_ref[here] + 0.1 * grad
                new_second = 0.999 * second_ref[here] + 0.001 * grad * grad
                scale = jnp.sqrt(new_second * (1.0 / (1.0 - 0.999**STEP_COUNT))) + 1e-15
                there = (slice(first, first + size), slice(128 * c, 128 * c + 128))
                staged.at[slot, 0][there] = params_ref[here] - rate * new_first / scale
                staged.at[slot, 1][there] = new_first
                staged.at[slot, 2][there] = new_second
        for copy in copies(slot, sub):
            copy.start()
        return carry

    lax.fori_loop(0, 16, part, 0)
    for sub in range(16 - STAGES, 16):
        for copy in copies(sub % STAGES, sub):
            copy.wait()


def update(params, first_moment, second_moment, own, other, view, shear, offset, center):
    smem = pl.BlockSpec(memory_space=pltpu.SMEM)
    vmem = pl.BlockSpec(memory_space=pltpu.VMEM)
    anywhere = pl.BlockSpec(memory_space=pl.ANY)
    shape = jax.ShapeDtypeStruct(params.shape, jnp.float32)
    return pl.pallas_call(
        update_kernel,
        out_shape=(shape, shape, shape, jax.ShapeDtypeStruct((1, 1), jnp.float32)),
        in_specs=[vmem, vmem, vmem, vmem, vmem, smem, smem, smem, smem],
        out_specs=(anywhere, anywhere, anywhere, vmem),
        scratch_shapes=[
            pltpu.VMEM((59 * 8, 128), jnp.float32),
            pltpu.VMEM((STAGES, 3, 59, 1024), jnp.float32),
            pltpu.SemaphoreType.DMA((STAGES, 3)),
        ],
        compiler_params=pltpu.CompilerParams(vmem_limit_bytes=24 * MIB),
        name="update",
    )(params, first_moment, second_moment, own, other, view, shear, offset, center)


def shards(
    params,
    first_moment,
    second_moment,
    target,
    view_shear,
    view_offset,
    cam_center,
    background,
    send_index,
    send_count,
    tile_list,
    tile_count,
):
    view_index = lax.axis_index("view")
    view = view_index.astype(jnp.int32).reshape(1)
    incoming = project_and_pick(params, send_index[0], view, view_shear, view_offset, cam_center)
    target_tiles = target[0].reshape(3, 16, 32, 16).transpose(2, 0, 1, 3).reshape(96, 256)
    own_grad, other_grad = render_step(
        incoming, tile_list[0, 0], tile_count, view, background, target_tiles, send_index[0], send_count
    )
    new_params, new_first, new_second, mean_loss = update(
        params, first_moment, second_moment, own_grad, other_grad, view, view_shear, view_offset, cam_center
    )
    return (new_params, new_first, new_second, mean_loss[0, 0])


def solution(mesh):
    placed = (
        P(None, "tile"),
        P(None, "tile"),
        P(None, "tile"),
        P("view", None, "tile", None),
        P(),
        P(),
        P(),
        P(),
        P("tile", None, None),
        P("tile", None),
        P("view", "tile", None, None),
        P("tile", None),
    )
    return jax.shard_map(
        shards,
        mesh=mesh,
        in_specs=placed,
        out_specs=(P(None, "tile"), P(None, "tile"), P(None, "tile"), P()),
        check_vma=False,
    )
```

```python
import functools
import math

import jax
import jax.numpy as jnp
from jax import lax
from jax.experimental import pallas as pl
from jax.experimental.pallas import tpu as pltpu
from jax.sharding import PartitionSpec as P

STEP_COUNT = 20
LIST = 256


def window_taps():
    raw_taps = [math.exp(-(position - 5) * (position - 5) / 4.5) for position in range(11)]
    return [element / sum(raw_taps) for element in raw_taps]


def harmonics(unit_x, unit_y, unit_z):
    square_x = unit_x * unit_x
    square_y = unit_y * unit_y
    square_z = unit_z * unit_z
    return [
        0.28209479177387814 * jnp.ones_like(unit_x),
        -0.4886025119029199 * unit_y,
        0.4886025119029199 * unit_z,
        -0.4886025119029199 * unit_x,
        1.0925484305920792 * unit_x * unit_y,
        -1.0925484305920792 * unit_y * unit_z,
        0.31539156525252005 * (2.0 * square_z - square_x - square_y),
        -1.0925484305920792 * unit_x * unit_z,
        0.5462742152960396 * (square_x - square_y),
        -0.5900435899266435 * unit_y * (3.0 * square_x - square_y),
        2.890611442640554 * unit_x * unit_y * unit_z,
        -0.4570457994644658 * unit_y * (4.0 * square_z - square_x - square_y),
        0.3731763325901154 * unit_z * (2.0 * square_z - 3.0 * square_x - 3.0 * square_y),
        -0.4570457994644658 * unit_x * (4.0 * square_z - square_x - square_y),
        1.445305721320277 * unit_z * (square_x - square_y),
        -0.5900435899266435 * unit_x * (square_x - 3.0 * square_y),
    ]


def ssim_map(level_x, level_y, energy_x, energy_y, product_xy):
    upper = (2.0 * level_x * level_y + 0.0001) * (2.0 * (product_xy - level_x * level_y) + 0.0009)
    lower = (level_x * level_x + level_y * level_y + 0.0001) * (
        energy_x - level_x * level_x + (energy_y - level_y * level_y) + 0.0009
    )
    return upper / lower


MESH = pl.DeviceIdType.MESH
MIB = 1024 * 1024
NN = (((1,), (0,)), ((), ()))
NT = (((1,), (1,)), ((), ()))
TN = (((0,), (0,)), ((), ()))


def mxu(left, right, dims):
    return lax.dot_general(left, right, dims, preferred_element_type=jnp.float32)


def split2(value):
    high = value.astype(jnp.bfloat16)
    low = (value - high.astype(jnp.float32)).astype(jnp.bfloat16)
    return high, low


def split3(value):
    high = value.astype(jnp.bfloat16)
    rest = value - high.astype(jnp.float32)
    middle = rest.astype(jnp.bfloat16)
    low = (rest - middle.astype(jnp.float32)).astype(jnp.bfloat16)
    return high, middle, low


def project_rows(rows, cameras):
    pos_x, pos_y, pos_z = rows[0:3]
    scales = [jnp.exp(row) for row in rows[3:6]]
    quat_w, quat_x, quat_y, quat_z = rows[6:10]
    norm = 1.0 / jnp.sqrt(
        quat_w * quat_w + quat_x * quat_x + quat_y * quat_y + quat_z * quat_z
    )
    quat_w, quat_x, quat_y, quat_z = quat_w * norm, quat_x * norm, quat_y * norm, quat_z * norm
    rotation = [
        [
            1.0 - 2.0 * (quat_y * quat_y + quat_z * quat_z),
            2.0 * (quat_x * quat_y - quat_w * quat_z),
            2.0 * (quat_x * quat_z + quat_w * quat_y),
        ],
        [
            2.0 * (quat_x * quat_y + quat_w * quat_z),
            1.0 - 2.0 * (quat_x * quat_x + quat_z * quat_z),
            2.0 * (quat_y * quat_z - quat_w * quat_x),
        ],
        [
            2.0 * (quat_x * quat_z - quat_w * quat_y),
            2.0 * (quat_y * quat_z + quat_w * quat_x),
            1.0 - 2.0 * (quat_x * quat_x + quat_y * quat_y),
        ],
    ]
    opacity = 1.0 / (1.0 + jnp.exp(-rows[10]))
    records = []
    for shear_x, shear_y, offset_x, offset_y, center_x, center_y, center_z in cameras:
        first = [(rotation[0][k] + shear_x * rotation[2][k]) * scales[k] for k in range(3)]
        second = [(rotation[1][k] + shear_y * rotation[2][k]) * scales[k] for k in range(3)]
        cov_xx = first[0] * first[0] + first[1] * first[1] + first[2] * first[2] + 0.3
        cov_yy = second[0] * second[0] + second[1] * second[1] + second[2] * second[2] + 0.3
        cov_xy = first[0] * second[0] + first[1] * second[1] + first[2] * second[2]
        inverse = 1.0 / (cov_xx * cov_yy - cov_xy * cov_xy)
        toward_x = pos_x - center_x
        toward_y = pos_y - center_y
        toward_z = pos_z - center_z
        shrink = 1.0 / jnp.sqrt(toward_x * toward_x + toward_y * toward_y + toward_z * toward_z)
        basis = harmonics(toward_x * shrink, toward_y * shrink, toward_z * shrink)
        colors = []
        for c in range(3):
            total = basis[0] * rows[11 + c]
            for k in range(1, 16):
                total = total + basis[k] * rows[11 + 3 * k + c]
            colors.append(0.5 + total)
        records.append(
            [
                pos_x + shear_x * pos_z + offset_x,
                pos_y + shear_y * pos_z + offset_y,
                cov_yy * inverse,
                -cov_xy * inverse,
                cov_xx * inverse,
                opacity,
                *colors,
            ]
        )
    return records


def camera_of(refs, view):
    shear_ref, offset_ref, center_ref = refs
    return (
        shear_ref[view, 0],
        shear_ref[view, 1],
        offset_ref[view, 0],
        offset_ref[view, 1],
        center_ref[view, 0],
        center_ref[view, 1],
        center_ref[view, 2],
    )


BLOCK = 4096


def dense_rows(source_ref, sub):
    count = source_ref.shape[0]
    columns = pl.ds(pl.multiple_of(1024 * sub, 1024), 1024)
    rows = []
    for first in range(0, count, 8):
        size = min(8, count - first)
        block = source_ref[first : first + size, columns].reshape(size, 8, 128)
        rows += [block[r] for r in range(size)]
    return rows


def axis_peers(me, stride):
    place = lax.rem(me // stride, 4)
    return [me + (lax.rem(place + j, 4) - place) * stride for j in range(1, 4)]


def signal_all(semaphore, peers):
    for peer in peers:
        pl.semaphore_signal(semaphore, inc=1, device_id={"tile": peer}, device_id_type=MESH)


def greet_all(stage, semaphores):
    plane_sem, cube_sem = semaphores
    me = lax.axis_index("tile")
    lines = [axis_peers(me, stride) for stride in (1, 4, 16)]
    barrier = pltpu.get_barrier_semaphore()
    if stage == 0:
        for line in lines:
            signal_all(barrier, line)
    elif stage == 1:
        pl.semaphore_wait(barrier, 9)
        signal_all(plane_sem, lines[1])
    elif stage == 2:
        pl.semaphore_wait(plane_sem, 3)
        signal_all(cube_sem, lines[2])
    else:
        pl.semaphore_wait(cube_sem, 3)


def block_copy(outgoing, incoming, send_sem, recv_sem, peer):
    me = lax.axis_index("tile")
    return pltpu.make_async_remote_copy(
        src_ref=outgoing.at[peer],
        dst_ref=incoming.at[me],
        send_sem=send_sem,
        recv_sem=recv_sem,
        device_id={"tile": peer},
        device_id_type=MESH,
    )


def send_block(outgoing, incoming, send_sem, recv_sem, peer):
    @pl.when(peer != lax.axis_index("tile"))
    def _():
        block_copy(outgoing, incoming, send_sem, recv_sem, peer).start()


def finish_blocks(outgoing, incoming, send_sem, recv_sem):
    me = lax.axis_index("tile")
    pltpu.make_async_remote_copy(
        src_ref=outgoing.at[0:63],
        dst_ref=incoming.at[0:63],
        send_sem=send_sem,
        recv_sem=recv_sem,
        device_id={"tile": lax.rem(me + 1, 64)},
        device_id_type=MESH,
    ).wait()
    incoming[me] = outgoing[me]


def exchange_scratch(rows):
    return [
        pltpu.VMEM((64, rows, 128), jnp.float32),
        pltpu.VMEM((64, rows, 128), jnp.float32),
        pltpu.SemaphoreType.DMA,
        pltpu.SemaphoreType.DMA,
        pltpu.SemaphoreType.REGULAR,
        pltpu.SemaphoreType.REGULAR,
    ]


def project_kernel(
    source_ref, index_ref, view_ref, shear_ref, offset_ref, center_ref, incoming,
    params_ref, table, high_parts, low_parts, outgoing, send_sem, recv_sem, plane_sem, cube_sem, load_sem,
):
    greetings = (plane_sem, cube_sem)
    loads = [
        pltpu.make_async_copy(
            source_ref.at[:, pl.ds(BLOCK * k, BLOCK)], params_ref.at[:, pl.ds(BLOCK * k, BLOCK)], load_sem.at[k]
        )
        for k in range(16384 // BLOCK)
    ]
    for load in loads:
        load.start()
    greet_all(0, greetings)
    camera = camera_of((shear_ref, offset_ref, center_ref), view_ref[0])

    def part(sub, carry):
        record = project_rows(dense_rows(params_ref, sub), [camera])[0]
        first = pl.multiple_of(8 * sub, 8)
        for q in range(9):
            table[q, pl.ds(first, 8), :] = record[q]
        return carry

    for k, load in enumerate(loads):
        load.wait()
        lax.fori_loop(k * BLOCK // 1024, (k + 1) * BLOCK // 1024, part, 0, unroll=2)
        if k == 1:
            greet_all(1, greetings)
    greet_all(2, greetings)
    for q in range(9):
        for half in range(2):
            store_parts(
                table[q, 64 * half : 64 * half + 64, :],
                high_parts, low_parts, q, pl.ds(128 * half, 128),
            )
    low_ids = lax.broadcasted_iota(jnp.int32, (256, 256), 0)
    high_ids = lax.broadcasted_iota(jnp.int32, (64, 256), 0)

    def pick(pair, carry):
        index = jnp.concatenate(
            [index_ref[pl.ds(pair, 1), :], index_ref[pl.ds(pair + 32, 1), :]], axis=1
        )
        high = (index >> 7) & 63
        low = (index & 127) + ((index >> 13) << 7)
        rows = pick_rows(high_parts, low_parts, one_hot(low_ids, low), high_ids == high)
        for q in range(9):
            outgoing[pair, q : q + 1, :] = rows[q][:, 0:128]
            outgoing[pair + 32, q : q + 1, :] = rows[q][:, 128:256]
        return carry

    me = lax.axis_index("tile")

    def group(part, carry):
        first = lax.rem(part + me, 4) * 8
        lax.fori_loop(0, 8, lambda k, carry: pick(first + k, carry), 0, unroll=4)

        @pl.when(part == 0)
        def _():
            greet_all(3, greetings)

        def send(k, carry):
            for peer in (first + k, first + k + 32):
                send_block(outgoing, incoming, send_sem, recv_sem, peer)
            return carry

        lax.fori_loop(0, 8, send, 0)
        return carry

    lax.fori_loop(0, 4, group, 0)
    finish_blocks(outgoing, incoming, send_sem, recv_sem)


def project_and_pick(params, send_index, view, shear, offset, center):
    smem = pl.BlockSpec(memory_space=pltpu.SMEM)
    return pl.pallas_call(
        project_kernel,
        out_shape=jax.ShapeDtypeStruct((64, 9, 128), jnp.float32),
        in_specs=[
            pl.BlockSpec(memory_space=pl.ANY),
            pl.BlockSpec(memory_space=pltpu.VMEM),
            smem,
            smem,
            smem,
            smem,
        ],
        out_specs=pl.BlockSpec(memory_space=pltpu.VMEM),
        scratch_shapes=[
            pltpu.VMEM((59, 16384), jnp.float32),
            pltpu.VMEM((9, 128, 128), jnp.float32),
            pltpu.VMEM((576, 512), jnp.bfloat16),
            pltpu.VMEM((128, 256), jnp.bfloat16),
            pltpu.VMEM((64, 9, 128), jnp.float32),
            pltpu.SemaphoreType.DMA,
            pltpu.SemaphoreType.DMA,
            pltpu.SemaphoreType.REGULAR,
            pltpu.SemaphoreType.REGULAR,
            pltpu.SemaphoreType.DMA((16384 // BLOCK,)),
        ],
        compiler_params=pltpu.CompilerParams(
            collective_id=0, has_side_effects=True, vmem_limit_bytes=56 * MIB
        ),
        name="project_and_pick",
    )(params, send_index, view, shear, offset, center)


def slot_place(index):
    return (index >> 7) & 31, (index & 127) + ((index >> 12) << 7)


def one_hot(ids, values):
    return (ids == values).astype(jnp.float32).astype(jnp.bfloat16)


def store_parts(rows, high_parts, low_parts, q, columns):
    count = rows.shape[0]
    high, middle, low = split3(rows)
    here = pl.ds(count * q, count)
    width = columns.size
    high_parts[here, columns] = high
    high_parts[here, pl.ds(columns.start + 256, width)] = middle
    if q < 2:
        low_parts[here, columns] = low


def both_parts(value, right, dims):
    sums = mxu(jnp.concatenate(split2(value), axis=0), right, dims)
    return sums[: value.shape[0]] + sums[value.shape[0] :]


def pick_rows(high_parts, low_parts, hot, mask):
    count = mask.shape[0]
    found = mxu(high_parts[...], jnp.concatenate([hot, hot], axis=0), NN)
    found_low = mxu(low_parts[...], hot, NN)
    rows = []
    for q in range(9):
        part = found[count * q : count * q + count]
        if q < 2:
            part = part + found_low[count * q : count * q + count]
        rows.append(jnp.sum(jnp.where(mask, part, 0.0), axis=0, keepdims=True))
    return rows


def place_rows(rows, total, hot, mask):
    count = mask.shape[0]
    high_rows, low_rows = [], []
    for row in rows:
        high = row.astype(jnp.bfloat16).astype(jnp.float32)
        high_rows.append(jnp.where(mask, high, 0.0))
        low_rows.append(jnp.where(mask, row - high, 0.0))
    placed = jnp.concatenate(high_rows + low_rows, axis=0).astype(jnp.bfloat16)
    sums = mxu(placed, hot, NT)
    total[...] += sums[: 9 * count] + sums[9 * count :]


def tile_deltas(tile, band, u_row, w_row):
    offsets = lax.broadcasted_iota(jnp.int32, (16, 256), 0)
    pixel_x = (offsets + 16 * tile).astype(jnp.float32) + 0.5
    pixel_y = (offsets + 16 * band).astype(jnp.float32) + 0.5
    return pixel_x - u_row, pixel_y - w_row


def forward_tile(tile, band, picked, before, cover_ref, keep_ref, total):
    rows = [picked[tile, q : q + 1, :] for q in range(9)]
    delta_x, delta_y = tile_deltas(tile, band, rows[0], rows[1])
    along_x = -0.5 * rows[2] * delta_x * delta_x
    mixed = -rows[3] * delta_x
    along_y = -0.5 * rows[4] * delta_y * delta_y
    color_ids = lax.broadcasted_iota(jnp.int32, (128, 256), 0)
    colors = jnp.zeros((128, 256), jnp.float32)
    for c in range(3):
        colors = jnp.where(color_ids == 3 * tile + c, rows[6 + c], colors)
    colors = jnp.concatenate(split2(colors), axis=0)
    pieces = []
    for i in range(16):
        exponent = along_x + (mixed * delta_y[i : i + 1] + along_y[i : i + 1])
        pieces.append(rows[5] * jnp.exp(exponent))
    cover = jnp.concatenate(pieces, axis=0)
    keep = jnp.exp(both_parts(jnp.log(1.0 - cover), before[...], NN))
    cover_ref[tile] = cover
    keep_ref[tile] = keep
    shown = mxu(jnp.concatenate(split2(cover * keep), axis=0), colors, NT)
    total[...] += shown[0:256, 0:128] + shown[0:256, 128:256] + shown[256:512, 0:128]


def backward_tile(tile, band, picked, after, cover_ref, keep_ref, grad_ref, results):
    rows = [picked[tile, q : q + 1, :] for q in range(9)]
    grads = jnp.concatenate([grad_ref[pl.ds(3 * tile + c, 1), :] for c in range(3)], axis=0)
    colors = jnp.concatenate(rows[6:9], axis=0)
    grads_high = grads.astype(jnp.bfloat16).astype(jnp.float32)
    grads_low = grads - grads_high
    colors_high = colors.astype(jnp.bfloat16).astype(jnp.float32)
    colors_low = colors - colors_high
    blank = jnp.zeros((7, 256), jnp.float32)
    left = jnp.concatenate([grads_high, grads_high, grads_low, blank], axis=0).astype(jnp.bfloat16)
    right = jnp.concatenate([colors_high, colors_low, colors_high, blank], axis=0).astype(jnp.bfloat16)
    both = jnp.concatenate([grads_high, grads_low, blank, blank[0:3]], axis=0).astype(jnp.bfloat16)
    delta_x, delta_y = tile_deltas(tile, band, rows[0], rows[1])
    shade = mxu(left, right, TN)
    weight = keep_ref[tile]
    lit = weight * shade
    behind = mxu(lit.astype(jnp.bfloat16), after[...], NN)
    pull = lit - behind * cover_ref[tile]
    sum_0 = jnp.zeros((16, 256), jnp.float32)
    sum_y = sum_0
    sum_yy = sum_0
    for i in range(16):
        piece = pull[16 * i : 16 * i + 16]
        level = delta_y[i : i + 1]
        piece_y = piece * level
        sum_0 = sum_0 + piece
        sum_y = sum_y + piece_y
        sum_yy = sum_yy + piece_y * level
    weight_high, weight_low = split2(weight)
    color_grad = mxu(both, weight_high, NN)
    color_grad = color_grad[0:3] + color_grad[3:6] + mxu(both, weight_low, NN)[0:3]
    sum_x = sum_0 * delta_x

    def fold(value):
        return jnp.sum(value, axis=0, keepdims=True)

    moment_x = fold(sum_x)
    moment_y = fold(sum_y)
    live = rows[5] > 0.0
    values = [
        rows[2] * moment_x + rows[3] * moment_y,
        rows[4] * moment_y + rows[3] * moment_x,
        -0.5 * fold(sum_x * delta_x),
        -fold(sum_y * delta_x),
        -0.5 * fold(sum_yy),
        jnp.where(live, fold(sum_0) / jnp.where(live, rows[5], 1.0), 0.0),
        color_grad[0:1],
        color_grad[1:2],
        color_grad[2:3],
    ]
    for q in range(9):
        results[tile, q : q + 1, :] = values[q]


def blurred_down(planes, count):
    taps = window_taps()
    result = taps[5] * planes[5 : 5 + count]
    for k in range(5):
        result = result + taps[k] * (planes[k : k + count] + planes[10 - k : 10 - k + count])
    return result


def blurred_across(planes, spread):
    taps = window_taps()
    spread[:, 0:8, :] = pltpu.roll(planes[:, 8:16], 3, 2)
    spread[:, 8:24, :] = planes
    spread[:, 24:32, :] = pltpu.roll(planes[:, 0:8], 125, 2)
    result = taps[5] * planes
    for k in range(5):
        result = result + taps[k] * (spread[:, 3 + k : 19 + k, :] + spread[:, 13 - k : 29 - k, :])
    return result


def rows_within(field_ref, band, last_band):
    rows = lax.broadcasted_iota(jnp.int32, (36, 16, 128), 0) - 10 + 16 * band
    within = (rows >= 0) & (rows < 16 * (last_band + 1))
    return jnp.where(within, field_ref[...].reshape(36, 16, 128), 0.0), within


def window_of(plane, spread):
    return blurred_across(blurred_down(plane, 26), spread)


def truth_step(band, last_band, truth_ref, spread, truth_stats):
    truth, _ = rows_within(truth_ref, band, last_band)
    truth_stats[0] = window_of(truth, spread.at[0])
    truth_stats[1] = window_of(truth * truth, spread.at[1])


def window_step(band, last_band, image_ref, truth_ref, grad_ref, spread, truth_stats):
    image, within = rows_within(image_ref, band, last_band)
    truth, _ = rows_within(truth_ref, band, last_band)
    mean_x = window_of(image, spread.at[0])
    power_x = window_of(image * image, spread.at[1])
    cross_xy = window_of(image * truth, spread.at[2])
    mean_y, power_y = truth_stats[0], truth_stats[1]
    similarity, ssim_back = jax.vjp(
        lambda level_x, energy_x, product_xy: ssim_map(
            level_x, mean_y, energy_x, power_y, product_xy
        ),
        mean_x,
        power_x,
        cross_xy,
    )
    lanes = lax.broadcasted_iota(jnp.int32, (26, 16, 128), 2)
    counted = within[5:31] & (lanes < 96)
    pulled = []
    for k, plane in enumerate(ssim_back(jnp.where(counted, -0.8, 0.0))):
        pulled.append(blurred_across(blurred_down(plane, 16), spread.at[k, 0:16]))
    shown = image[10:26]
    wanted = truth[10:26]
    difference = shown - wanted
    smooth = jnp.sqrt(difference * difference + 0.0001)
    loss = jnp.where(lanes[0:16] < 96, 0.2 * smooth + 0.8 * (1.0 - similarity[5:21]), 0.0)
    pixel_grad = 0.2 * difference / smooth + pulled[0] + 2.0 * shown * pulled[1] + wanted * pulled[2]
    grad_ref[...] = jnp.transpose(pixel_grad.reshape(256, 128))
    return jnp.sum(jnp.sum(loss, axis=0), axis=0, keepdims=True)


def render_kernel(
    slots_ref, list_ref, count_ref, view_ref, back_ref, target_ref, index_ref, sent_ref,
    own_ref, other_ref,
    high_parts, low_parts, before, after, picked, cover_ref, keep_ref, results, total, slot_total, owner_total,
    target_rows, image_ref, truth_ref, grad_ref, spread, truth_stats,
    outgoing, incoming, send_sem, recv_sem, plane_sem, cube_sem, halo_send, halo_recv, swap_send, swap_recv,
):
    me = lax.axis_index("tile")
    pair = 1 - lax.axis_index("view")
    band = me
    last_band = lax.axis_size("tile") - 1
    view = view_ref[0]
    barrier = pltpu.get_barrier_semaphore()
    lines = [axis_peers(me, stride) for stride in (1, 4, 16)]
    for line in lines:
        signal_all(barrier, line)
    pl.semaphore_signal(barrier, inc=1, device_id={"view": pair}, device_id_type=MESH)

    for q in range(9):
        for half in range(2):
            store_parts(
                slots_ref[32 * half : 32 * half + 32, q, :], high_parts, low_parts, q, pl.ds(128 * half, 128)
            )
    row_ids = lax.broadcasted_iota(jnp.int32, (256, 256), 0)
    column_ids = lax.broadcasted_iota(jnp.int32, (256, 256), 1)
    before[...] = (row_ids < column_ids).astype(jnp.float32).astype(jnp.bfloat16)
    after[...] = (row_ids > column_ids).astype(jnp.float32).astype(jnp.bfloat16)
    own_pixels = slice(160, 416)
    target_rows[0:96, :] = target_ref[...]
    target_rows[96:128, :] = jnp.zeros((32, 256), jnp.float32)
    truth_ref[own_pixels, :] = jnp.transpose(target_rows[...])
    lanes = lax.broadcasted_iota(jnp.int32, (1, 256), 1)
    high_ids = lax.broadcasted_iota(jnp.int32, (32, 256), 0)

    def pick(tile, carry):
        high, low = slot_place(list_ref[pl.ds(tile, 1), :])
        low_ids = lax.broadcasted_iota(jnp.int32, (256, 256), 0)
        rows = pick_rows(high_parts, low_parts, one_hot(low_ids, low), high_ids == high)
        rows[5] = jnp.where(lanes < count_ref[0, tile], rows[5], 0.0)
        for c in range(3):
            rows[6 + c] = rows[6 + c] - back_ref[view, c]
        for q in range(9):
            picked[tile, q : q + 1, :] = rows[q]
        return carry

    lax.fori_loop(0, 32, pick, 0, unroll=4)
    pl.semaphore_wait(barrier, 10)
    signal_all(plane_sem, lines[1])
    total[...] = jnp.zeros_like(total)

    def forward(tile, carry):
        forward_tile(tile, band, picked, before, cover_ref, keep_ref, total)
        return carry

    lax.fori_loop(0, 12, forward, 0, unroll=4)
    pl.semaphore_wait(plane_sem, 3)
    signal_all(cube_sem, lines[2])
    lax.fori_loop(12, 24, forward, 0, unroll=4)
    pl.semaphore_wait(cube_sem, 3)

    following, previous = lax.rem(me + 1, 64), lax.rem(me + 63, 64)

    def halo(field, k, peer, source, target):
        return pltpu.make_async_remote_copy(
            src_ref=field.at[pl.ds(source, 160), :],
            dst_ref=field.at[pl.ds(target, 160), :],
            send_sem=halo_send.at[k],
            recv_sem=halo_recv.at[k],
            device_id={"tile": peer},
            device_id_type=MESH,
        )

    copies = [halo(truth_ref, 0, following, 256, 0), halo(truth_ref, 1, previous, 160, 416)]
    for copy in copies:
        copy.start()
    lax.fori_loop(24, 32, forward, 0, unroll=4)
    color_lanes = lax.broadcasted_iota(jnp.int32, (1, 128), 1)
    backdrop = jnp.zeros((1, 128), jnp.float32)
    for c in range(3):
        here = (lax.rem(color_lanes, 3) == c) & (color_lanes < 96)
        backdrop = jnp.where(here, back_ref[view, c], backdrop)
    image_ref[own_pixels, :] = total[...] + backdrop
    shown = [halo(image_ref, 2, following, 256, 0), halo(image_ref, 3, previous, 160, 416)]
    for copy in shown:
        copy.start()
    for copy in copies:
        copy.wait()
    truth_step(band, last_band, truth_ref, spread, truth_stats)

    def prepare(tile, carry):
        cover = cover_ref[tile]
        keep_ref[tile] = cover * keep_ref[tile]
        cover_ref[tile] = cover / (1.0 - cover)
        return carry

    lax.fori_loop(0, 32, prepare, 0, unroll=2)
    for copy in shown:
        copy.wait()
    loss = window_step(band, last_band, image_ref, truth_ref, grad_ref, spread, truth_stats)

    def backward(group, carry):
        for slot in range(4):
            backward_tile(
                4 * group + slot, band, picked, after, cover_ref, keep_ref, grad_ref, results
            )
        return carry

    lax.fori_loop(0, 8, backward, 0)
    slot_total[...] = jnp.zeros_like(slot_total)

    def joined(values):
        return jnp.concatenate(values, axis=1)

    def place_slots(tile, carry):
        tiles = (tile, tile + 16)
        high, low = slot_place(joined([list_ref[pl.ds(t, 1), :] for t in tiles]))
        low_ids = lax.broadcasted_iota(jnp.int32, (256, 512), 0)
        slot_ids = lax.broadcasted_iota(jnp.int32, (32, 512), 0)
        rows = [joined([results[t, q : q + 1, :] for t in tiles]) for q in range(9)]
        place_rows(rows, slot_total, one_hot(low_ids, low), slot_ids == high)
        return carry

    lax.fori_loop(0, 16, place_slots, 0, unroll=4)
    for q in range(9):
        for half in range(2):
            outgoing[32 * half : 32 * half + 32, q, :] = slot_total[
                32 * q : 32 * q + 32, 128 * half : 128 * half + 128
            ]
    outgoing[:, 9, :] = jnp.broadcast_to(loss, (64, 128))

    def send(p, carry):
        block_copy(outgoing, incoming, send_sem, recv_sem, lax.rem(me + p, 64)).start()
        return carry

    lax.fori_loop(1, 64, send, 0)
    owner_total[...] = jnp.zeros_like(owner_total)
    owner_ids = lax.broadcasted_iota(jnp.int32, (64, 512), 0)
    finish_blocks(outgoing, incoming, send_sem, recv_sem)

    def place_owned(first, carry):
        bands = (first, first + 16, first + 32, first + 48)
        index = joined([index_ref[pl.ds(d, 1), :] for d in bands])
        live = joined([(color_lanes < sent_ref[0, d]).astype(jnp.int32) for d in bands])
        high = jnp.where(live > 0, (index >> 7) & 63, -1)
        low = (index & 127) + ((index >> 13) << 7)
        low_ids = lax.broadcasted_iota(jnp.int32, (256, 512), 0)
        rows = [joined([incoming[d, q : q + 1, :] for d in bands]) for q in range(9)]
        place_rows(rows, owner_total, one_hot(low_ids, low), owner_ids == high)
        return carry

    lax.fori_loop(0, 16, place_owned, 0, unroll=4)
    for q in range(9):
        for half in range(2):
            own_ref[q, 64 * half : 64 * half + 64, :] = owner_total[
                64 * q : 64 * q + 64, 128 * half : 128 * half + 128
            ]
    losses = jnp.sum(incoming[:, 9, :], axis=0, keepdims=True)
    own_ref[9] = jnp.broadcast_to(losses, (128, 128))
    swap = pltpu.make_async_remote_copy(
        src_ref=own_ref,
        dst_ref=other_ref,
        send_sem=swap_send,
        recv_sem=swap_recv,
        device_id={"view": pair},
        device_id_type=MESH,
    )
    swap.start()
    swap.wait()


def render_step(slots, lists, counts, view, back, target_tiles, send_index, send_count):
    smem = pl.BlockSpec(memory_space=pltpu.SMEM)
    vmem = pl.BlockSpec(memory_space=pltpu.VMEM)
    shape = jax.ShapeDtypeStruct((10, 128, 128), jnp.float32)
    f32, bf16 = jnp.float32, jnp.bfloat16
    return pl.pallas_call(
        render_kernel,
        out_shape=(shape, shape),
        in_specs=[vmem, vmem, smem, smem, smem, vmem, vmem, smem],
        out_specs=(vmem, vmem),
        scratch_shapes=[
            pltpu.VMEM((288, 512), bf16),
            pltpu.VMEM((64, 256), bf16),
            pltpu.VMEM((256, 256), bf16),
            pltpu.VMEM((256, 256), bf16),
            pltpu.VMEM((32, 9, 256), f32),
            pltpu.VMEM((32, 256, 256), f32),
            pltpu.VMEM((32, 256, 256), f32),
            pltpu.VMEM((32, 9, 256), f32),
            pltpu.VMEM((256, 128), f32),
            pltpu.VMEM((288, 256), f32),
            pltpu.VMEM((576, 256), f32),
            pltpu.VMEM((128, 256), f32),
            pltpu.VMEM((576, 128), f32),
            pltpu.VMEM((576, 128), f32),
            pltpu.VMEM((128, 256), f32),
            pltpu.VMEM((3, 26, 32, 128), f32),
            pltpu.VMEM((2, 26, 16, 128), f32),
            *exchange_scratch(10),
            pltpu.SemaphoreType.DMA((4,)),
            pltpu.SemaphoreType.DMA((4,)),
            pltpu.SemaphoreType.DMA,
            pltpu.SemaphoreType.DMA,
        ],
        compiler_params=pltpu.CompilerParams(
            collective_id=1, has_side_effects=True, vmem_limit_bytes=34 * MIB
        ),
        cost_estimate=pl.CostEstimate(flops=20_000_000_000, bytes_accessed=4_000_000, transcendentals=7_000_000),
        name="render_step",
    )(slots, lists, counts, view, back, target_tiles, send_index, send_count)


RATES = [0.016] * 3 + [0.005] * 3 + [0.001] * 4 + [0.05] + [0.0025] * 3 + [0.000125] * 45
LOSS_TERMS = 2 * 3 * 1024 * 512


STAGES = 4


def update_kernel(
    params_ref, first_ref, second_ref, own_ref, other_ref, view_ref, shear_ref, offset_ref, center_ref,
    params_out, first_out, second_out, loss_out, dense, staged, copy_sem,
):
    refs = (shear_ref, offset_ref, center_ref)
    cameras = [camera_of(refs, 0), camera_of(refs, 1)]
    is_first = view_ref[0] == 0
    losses = own_ref[9, 0:1, :] + other_ref[9, 0:1, :]
    loss_out[...] = jnp.sum(losses, axis=1, keepdims=True) / LOSS_TERMS

    def copies(slot, sub):
        columns = pl.ds(pl.multiple_of(1024 * sub, 1024), 1024)
        return [
            pltpu.make_async_copy(staged.at[slot, k], out.at[:, columns], copy_sem.at[slot, k])
            for k, out in enumerate((params_out, first_out, second_out))
        ]

    def part(sub, carry):
        slot = lax.rem(sub, STAGES)

        @pl.when(sub >= STAGES)
        def _():
            for copy in copies(slot, sub - STAGES):
                copy.wait()

        rows = dense_rows(params_ref, sub)
        _, pull_back = jax.vjp(lambda *values: project_rows(values, cameras), *rows)
        here = pl.ds(pl.multiple_of(8 * sub, 8), 8)
        own = [own_ref[q, here, :] for q in range(9)]
        other = [other_ref[q, here, :] for q in range(9)]
        gradient = pull_back(
            [
                [jnp.where(is_first, a, b) for a, b in zip(own, other)],
                [jnp.where(is_first, b, a) for a, b in zip(own, other)],
            ]
        )
        for r in range(59):
            dense[8 * r : 8 * r + 8, :] = gradient[r]
        for first in range(0, 59, 8):
            size = min(8, 59 - first)
            row_ids = lax.broadcasted_iota(jnp.int32, (size, 128), 0)
            rate = jnp.full((size, 128), RATES[first], jnp.float32)
            for r in range(1, size):
                if RATES[first + r] != RATES[first + r - 1]:
                    rate = jnp.where(row_ids >= r, RATES[first + r], rate)
            rate = rate / (1.0 - 0.9**STEP_COUNT)
            for c in range(8):
                columns = pl.ds(pl.multiple_of(1024 * sub + 128 * c, 128), 128)
                here = (slice(first, first + size), columns)
                grad = dense[pl.ds(8 * first + c, size, stride=8), :]
                new_first = 0.9 * first_ref[here] + 0.1 * grad
                new_second = 0.999 * second_ref[here] + 0.001 * grad * grad
                scale = jnp.sqrt(new_second * (1.0 / (1.0 - 0.999**STEP_COUNT))) + 1e-15
                there = (slice(first, first + size), slice(128 * c, 128 * c + 128))
                staged.at[slot, 0][there] = params_ref[here] - rate * new_first / scale
                staged.at[slot, 1][there] = new_first
                staged.at[slot, 2][there] = new_second
        for copy in copies(slot, sub):
            copy.start()
        return carry

    lax.fori_loop(0, 16, part, 0)
    for sub in range(16 - STAGES, 16):
        for copy in copies(sub % STAGES, sub):
            copy.wait()


def update(params, first_moment, second_moment, own, other, view, shear, offset, center):
    smem = pl.BlockSpec(memory_space=pltpu.SMEM)
    vmem = pl.BlockSpec(memory_space=pltpu.VMEM)
    anywhere = pl.BlockSpec(memory_space=pl.ANY)
    shape = jax.ShapeDtypeStruct(params.shape, jnp.float32)
    return pl.pallas_call(
        update_kernel,
        out_shape=(shape, shape, shape, jax.ShapeDtypeStruct((1, 1), jnp.float32)),
        in_specs=[vmem, vmem, vmem, vmem, vmem, smem, smem, smem, smem],
        out_specs=(anywhere, anywhere, anywhere, vmem),
        scratch_shapes=[
            pltpu.VMEM((59 * 8, 128), jnp.float32),
            pltpu.VMEM((STAGES, 3, 59, 1024), jnp.float32),
            pltpu.SemaphoreType.DMA((STAGES, 3)),
        ],
        compiler_params=pltpu.CompilerParams(vmem_limit_bytes=24 * MIB),
        name="update",
    )(params, first_moment, second_moment, own, other, view, shear, offset, center)


def shards(
    params,
    first_moment,
    second_moment,
    target,
    view_shear,
    view_offset,
    cam_center,
    background,
    send_index,
    send_count,
    tile_list,
    tile_count,
):
    view_index = lax.axis_index("view")
    view = view_index.astype(jnp.int32).reshape(1)
    incoming = project_and_pick(params, send_index[0], view, view_shear, view_offset, cam_center)
    target_tiles = target[0].reshape(3, 16, 32, 16).transpose(2, 0, 1, 3).reshape(96, 256)
    own_grad, other_grad = render_step(
        incoming, tile_list[0, 0], tile_count, view, background, target_tiles, send_index[0], send_count
    )
    new_params, new_first, new_second, mean_loss = update(
        params, first_moment, second_moment, own_grad, other_grad, view, view_shear, view_offset, cam_center
    )
    return (new_params, new_first, new_second, mean_loss[0, 0])


def solution(mesh):
    placed = (
        P(None, "tile"),
        P(None, "tile"),
        P(None, "tile"),
        P("view", None, "tile", None),
        P(),
        P(),
        P(),
        P(),
        P("tile", None, None),
        P("tile", None),
        P("view", "tile", None, None),
        P("tile", None),
    )
    return jax.shard_map(
        shards,
        mesh=mesh,
        in_specs=placed,
        out_specs=(P(None, "tile"), P(None, "tile"), P(None, "tile"), P()),
        check_vma=False,
    )
```
